512 devices in a mesh: seq: 16 (over y, x), bal: 32 (over z, core).
Axes of the slice: x: 4, y: 4, z: 16, core: 2. Of those that a mesh axis runs over, the one named last changes fastest.
Arguments:
- tokens: bfloat16 [24576, 3072], P(('bal', 'seq')), may hold values from -6 to 6
- qkv_weight: bfloat16 [3072, 16, 3, 128], P(None, 'seq'), may hold values from -0.109375 to 0.109375
- q_gain: float32 [16, 128], P('seq'), may hold values from 0.5 to 2
- k_gain: float32 [16, 128], P('seq'), may hold values from 0.5 to 2
- key_tiles: int32 [16, 192, 64], P('seq'), may hold values from 0 to 191, as said below
- key_counts: int32 [16, 192], P('seq'), may hold values from 1 to 64, as said below
Outputs:
- attended: bfloat16 [24576, 2048], P(('bal', 'seq'))
The draws below stay inside these ranges and needn't reach their ends.
Inputs may be any that keep to these rules, and one draw needn't show every extreme that they name: Each row of key_tiles lists 64 distinct tiles; only the first key_counts entries of a row are attended. `key_counts`: every head has a query tile that attends all 64 listed tiles.
All inputs are finite; a program needn't handle non-finite values.
Results may differ from the reference program's by a relative error of at most 0.0079.
Values may be sent and summed in bfloat16 or wider, within the bound.
No kernel may reach another device: no remote copies, remote signals or barrier semaphores. Data moves between devices by JAX's collectives and lax.ppermute only.
A program may use at most 128 MiB of HBM per device.

```python
import math
import jax
import jax.numpy as jnp
from jax import lax

D = 3072
HD = 128
HEADS = 16
TILE = 128
QT = 192
MAXK = 64
S = 24576


def draw_key_tiles(key, part):
    key = jax.random.fold_in(key, 7)
    scores = jax.random.randint(key, (HEADS, QT, QT), 0, 1 << 16) * QT + jnp.arange(QT, dtype=jnp.int32)
    order = jnp.argsort(scores, axis=-1)[:, :, :MAXK]
    return order.astype(jnp.int32)


def draw_key_counts(key, part):
    key = jax.random.fold_in(key, 11)
    key_level, key_light, key_heavy, key_pick, key_peak = jax.random.split(key, 5)
    level = jax.random.randint(key_level, (HEADS, 1), max(MAXK // 6, 1), MAXK // 2 + 1)
    light = 1 + jax.random.randint(key_light, (HEADS, QT), 0, 1 << 20) % level
    heavy_value = jax.random.randint(key_heavy, (HEADS, QT), MAXK // 2, MAXK + 1)
    heavy = jax.random.randint(key_pick, (HEADS, QT), 0, 8) == 0
    counts = jnp.where(heavy, heavy_value, light)
    peak = jax.random.randint(key_peak, (HEADS, 1), 0, QT)
    counts = jnp.where(jnp.arange(QT, dtype=jnp.int32)[None, :] == peak, MAXK, counts)
    return counts.astype(jnp.int32)


def shard_levels(rng, shape, shards, least, largest):
    loudness, own = 1.0, jax.random.fold_in(rng, 6)
    for axis_at, blocks in shards:
        steps = jnp.exp(jax.random.uniform(jax.random.fold_in(own, axis_at), (blocks,), jnp.float32, least / len(shards), largest / len(shards)))
        loudness = loudness * jnp.repeat(steps, shape[axis_at] // blocks).reshape([-1 if axis == axis_at else 1 for axis in range(len(shape))])
    return loudness


def normal_values(own_key, shape, spread, most, cuts=(), kind=jnp.bfloat16):
    drawn = jax.random.normal(own_key, shape, jnp.float32) * spread
    if len(cuts) > 0:
        drawn = shard_levels(own_key, shape, cuts, -0.22, 0.18) * drawn
    return jnp.clip(drawn, min=-most, max=most).astype(kind)


def setup_inputs(seed: int = 0) -> dict:
    key_list = jax.random.split(jax.random.key(seed), 7)
    return {
        "tokens": normal_values(key_list[0], (S, D), 1.0, 6.0, ((0, 512),)),
        "qkv_weight": normal_values(key_list[1], (D, HEADS, 3, HD), D ** -0.5, 0.109375, ((1, 16),)),
        "q_gain": jnp.clip(jnp.exp(math.log(2.0) - 1.3862944 * jax.random.uniform(key_list[2], (HEADS, HD), jnp.float32) ** shard_levels(key_list[2], (HEADS, HD), ((0, 16),), -0.2, 0.2)), 0.5, 2.0),
        "k_gain": jnp.clip(jnp.exp(math.log(2.0) - 1.3862944 * jax.random.uniform(key_list[3], (HEADS, HD), jnp.float32) ** shard_levels(key_list[3], (HEADS, HD), ((0, 16),), -0.2, 0.2)), 0.5, 2.0),
        "key_tiles": draw_key_tiles(jax.random.fold_in(key_list[6], 71), 0),
        "key_counts": draw_key_counts(jax.random.fold_in(key_list[6], 71), 0),
    }


def normalize(values, gain):
    mean_square = lax.optimization_barrier(jnp.mean(values * values, axis=-1, keepdims=True))
    return (values * lax.rsqrt(mean_square + 1e-06) * gain).astype(jnp.bfloat16)

def reference(tokens, qkv_weight, q_gain, k_gain, key_tiles, key_counts):
    length = tokens.shape[0]
    scale = HD ** (-0.5)

    def one_head(head):
        weight = lax.dynamic_index_in_dim(qkv_weight, head, 1, keepdims=False).reshape(D, 3 * HD)
        proj = jnp.dot(tokens, weight, preferred_element_type=jnp.float32).reshape(length, 3, HD)
        gain_q = lax.dynamic_index_in_dim(q_gain, head, 0, keepdims=False)
        gain_k = lax.dynamic_index_in_dim(k_gain, head, 0, keepdims=False)
        query_tiles = normalize(proj[:, 0], gain_q).reshape(QT, TILE, HD)
        key_block = normalize(proj[:, 1], gain_k).reshape(QT, TILE, HD)
        value_block = proj[:, 2].astype(jnp.bfloat16).reshape(QT, TILE, HD)
        lists = lax.dynamic_index_in_dim(key_tiles, head, 0, keepdims=False)
        counts = lax.dynamic_index_in_dim(key_counts, head, 0, keepdims=False)

        def one_tile(index):
            chosen = lists[index]
            picked_keys = key_block[chosen].reshape(MAXK * TILE, HD)
            picked_values = value_block[chosen].reshape(MAXK * TILE, HD)
            scores = jnp.dot(query_tiles[index], picked_keys.T, preferred_element_type=jnp.float32) * scale
            live = jnp.repeat(jnp.arange(MAXK, dtype=jnp.int32) < counts[index], TILE)
            weights = jnp.where(live[None, :], jnp.exp(scores), jnp.float32(0.0))
            total = lax.optimization_barrier(jnp.sum(weights, axis=-1, keepdims=True))
            acc = jnp.dot(weights.astype(jnp.bfloat16), picked_values, preferred_element_type=jnp.float32)
            return (acc / total).astype(jnp.bfloat16)
        return lax.map(one_tile, jnp.arange(QT, dtype=jnp.int32)).reshape(length, HD)
    outputs = lax.map(one_head, jnp.arange(HEADS, dtype=jnp.int32))
    return jnp.transpose(outputs, (1, 0, 2)).reshape(length, HEADS * HD)
```

```python
import functools
import jax
import jax.numpy as jnp
from jax import lax
from jax.experimental import pallas as pl
from jax.experimental.pallas import tpu as pltpu
from jax.sharding import PartitionSpec as P

TILE = 128
HEAD = 128
PIECE = 48
GROUP = 8
LOG2E = 1.4426950408889634
MESH_AXES = ("seq", "bal")
VMEM = pl.BlockSpec(memory_space=pltpu.VMEM)
SMEM = pl.BlockSpec(memory_space=pltpu.SMEM)


def plane_perm(phase, shift):
    pairs = []
    for bal in range(32):
        for y in range(4):
            for x in range(4):
                along_x = (bal % 2 == 0) == (phase == 1)
                to_y = y if along_x else (y + shift) % 4
                to_x = (x + shift) % 4 if along_x else x
                pairs.append(((4 * y + x) * 32 + bal, (4 * to_y + to_x) * 32 + bal))
    return pairs


def send(block, phase, shift):
    return lax.ppermute(block, MESH_AXES, plane_perm(phase, shift))


def gather_tokens(tokens):
    before = send(tokens, 1, 1)
    after = send(tokens, 1, -1)
    across = send(tokens, 1, 2)
    line = jnp.concatenate((tokens, before, after, across), axis=0)
    line_before = send(line, 2, 1)
    line_after = send(line, 2, -1)
    half = line.shape[0] // 2
    across_low = send(line_before[:half], 2, 1)
    across_high = send(line_after[half:], 2, -1)
    return line, line_before, line_after, across_low, across_high


def project_kernel(place, line, before, after, low, high, weight, q_gain, k_gain, q_out, kv_out):
    first = place[0]
    second = place[1]
    first_step = place[2]
    second_step = place[3]

    def normalize(values, gain):
        mean_square = jnp.mean(values * values, axis=-1, keepdims=True)
        return (values * lax.rsqrt(mean_square + 1e-06) * gain).astype(jnp.bfloat16)

    def project(block, shift, pieces):
        proj = jnp.dot(block[...], weight[...], preferred_element_type=jnp.float32)
        query = normalize(proj[:, :HEAD], q_gain[...])
        key = normalize(proj[:, HEAD : 2 * HEAD], k_gain[...])
        value = proj[:, 2 * HEAD :].astype(jnp.bfloat16)
        for at, piece in enumerate(pieces):
            spot = ((first + piece) % 4) * first_step + ((second + shift) % 4) * second_step
            rows = pl.ds(pl.multiple_of(spot * PIECE, PIECE), PIECE)
            here = slice(at * PIECE, (at + 1) * PIECE)
            q_out[rows, :] = query[here]
            kv_out[rows, :HEAD] = key[here]
            kv_out[rows, HEAD:] = value[here]

    project(line, 0, (0, 3, 1, 2))
    project(before, 3, (0, 3, 1, 2))
    project(after, 1, (0, 3, 1, 2))
    project(low, 2, (0, 3))
    project(high, 2, (1, 2))


def project(blocks, weight, q_gain, k_gain, place):
    rows = 16 * PIECE
    return pl.pallas_call(
        project_kernel,
        out_shape=(
            jax.ShapeDtypeStruct((rows, HEAD), jnp.bfloat16),
            jax.ShapeDtypeStruct((rows, 2 * HEAD), jnp.bfloat16),
        ),
        in_specs=[SMEM] + [VMEM] * 8,
        out_specs=(VMEM, VMEM),
        compiler_params=pltpu.CompilerParams(vmem_limit_bytes=40 * 1024 * 1024),
        name="project",
    )(place, *blocks, weight, q_gain, k_gain)


def attend_kernel(scale, lists, counts, q, kv, out):
    ones = jnp.ones((GROUP * TILE, HEAD), jnp.bfloat16)

    def one_slot(slot, _):
        query = q[slot]
        count = counts[slot]

        def turn(step, acc):
            picks = [lists[slot, step * GROUP + at] for at in range(GROUP)]
            keys = jnp.concatenate([kv[pick, :, :HEAD] for pick in picks], axis=0)
            values = jnp.concatenate([kv[pick, :, HEAD:] for pick in picks], axis=0)
            scores = lax.dot_general(
                query, keys, (((1,), (1,)), ((), ())), preferred_element_type=jnp.float32
            )
            live = (count - step * GROUP) * TILE
            column = lax.broadcasted_iota(jnp.int32, scores.shape, 1)
            weights = jnp.where(column < live, jnp.exp2(scores * scale), 0.0)
            return acc + jnp.dot(
                weights.astype(jnp.bfloat16),
                jnp.concatenate((values, ones), axis=1),
                preferred_element_type=jnp.float32,
            )

        acc = lax.fori_loop(
            0, (count + GROUP - 1) // GROUP, turn, jnp.zeros((TILE, 2 * HEAD), jnp.float32)
        )
        out[slot] = (acc[:, :HEAD] / acc[:, HEAD:]).astype(jnp.bfloat16)
        return 0

    lax.fori_loop(0, q.shape[0], one_slot, 0)


def attend(q, kv, lists, counts):
    scale = HEAD ** (-0.5) * LOG2E
    return pl.pallas_call(
        functools.partial(attend_kernel, scale),
        out_shape=jax.ShapeDtypeStruct(q.shape, jnp.bfloat16),
        in_specs=[SMEM, SMEM, VMEM, VMEM],
        out_specs=VMEM,
        compiler_params=pltpu.CompilerParams(vmem_limit_bytes=48 * 1024 * 1024),
        name="attend",
    )(lists, counts, q, kv)


def on_device(tokens, qkv_weight, q_gain, k_gain, key_tiles, key_counts):
    me_seq = lax.axis_index("seq")
    me_bal = lax.axis_index("bal")
    y, x = me_seq // 4, me_seq % 4
    core = me_bal % 2
    place = jnp.where(
        core == 0, jnp.stack((x, y, 1 + 0 * x, 4 + 0 * x)), jnp.stack((y, x, 4 + 0 * x, 1 + 0 * x))
    ).astype(jnp.int32)
    weight = qkv_weight.reshape(qkv_weight.shape[0], 3 * HEAD)
    blocks = gather_tokens(tokens)
    queries, pairs = project(blocks, weight, q_gain, k_gain, place)
    slots = queries.shape[0] // TILE
    all_pairs = lax.all_gather(pairs, "bal", axis=0, tiled=True)
    lists = lax.dynamic_slice_in_dim(key_tiles[0], me_bal * slots, slots, 0)
    counts = lax.dynamic_slice_in_dim(key_counts[0], me_bal * slots, slots, 0)
    result = attend(
        queries.reshape(slots, TILE, HEAD),
        all_pairs.reshape(-1, TILE, 2 * HEAD),
        lists,
        counts,
    )
    return lax.all_to_all(
        result.reshape(slots * TILE, HEAD), "seq", split_axis=0, concat_axis=1, tiled=True
    )


def solution(mesh):
    placed = (
        P(("bal", "seq"), None),
        P(None, "seq", None, None),
        P("seq", None),
        P("seq", None),
        P("seq", None, None),
        P("seq", None),
    )
    return jax.shard_map(
        on_device, mesh=mesh, in_specs=placed, out_specs=P(("bal", "seq"), None), check_vma=False
    )
```

```python
import functools
import jax
import jax.numpy as jnp
from jax import lax
from jax.experimental import pallas as pl
from jax.experimental.pallas import tpu as pltpu
from jax.sharding import PartitionSpec as P

TILE = 128
HEAD = 128
PIECE = 48
GROUP = 8
PLANES = 16
BLOCKS = 16
LOG2E = 1.4426950408889634
MESH_AXES = ("seq", "bal")
VMEM = pl.BlockSpec(memory_space=pltpu.VMEM)
SMEM = pl.BlockSpec(memory_space=pltpu.SMEM)


def plane_perm(phase, shift):
    pairs = []
    for bal in range(32):
        for y in range(4):
            for x in range(4):
                along_x = (bal % 2 == 0) == (phase == 1)
                to_y = y if along_x else (y + shift) % 4
                to_x = (x + shift) % 4 if along_x else x
                pairs.append(((4 * y + x) * 32 + bal, (4 * to_y + to_x) * 32 + bal))
    return pairs


def send(block, phase, shift):
    return lax.ppermute(block, MESH_AXES, plane_perm(phase, shift))


def swap_cores(block):
    return lax.ppermute(block, "bal", [(at, at ^ 1) for at in range(32)])


def pass_on(block):
    pairs = []
    for z in range(PLANES):
        pairs.append((2 * z, 2 * ((z + 1) % PLANES)))
        pairs.append((2 * z + 1, 2 * ((z - 1) % PLANES) + 1))
    return lax.ppermute(block, "bal", pairs)


def project_kernel(lines, place, *refs):
    first = place[0]
    second = place[1]
    first_step = place[2]
    second_step = place[3]
    count = sum(len(halves) for _, halves in lines)
    blocks = refs[:count]
    weight, q_gain, k_gain = refs[count : count + 3]
    q_out, kv_out = refs[-2:]
    if len(refs) > count + 5:
        carried = refs[count + 3]
        q_out[...] = carried[...]

    def normalize(values, gain):
        mean_square = jnp.mean(values * values, axis=-1, keepdims=True)
        return (values * lax.rsqrt(mean_square + 1e-06) * gain).astype(jnp.bfloat16)

    at_block = 0
    for at_line, (shift, halves) in enumerate(lines):
        for pieces in halves:
            proj = jnp.dot(
                blocks[at_block][...], weight[...], preferred_element_type=jnp.float32
            )
            at_block += 1
            query = normalize(proj[:, :HEAD], q_gain[...])
            key = normalize(proj[:, HEAD : 2 * HEAD], k_gain[...])
            value = proj[:, 2 * HEAD :].astype(jnp.bfloat16)
            for at, piece in enumerate(pieces):
                here = slice(at * PIECE, (at + 1) * PIECE)
                along = (first + piece) % 4
                spot = along * first_step + ((second + shift) % 4) * second_step
                rows = pl.ds(pl.multiple_of(spot * PIECE, PIECE), PIECE)
                q_out[rows, :] = query[here]
                rows = pl.ds(pl.multiple_of((at_line * 4 + along) * PIECE, PIECE), PIECE)
                kv_out[rows, :HEAD] = key[here]
                kv_out[rows, HEAD:] = value[here]


def project(lines, blocks, weight, q_gain, k_gain, place, carried=None):
    rows = 16 * PIECE
    more = () if carried is None else (carried,)
    return pl.pallas_call(
        functools.partial(project_kernel, lines),
        out_shape=(
            jax.ShapeDtypeStruct((rows, HEAD), jnp.bfloat16),
            jax.ShapeDtypeStruct((len(lines) * 4 * PIECE, 2 * HEAD), jnp.bfloat16),
        ),
        in_specs=[SMEM] + [VMEM] * (len(blocks) + 3 + len(more)),
        out_specs=(VMEM, VMEM),
        compiler_params=pltpu.CompilerParams(vmem_limit_bytes=32 * 1024 * 1024),
        name="project",
    )(place, *blocks, weight, q_gain, k_gain, *more)


def attend_kernel(scale, place, lists, counts, q, lines, *refs):
    pieces = refs[: BLOCKS]
    out, kv, ready = refs[BLOCKS:]
    second = place[1]
    core = place[4]
    plane = place[5]
    line_rows = 4 * PIECE

    def load(block):
        same = block <= PLANES // 2
        away = block if same else block - PLANES // 2
        from_plane = (plane + PLANES + away * (2 * core - 1)) % PLANES
        from_core = core if same else 1 - core
        bal = 2 * from_plane + from_core
        across = place[1] if same else place[0]
        along_step = jnp.where(from_core == 0, 1, 4)
        across_step = 5 - along_step
        for at_line, shift in enumerate((0, 3, 1, 2)):
            line_spot = ((across + shift) % 4) * across_step
            for along in range(4):
                spot = block * 16 + line_spot + along * along_step
                rows = pl.ds(pl.multiple_of(spot * PIECE, PIECE), PIECE)
                if at_line == 0:
                    start = bal * line_rows + along * PIECE
                    source = lines.at[pl.ds(pl.multiple_of(start, PIECE), PIECE), :]
                else:
                    start = (at_line - 1) * line_rows + along * PIECE
                    source = pieces[block].at[pl.ds(start, PIECE), :]
                pltpu.make_async_copy(source, kv.at[rows, :], ready).start()

    for block in range(BLOCKS):
        load(block)
    pltpu.make_async_copy(kv, kv, ready).wait()
    ones = jnp.ones((GROUP * TILE, HEAD), jnp.bfloat16)

    def one_slot(slot, _):
        query = q[slot]
        count = counts[slot]

        def turn(step, acc):
            picks = [
                pl.ds(pl.multiple_of(lists[slot, step * GROUP + at] * TILE, TILE), TILE)
                for at in range(GROUP)
            ]
            keys = jnp.concatenate([kv[pick, :HEAD] for pick in picks], axis=0)
            values = jnp.concatenate([kv[pick, HEAD:] for pick in picks], axis=0)
            scores = lax.dot_general(
                query, keys, (((1,), (1,)), ((), ())), preferred_element_type=jnp.float32
            )
            live = (count - step * GROUP) * TILE
            column = lax.broadcasted_iota(jnp.int32, scores.shape, 1)
            weights = jnp.where(column < live, jnp.exp2(scores * scale), 0.0)
            return acc + jnp.dot(
                weights.astype(jnp.bfloat16),
                jnp.concatenate((values, ones), axis=1),
                preferred_element_type=jnp.float32,
            )

        out[slot] = lax.fori_loop(
            0, (count + GROUP - 1) // GROUP, turn, jnp.zeros((TILE, 2 * HEAD), jnp.float32)
        )
        return 0

    lax.fori_loop(0, q.shape[0], one_slot, 0)


def attend(place, q, lines, pieces, lists, counts):
    scale = HEAD ** (-0.5) * LOG2E
    block_rows = 16 * PIECE
    return pl.pallas_call(
        functools.partial(attend_kernel, scale),
        out_shape=jax.ShapeDtypeStruct((q.shape[0], TILE, 2 * HEAD), jnp.float32),
        in_specs=[SMEM, SMEM, SMEM, VMEM] + [pl.BlockSpec(memory_space=pl.ANY)] * (1 + BLOCKS),
        out_specs=VMEM,
        scratch_shapes=[
            pltpu.VMEM((BLOCKS * block_rows, 2 * HEAD), jnp.bfloat16),
            pltpu.SemaphoreType.DMA,
        ],
        compiler_params=pltpu.CompilerParams(vmem_limit_bytes=32 * 1024 * 1024),
        name="attend",
    )(place, lists, counts, q, lines, *pieces)


def local_lists(key_tiles, key_counts, me_bal, slots):
    core, plane = me_bal % 2, me_bal // 2
    mine = jnp.stack((me_bal, me_bal ^ 1))
    tiles = key_tiles.reshape(2 * PLANES, slots, -1)[mine].reshape(2 * slots, -1)
    counts = key_counts.reshape(2 * PLANES, slots)[mine].reshape(2 * slots, 1)
    bal = tiles // slots
    away = ((bal // 2 - plane) * (2 * core - 1)) % PLANES
    same = bal % 2 == core
    half = PLANES // 2
    held = jnp.where(same, away <= half, (away >= 1) & (away < half))
    block = jnp.where(same, away, away + half)
    entries = jnp.arange(tiles.shape[1], dtype=jnp.int32)
    held = held & (entries[None, :] < counts)
    order = jnp.cumsum(held.astype(jnp.int32), axis=1) - 1
    picks = jnp.where(held, block * slots + tiles % slots, 0)
    placed = (order[:, :, None] == entries[None, None, :]) & held[:, :, None]
    lists = jnp.sum(jnp.where(placed, picks[:, :, None], 0), axis=1)
    return lists, jnp.sum(held.astype(jnp.int32), axis=1)


def on_device(tokens, qkv_weight, q_gain, k_gain, key_tiles, key_counts):
    me_seq = lax.axis_index("seq")
    me_bal = lax.axis_index("bal")
    y, x = me_seq // 4, me_seq % 4
    core = me_bal % 2
    place = jnp.stack(
        (
            jnp.where(core == 0, x, y),
            jnp.where(core == 0, y, x),
            jnp.where(core == 0, 1, 4),
            jnp.where(core == 0, 4, 1),
            core,
            me_bal // 2,
        )
    ).astype(jnp.int32)
    weight = qkv_weight.reshape(qkv_weight.shape[0], 3 * HEAD)
    slots = 16 * PIECE // TILE
    lists, counts = local_lists(key_tiles[0], key_counts[0], me_bal, slots)

    before = send(tokens, 1, 1)
    after = send(tokens, 1, -1)
    across = send(tokens, 1, 2)
    low = jnp.concatenate((tokens, before), axis=0)
    before_low = send(low, 2, 1)
    high = jnp.concatenate((after, across), axis=0)
    after_high = send(high, 2, -1)
    after_low = send(low, 2, -1)
    before_high = send(high, 2, 1)
    across_low = send(before_low, 2, 1)
    across_high = send(after_high, 2, -1)

    halves = ((0, 3), (1, 2))
    own_queries, own_line = project(
        ((0, halves),), (low, high), weight, q_gain, k_gain, place
    )
    lines = lax.all_gather(own_line, "bal", axis=0, tiled=True)
    queries, rest = project(
        ((3, halves), (1, halves), (2, halves)),
        (before_low, before_high, after_low, after_high, across_low, across_high),
        weight,
        q_gain,
        k_gain,
        place,
        own_queries,
    )
    same, other = [rest], []
    same.append(pass_on(rest))
    swapped = swap_cores(jnp.concatenate((rest.reshape(-1, HEAD), queries), axis=0))
    moving = swapped[: 2 * rest.shape[0]].reshape(rest.shape)
    other_queries = swapped[2 * rest.shape[0] :]
    for step in range(1, PLANES // 2):
        moving = pass_on(moving)
        other.append(moving)
        same.append(pass_on(same[-1]))

    both = jnp.concatenate((queries, other_queries), axis=0).reshape(2 * slots, TILE, HEAD)
    sums = attend(place, both, lines, same + other, lists, counts)
    sums = sums[:slots] + swap_cores(sums[slots:])
    result = (sums[:, :, :HEAD] / sums[:, :, HEAD:]).astype(jnp.bfloat16)
    return lax.all_to_all(
        result.reshape(slots * TILE, HEAD), "seq", split_axis=0, concat_axis=1, tiled=True
    )


def solution(mesh):
    placed = (
        P(("bal", "seq"), None),
        P(None, "seq", None, None),
        P("seq", None),
        P("seq", None),
        P("seq", None, None),
        P("seq", None),
    )
    return jax.shard_map(
        on_device, mesh=mesh, in_specs=placed, out_specs=P(("bal", "seq"), None), check_vma=False
    )
```

```python
import functools
import jax
import jax.numpy as jnp
from jax import lax
from jax.experimental import pallas as pl
from jax.experimental.pallas import tpu as pltpu
from jax.sharding import PartitionSpec as P

TILE = 128
HEAD = 128
PIECE = 48
GROUP = 8
LOG2E = 1.4426950408889634
MESH_AXES = ("seq", "bal")
VMEM = pl.BlockSpec(memory_space=pltpu.VMEM)
SMEM = pl.BlockSpec(memory_space=pltpu.SMEM)


def plane_perm(phase, shift):
    pairs = []
    for bal in range(32):
        for y in range(4):
            for x in range(4):
                along_x = (bal % 2 == 0) == (phase == 1)
                to_y = y if along_x else (y + shift) % 4
                to_x = (x + shift) % 4 if along_x else x
                pairs.append(((4 * y + x) * 32 + bal, (4 * to_y + to_x) * 32 + bal))
    return pairs


def send(block, phase, shift):
    return lax.ppermute(block, MESH_AXES, plane_perm(phase, shift))


def project_kernel(lines, carry, place, *refs):
    first = place[0]
    second = place[1]
    first_step = place[2]
    second_step = place[3]
    count = sum(len(halves) for _, halves in lines)
    blocks = refs[:count]
    weight, q_gain, k_gain = refs[count : count + 3]
    q_out, kv_out = refs[-2:]
    if carry:
        q_out[...] = refs[count + 3][...]
        kv_out[...] = refs[count + 4][...]

    def normalize(values, gain):
        mean_square = jnp.mean(values * values, axis=-1, keepdims=True)
        return (values * lax.rsqrt(mean_square + 1e-06) * gain).astype(jnp.bfloat16)

    whole = jnp.concatenate([weight[at] for at in range(3)], axis=1)
    at_block = 0
    for shift, halves in lines:
        for pieces in halves:
            proj = jnp.dot(blocks[at_block][...], whole, preferred_element_type=jnp.float32)
            at_block += 1
            query = normalize(proj[:, :HEAD], q_gain[...])
            key = normalize(proj[:, HEAD : 2 * HEAD], k_gain[...])
            value = proj[:, 2 * HEAD :].astype(jnp.bfloat16)
            for at, piece in enumerate(pieces):
                here = slice(at * PIECE, (at + 1) * PIECE)
                spot = ((first + piece) % 4) * first_step + ((second + shift) % 4) * second_step
                rows = pl.ds(pl.multiple_of(spot * PIECE, PIECE), PIECE)
                q_out[rows, :] = query[here]
                kv_out[rows, :HEAD] = key[here]
                kv_out[rows, HEAD:] = value[here]


def project(lines, blocks, weight, q_gain, k_gain, place, carried=()):
    rows = 16 * PIECE
    return pl.pallas_call(
        functools.partial(project_kernel, lines, len(carried) > 0),
        out_shape=(
            jax.ShapeDtypeStruct((rows, HEAD), jnp.bfloat16),
            jax.ShapeDtypeStruct((rows, 2 * HEAD), jnp.bfloat16),
        ),
        in_specs=[SMEM] + [VMEM] * (len(blocks) + 3 + len(carried)),
        out_specs=(VMEM, VMEM),
        compiler_params=pltpu.CompilerParams(vmem_limit_bytes=32 * 1024 * 1024),
        name="project",
    )(place, *blocks, weight, q_gain, k_gain, *carried)


def attend_kernel(scale, lists, counts, q, kv, out, held, ready):
    ones = jnp.ones((GROUP * TILE, HEAD), jnp.bfloat16)
    slots = q.shape[0]

    def fetch(slot, step, buffer):
        for at in range(GROUP):
            pick = lists[slot, step * GROUP + at]
            pltpu.make_async_copy(kv.at[pick], held.at[buffer, at], ready.at[buffer]).start()

    fetch(0, 0, 0)

    def one_slot(slot, turns_before):
        query = q[slot]
        count = counts[slot]
        turns = (count + GROUP - 1) // GROUP

        def turn(step, acc):
            buffer = (turns_before + step) % 2
            last = step + 1 == turns
            next_slot = jnp.where(last, slot + 1, slot)
            next_step = jnp.where(last, 0, step + 1)

            @pl.when(next_slot < slots)
            def _():
                fetch(next_slot, next_step, 1 - buffer)

            pltpu.make_async_copy(held.at[buffer], held.at[buffer], ready.at[buffer]).wait()
            keys = held[buffer, :, :, :HEAD].reshape(GROUP * TILE, HEAD)
            values = held[buffer, :, :, HEAD:].reshape(GROUP * TILE, HEAD)
            scores = lax.dot_general(
                query, keys, (((1,), (1,)), ((), ())), preferred_element_type=jnp.float32
            )
            live = (count - step * GROUP) * TILE
            column = lax.broadcasted_iota(jnp.int32, scores.shape, 1)
            weights = jnp.where(column < live, jnp.exp2(scores * scale), 0.0)
            return acc + jnp.dot(
                weights.astype(jnp.bfloat16),
                jnp.concatenate((values, ones), axis=1),
                preferred_element_type=jnp.float32,
            )

        acc = lax.fori_loop(0, turns, turn, jnp.zeros((TILE, 2 * HEAD), jnp.float32))
        out[slot] = (acc[:, :HEAD] / acc[:, HEAD:]).astype(jnp.bfloat16)
        return turns_before + turns

    lax.fori_loop(0, slots, one_slot, 0)


def attend(q, kv, lists, counts):
    scale = HEAD ** (-0.5) * LOG2E
    return pl.pallas_call(
        functools.partial(attend_kernel, scale),
        out_shape=jax.ShapeDtypeStruct(q.shape, jnp.bfloat16),
        in_specs=[SMEM, SMEM, VMEM, pl.BlockSpec(memory_space=pl.ANY)],
        out_specs=VMEM,
        scratch_shapes=[
            pltpu.VMEM((2, GROUP, TILE, 2 * HEAD), jnp.bfloat16),
            pltpu.SemaphoreType.DMA((2,)),
        ],
        compiler_params=pltpu.CompilerParams(vmem_limit_bytes=56 * 1024 * 1024),
        name="attend",
    )(lists, counts, q, kv)


def on_device(tokens, qkv_weight, q_gain, k_gain, key_tiles, key_counts):
    me_seq = lax.axis_index("seq")
    me_bal = lax.axis_index("bal")
    y, x = me_seq // 4, me_seq % 4
    core = me_bal % 2
    place = jnp.stack(
        (
            jnp.where(core == 0, x, y),
            jnp.where(core == 0, y, x),
            jnp.where(core == 0, 1, 4),
            jnp.where(core == 0, 4, 1),
        )
    ).astype(jnp.int32)
    slots = 16 * PIECE // TILE
    lists = lax.dynamic_slice_in_dim(key_tiles[0], me_bal * slots, slots, 0)
    counts = lax.dynamic_slice_in_dim(key_counts[0], me_bal * slots, slots, 0)

    before = send(tokens, 1, 1)
    after = send(tokens, 1, -1)
    across = send(tokens, 1, 2)
    low = jnp.concatenate((tokens, before), axis=0)
    before_low = send(low, 2, 1)
    high = jnp.concatenate((after, across), axis=0)
    after_high = send(high, 2, -1)
    after_low = send(low, 2, -1)
    before_high = send(high, 2, 1)
    across_low = send(before_low, 2, 1)
    across_high = send(after_high, 2, -1)

    weight = jnp.transpose(qkv_weight[:, 0], (1, 0, 2))
    halves = ((0, 3), (1, 2))
    early = project(
        ((0, halves), (3, halves), (1, halves)),
        (low, high, before_low, before_high, after_low, after_high),
        weight,
        q_gain,
        k_gain,
        place,
    )
    queries, pairs = project(
        ((2, halves),), (across_low, across_high), weight, q_gain, k_gain, place, early
    )
    all_pairs = lax.all_gather(pairs, "bal", axis=0, tiled=True)
    result = attend(
        queries.reshape(slots, TILE, HEAD),
        all_pairs.reshape(-1, TILE, 2 * HEAD),
        lists,
        counts,
    )
    return lax.all_to_all(
        result.reshape(slots * TILE, HEAD), "seq", split_axis=0, concat_axis=1, tiled=True
    )


def solution(mesh):
    placed = (
        P(("bal", "seq"), None),
        P(None, "seq", None, None),
        P("seq", None),
        P("seq", None),
        P("seq", None, None),
        P("seq", None),
    )
    return jax.shard_map(
        on_device, mesh=mesh, in_specs=placed, out_specs=P(("bal", "seq"), None), check_vma=False
    )
```

```python
import functools
import jax
import jax.numpy as jnp
from jax import lax
from jax.experimental import pallas as pl
from jax.experimental.pallas import tpu as pltpu
from jax.sharding import PartitionSpec as P

TILE = 128
HEAD = 128
PIECE = 48
GROUP = 8
BUFFERS = 8
LOG2E = 1.4426950408889634
MESH_AXES = ("seq", "bal")
VMEM = pl.BlockSpec(memory_space=pltpu.VMEM)
SMEM = pl.BlockSpec(memory_space=pltpu.SMEM)


def plane_perm(phase, shift):
    pairs = []
    for bal in range(32):
        for y in range(4):
            for x in range(4):
                along_x = (bal % 2 == 0) == (phase == 1)
                to_y = y if along_x else (y + shift) % 4
                to_x = (x + shift) % 4 if along_x else x
                pairs.append(((4 * y + x) * 32 + bal, (4 * to_y + to_x) * 32 + bal))
    return pairs


def send(block, phase, shift):
    return lax.ppermute(block, MESH_AXES, plane_perm(phase, shift))


def project_kernel(shares, place, *refs):
    count = len(shares)
    blocks = refs[:count]
    weight, q_gain, k_gain = refs[count : count + 3]
    q_out, kv_out, block_in, weight_in, gain_in, q_held, kv_held, arrive, leave = refs[-9:]
    first = place[0]
    second = place[1]
    first_step = place[2]
    second_step = place[3]
    half = 2 * PIECE

    copies = [
        pltpu.make_async_copy(weight, weight_in, arrive.at[count]),
        pltpu.make_async_copy(q_gain, gain_in.at[0], arrive.at[count + 1]),
        pltpu.make_async_copy(k_gain, gain_in.at[1], arrive.at[count + 2]),
    ]
    for at in range(count):
        copies.append(pltpu.make_async_copy(blocks[at], block_in.at[at], arrive.at[at]))
    for copy in copies:
        copy.start()
    for copy in copies[:3]:
        copy.wait()

    def normalize(values, gain):
        mean_square = jnp.mean(values * values, axis=-1, keepdims=True)
        return (values * lax.rsqrt(mean_square + 1e-06) * gain).astype(jnp.bfloat16)

    whole = jnp.concatenate([weight_in[at] for at in range(3)], axis=1)
    for at, (shift, pieces) in enumerate(shares):
        copies[3 + at].wait()
        proj = jnp.dot(block_in[at], whole, preferred_element_type=jnp.float32)
        here = slice(at * half, (at + 1) * half)
        q_held[here, :] = normalize(proj[:, :HEAD], gain_in[0])
        kv_held[here, :HEAD] = normalize(proj[:, HEAD : 2 * HEAD], gain_in[1])
        kv_held[here, HEAD:] = proj[:, 2 * HEAD :].astype(jnp.bfloat16)
        for order, piece in enumerate(pieces):
            spot = ((first + piece) % 4) * first_step + ((second + shift) % 4) * second_step
            rows = pl.ds(pl.multiple_of(spot * PIECE, PIECE), PIECE)
            source = pl.ds(at * half + order * PIECE, PIECE)
            pltpu.make_async_copy(q_held.at[source, :], q_out.at[rows, :], leave.at[0]).start()
            pltpu.make_async_copy(kv_held.at[source, :], kv_out.at[rows, :], leave.at[1]).start()
    pltpu.make_async_copy(q_held, q_held, leave.at[0]).wait()
    pltpu.make_async_copy(kv_held, kv_held, leave.at[1]).wait()


def project(shares, blocks, weight, q_gain, k_gain, place, begun=()):
    rows = 16 * PIECE
    count = len(blocks)
    done_rows = count * 2 * PIECE
    width = blocks[0].shape[1]
    anywhere = pl.BlockSpec(memory_space=pl.ANY)
    return pl.pallas_call(
        functools.partial(project_kernel, shares),
        out_shape=(
            jax.ShapeDtypeStruct((rows, HEAD), jnp.bfloat16),
            jax.ShapeDtypeStruct((rows, 2 * HEAD), jnp.bfloat16),
        ),
        in_specs=[SMEM] + [anywhere] * (count + 3 + len(begun)),
        out_specs=(anywhere, anywhere),
        scratch_shapes=[
            pltpu.VMEM((count, 2 * PIECE, width), jnp.bfloat16),
            pltpu.VMEM((3, width, HEAD), jnp.bfloat16),
            pltpu.VMEM((2, 1, HEAD), jnp.float32),
            pltpu.VMEM((done_rows, HEAD), jnp.bfloat16),
            pltpu.VMEM((done_rows, 2 * HEAD), jnp.bfloat16),
            pltpu.SemaphoreType.DMA((count + 3,)),
            pltpu.SemaphoreType.DMA((2,)),
        ],
        input_output_aliases={count + 4: 0, count + 5: 1} if begun else {},
        compiler_params=pltpu.CompilerParams(vmem_limit_bytes=56 * 1024 * 1024),
        name="project",
    )(place, *blocks, weight, q_gain, k_gain, *begun)


def attend_kernel(scale, lists, counts, q, kv, out, held, ready):
    ones = jnp.ones((GROUP * TILE, HEAD), jnp.bfloat16)
    slots = q.shape[0]

    def turns_of(slot):
        return (counts[slot] + GROUP - 1) // GROUP

    def fetch(ahead, buffer):
        slot, step = ahead

        @pl.when(slot < slots)
        def _():
            for at in range(GROUP):
                pick = lists[slot, step * GROUP + at]
                pltpu.make_async_copy(kv.at[pick], held.at[buffer, at], ready.at[buffer]).start()

        last = step + 1 >= turns_of(jnp.minimum(slot, slots - 1))
        return jnp.where(last, slot + 1, slot), jnp.where(last, 0, step + 1)

    ahead = (jnp.int32(0), jnp.int32(0))
    for buffer in range(BUFFERS - 1):
        ahead = fetch(ahead, buffer)

    def one_slot(slot, carry):
        query = q[slot]
        count = counts[slot]

        def turn(step, carry):
            acc, group, ahead = carry
            buffer = group % BUFFERS
            ahead = fetch(ahead, (group + BUFFERS - 1) % BUFFERS)
            pltpu.make_async_copy(held.at[buffer], held.at[buffer], ready.at[buffer]).wait()
            keys = held[buffer, :, :, :HEAD].reshape(GROUP * TILE, HEAD)
            values = held[buffer, :, :, HEAD:].reshape(GROUP * TILE, HEAD)
            scores = lax.dot_general(
                query, keys, (((1,), (1,)), ((), ())), preferred_element_type=jnp.float32
            )
            live = (count - step * GROUP) * TILE
            column = lax.broadcasted_iota(jnp.int32, scores.shape, 1)
            weights = jnp.where(column < live, jnp.exp2(scores * scale), 0.0)
            acc = acc + jnp.dot(
                weights.astype(jnp.bfloat16),
                jnp.concatenate((values, ones), axis=1),
                preferred_element_type=jnp.float32,
            )
            return acc, group + 1, ahead

        acc, group, ahead = lax.fori_loop(
            0, turns_of(slot), turn, (jnp.zeros((TILE, 2 * HEAD), jnp.float32), *carry)
        )
        out[slot] = (acc[:, :HEAD] / acc[:, HEAD:]).astype(jnp.bfloat16)
        return group, ahead

    lax.fori_loop(0, slots, one_slot, (jnp.int32(0), ahead))


def attend(q, kv, lists, counts):
    scale = HEAD ** (-0.5) * LOG2E
    return pl.pallas_call(
        functools.partial(attend_kernel, scale),
        out_shape=jax.ShapeDtypeStruct(q.shape, jnp.bfloat16),
        in_specs=[SMEM, SMEM, VMEM, pl.BlockSpec(memory_space=pl.ANY)],
        out_specs=VMEM,
        scratch_shapes=[
            pltpu.VMEM((BUFFERS, GROUP, TILE, 2 * HEAD), jnp.bfloat16),
            pltpu.SemaphoreType.DMA((BUFFERS,)),
        ],
        compiler_params=pltpu.CompilerParams(vmem_limit_bytes=56 * 1024 * 1024),
        name="attend",
    )(lists, counts, q, kv)


def on_device(tokens, qkv_weight, q_gain, k_gain, key_tiles, key_counts):
    me_seq = lax.axis_index("seq")
    me_bal = lax.axis_index("bal")
    y, x = me_seq // 4, me_seq % 4
    core = me_bal % 2
    place = jnp.stack(
        (
            jnp.where(core == 0, x, y),
            jnp.where(core == 0, y, x),
            jnp.where(core == 0, 1, 4),
            jnp.where(core == 0, 4, 1),
        )
    ).astype(jnp.int32)
    slots = 16 * PIECE // TILE
    lists = lax.dynamic_slice_in_dim(key_tiles[0], me_bal * slots, slots, 0)
    counts = lax.dynamic_slice_in_dim(key_counts[0], me_bal * slots, slots, 0)

    before = send(tokens, 1, 1)
    after = send(tokens, 1, -1)
    across = send(tokens, 1, 2)
    low = jnp.concatenate((tokens, before), axis=0)
    before_low = send(low, 2, 1)
    high = jnp.concatenate((after, across), axis=0)
    after_high = send(high, 2, -1)
    after_low = send(low, 2, -1)
    before_high = send(high, 2, 1)
    across_low = send(before_low, 2, 1)
    across_high = send(after_high, 2, -1)

    weight = jnp.transpose(qkv_weight[:, 0], (1, 0, 2))
    low_pieces, high_pieces = (0, 3), (1, 2)
    begun = project(
        ((0, low_pieces), (0, high_pieces), (3, low_pieces), (1, high_pieces)),
        (low, high, before_low, after_high),
        weight,
        q_gain,
        k_gain,
        place,
    )
    queries, pairs = project(
        ((1, low_pieces), (3, high_pieces), (2, low_pieces), (2, high_pieces)),
        (after_low, before_high, across_low, across_high),
        weight,
        q_gain,
        k_gain,
        place,
        begun,
    )
    all_pairs = lax.all_gather(pairs, "bal", axis=0, tiled=True)
    result = attend(
        queries.reshape(slots, TILE, HEAD),
        all_pairs.reshape(-1, TILE, 2 * HEAD),
        lists,
        counts,
    )
    return lax.all_to_all(
        result.reshape(slots * TILE, HEAD), "seq", split_axis=0, concat_axis=1, tiled=True
    )


def solution(mesh):
    placed = (
        P(("bal", "seq"), None),
        P(None, "seq", None, None),
        P("seq", None),
        P("seq", None),
        P("seq", None, None),
        P("seq", None),
    )
    return jax.shard_map(
        on_device, mesh=mesh, in_specs=placed, out_specs=P(("bal", "seq"), None), check_vma=False
    )
```

```python
import functools
import jax
import jax.numpy as jnp
from jax import lax
from jax.experimental import pallas as pl
from jax.experimental.pallas import tpu as pltpu
from jax.sharding import PartitionSpec as P

TILE = 128
HEAD = 128
PIECE = 48
GROUP = 8
BUFFERS = 8
LOG2E = 1.4426950408889634
MESH_AXES = ("seq", "bal")
VMEM = pl.BlockSpec(memory_space=pltpu.VMEM)
SMEM = pl.BlockSpec(memory_space=pltpu.SMEM)


def plane_perm(phase, shift):
    pairs = []
    for bal in range(32):
        for y in range(4):
            for x in range(4):
                along_x = (bal % 2 == 0) == (phase == 1)
                to_y = y if along_x else (y + shift) % 4
                to_x = (x + shift) % 4 if along_x else x
                pairs.append(((4 * y + x) * 32 + bal, (4 * to_y + to_x) * 32 + bal))
    return pairs


def send(block, phase, shift):
    return lax.ppermute(block, MESH_AXES, plane_perm(phase, shift))


def project_kernel(shares, place, *refs):
    count = len(shares)
    blocks = refs[:count]
    weight, q_gain, k_gain = refs[count : count + 3]
    q_out, kv_out, block_in, weight_in, gain_in, q_held, kv_held, arrive, leave = refs[-9:]
    first = place[0]
    second = place[1]
    first_step = place[2]
    second_step = place[3]
    half = 2 * PIECE

    copies = [
        pltpu.make_async_copy(weight, weight_in, arrive.at[count]),
        pltpu.make_async_copy(q_gain, gain_in.at[0], arrive.at[count + 1]),
        pltpu.make_async_copy(k_gain, gain_in.at[1], arrive.at[count + 2]),
    ]
    for at in range(count):
        copies.append(pltpu.make_async_copy(blocks[at], block_in.at[at], arrive.at[at]))
    for copy in copies:
        copy.start()
    for copy in copies[:3]:
        copy.wait()

    def normalize(values, gain):
        mean_square = jnp.mean(values * values, axis=-1, keepdims=True)
        return (values * lax.rsqrt(mean_square + 1e-06) * gain).astype(jnp.bfloat16)

    whole = jnp.concatenate([weight_in[at] for at in range(3)], axis=1)
    for copy in copies[3:]:
        copy.wait()
    rows = block_in[...].reshape(count * half, block_in.shape[2])
    proj = jnp.dot(rows, whole, preferred_element_type=jnp.float32)
    q_held[...] = normalize(proj[:, :HEAD], gain_in[0])
    kv_held[:, :HEAD] = normalize(proj[:, HEAD : 2 * HEAD], gain_in[1])
    kv_held[:, HEAD:] = proj[:, 2 * HEAD :].astype(jnp.bfloat16)
    for at, (shift, pieces) in enumerate(shares):
        for order, piece in enumerate(pieces):
            spot = ((first + piece) % 4) * first_step + ((second + shift) % 4) * second_step
            target = pl.ds(pl.multiple_of(spot * PIECE, PIECE), PIECE)
            source = pl.ds(at * half + order * PIECE, PIECE)
            pltpu.make_async_copy(q_held.at[source, :], q_out.at[target, :], leave.at[0]).start()
            pltpu.make_async_copy(kv_held.at[source, :], kv_out.at[target, :], leave.at[1]).start()
    pltpu.make_async_copy(q_held, q_held, leave.at[0]).wait()
    pltpu.make_async_copy(kv_held, kv_held, leave.at[1]).wait()


def project(shares, blocks, weight, q_gain, k_gain, place, begun=()):
    rows = 16 * PIECE
    count = len(blocks)
    done_rows = count * 2 * PIECE
    width = blocks[0].shape[1]
    anywhere = pl.BlockSpec(memory_space=pl.ANY)
    return pl.pallas_call(
        functools.partial(project_kernel, shares),
        out_shape=(
            jax.ShapeDtypeStruct((rows, HEAD), jnp.bfloat16),
            jax.ShapeDtypeStruct((rows, 2 * HEAD), jnp.bfloat16),
        ),
        in_specs=[SMEM] + [anywhere] * (count + 3 + len(begun)),
        out_specs=(anywhere, anywhere),
        scratch_shapes=[
            pltpu.VMEM((count, 2 * PIECE, width), jnp.bfloat16),
            pltpu.VMEM((3, width, HEAD), jnp.bfloat16),
            pltpu.VMEM((2, 1, HEAD), jnp.float32),
            pltpu.VMEM((done_rows, HEAD), jnp.bfloat16),
            pltpu.VMEM((done_rows, 2 * HEAD), jnp.bfloat16),
            pltpu.SemaphoreType.DMA((count + 3,)),
            pltpu.SemaphoreType.DMA((2,)),
        ],
        input_output_aliases={count + 4: 0, count + 5: 1} if begun else {},
        compiler_params=pltpu.CompilerParams(vmem_limit_bytes=56 * 1024 * 1024),
        name="project",
    )(place, *blocks, weight, q_gain, k_gain, *begun)


def attend_kernel(scale, picks, counts, q, kv, out, held, ready):
    ones = jnp.ones((GROUP * TILE, HEAD), jnp.bfloat16)

    def fetch(group, buffer):
        for at in range(GROUP):
            pick = picks[group * GROUP + at]
            pltpu.make_async_copy(kv.at[pick], held.at[buffer, at], ready.at[buffer]).start()

    def arrive(buffer):
        pltpu.make_async_copy(held.at[buffer], held.at[buffer], ready.at[buffer]).wait()

    for buffer in range(BUFFERS - 1):
        fetch(buffer, buffer)

    def one_slot(slot, group):
        query = q[slot]
        count = counts[slot]
        turns = (count + GROUP - 1) // GROUP

        def turn(step, acc):
            at = group + step
            buffer = at % BUFFERS
            fetch(at + BUFFERS - 1, (at + BUFFERS - 1) % BUFFERS)
            arrive(buffer)
            keys = held[buffer, :, :, :HEAD].reshape(GROUP * TILE, HEAD)
            values = held[buffer, :, :, HEAD:].reshape(GROUP * TILE, HEAD)
            scores = lax.dot_general(
                query, keys, (((1,), (1,)), ((), ())), preferred_element_type=jnp.float32
            )
            live = (count - step * GROUP) * TILE
            column = lax.broadcasted_iota(jnp.int32, scores.shape, 1)
            weights = jnp.where(column < live, jnp.exp2(scores * scale), 0.0)
            return acc + jnp.dot(
                weights.astype(jnp.bfloat16),
                jnp.concatenate((values, ones), axis=1),
                preferred_element_type=jnp.float32,
            )

        acc = lax.fori_loop(0, turns, turn, jnp.zeros((TILE, 2 * HEAD), jnp.float32))
        out[slot] = (acc[:, :HEAD] / acc[:, HEAD:]).astype(jnp.bfloat16)
        return group + turns

    groups = lax.fori_loop(0, q.shape[0], one_slot, jnp.int32(0))
    for extra in range(BUFFERS - 1):
        arrive((groups + extra) % BUFFERS)


def flat_picks(lists, counts):
    slots, listed = lists.shape
    turns = (counts + GROUP - 1) // GROUP
    ends = jnp.cumsum(turns)
    room = slots * (listed // GROUP) + BUFFERS
    group = jnp.arange(room, dtype=jnp.int32)
    slot = jnp.sum((group[:, None] >= ends[None, :]).astype(jnp.int32), axis=1)
    slot = jnp.minimum(slot, slots - 1)
    step = jnp.clip(group - (ends - turns)[slot], 0, listed // GROUP - 1)
    return lists.reshape(slots * (listed // GROUP), GROUP)[
        slot * (listed // GROUP) + step
    ].reshape(-1)


def attend(q, kv, lists, counts):
    scale = HEAD ** (-0.5) * LOG2E
    return pl.pallas_call(
        functools.partial(attend_kernel, scale),
        out_shape=jax.ShapeDtypeStruct(q.shape, jnp.bfloat16),
        in_specs=[SMEM, SMEM, VMEM, pl.BlockSpec(memory_space=pl.ANY)],
        out_specs=VMEM,
        scratch_shapes=[
            pltpu.VMEM((BUFFERS, GROUP, TILE, 2 * HEAD), jnp.bfloat16),
            pltpu.SemaphoreType.DMA((BUFFERS,)),
        ],
        compiler_params=pltpu.CompilerParams(vmem_limit_bytes=56 * 1024 * 1024),
        name="attend",
    )(flat_picks(lists, counts), counts, q, kv)


def on_device(tokens, qkv_weight, q_gain, k_gain, key_tiles, key_counts):
    me_seq = lax.axis_index("seq")
    me_bal = lax.axis_index("bal")
    y, x = me_seq // 4, me_seq % 4
    core = me_bal % 2
    place = jnp.stack(
        (
            jnp.where(core == 0, x, y),
            jnp.where(core == 0, y, x),
            jnp.where(core == 0, 1, 4),
            jnp.where(core == 0, 4, 1),
        )
    ).astype(jnp.int32)
    slots = 16 * PIECE // TILE
    lists = lax.dynamic_slice_in_dim(key_tiles[0], me_bal * slots, slots, 0)
    counts = lax.dynamic_slice_in_dim(key_counts[0], me_bal * slots, slots, 0)

    before = send(tokens, 1, 1)
    after = send(tokens, 1, -1)
    across = send(tokens, 1, 2)
    low = jnp.concatenate((tokens, before), axis=0)
    before_low = send(low, 2, 1)
    high = jnp.concatenate((after, across), axis=0)
    after_high = send(high, 2, -1)
    after_low = send(low, 2, -1)
    before_high = send(high, 2, 1)
    across_low = send(before_low, 2, 1)
    across_high = send(after_high, 2, -1)

    weight = jnp.transpose(qkv_weight[:, 0], (1, 0, 2))
    low_pieces, high_pieces = (0, 3), (1, 2)
    begun = project(
        ((0, low_pieces), (0, high_pieces), (3, low_pieces), (1, high_pieces)),
        (low, high, before_low, after_high),
        weight,
        q_gain,
        k_gain,
        place,
    )
    begun = project(
        ((1, low_pieces), (3, high_pieces)),
        (after_low, before_high),
        weight,
        q_gain,
        k_gain,
        place,
        begun,
    )
    queries, pairs = project(
        ((2, low_pieces), (2, high_pieces)),
        (across_low, across_high),
        weight,
        q_gain,
        k_gain,
        place,
        begun,
    )
    all_pairs = lax.all_gather(pairs, "bal", axis=0, tiled=True)
    result = attend(
        queries.reshape(slots, TILE, HEAD),
        all_pairs.reshape(-1, TILE, 2 * HEAD),
        lists,
        counts,
    )
    return lax.all_to_all(
        result.reshape(slots * TILE, HEAD), "seq", split_axis=0, concat_axis=1, tiled=True
    )


def solution(mesh):
    placed = (
        P(("bal", "seq"), None),
        P(None, "seq", None, None),
        P("seq", None),
        P("seq", None),
        P("seq", None, None),
        P("seq", None),
    )
    return jax.shard_map(
        on_device, mesh=mesh, in_specs=placed, out_specs=P(("bal", "seq"), None), check_vma=False
    )
```

```python
import functools
import jax
import jax.numpy as jnp
from jax import lax
from jax.experimental import pallas as pl
from jax.experimental.pallas import tpu as pltpu
from jax.sharding import PartitionSpec as P

TILE = 128
HEAD = 128
PIECE = 48
GROUP = 8
PLANES = 16
BLOCKS = 16
LOG2E = 1.4426950408889634
MESH_AXES = ("seq", "bal")
VMEM = pl.BlockSpec(memory_space=pltpu.VMEM)
SMEM = pl.BlockSpec(memory_space=pltpu.SMEM)


def plane_perm(phase, shift):
    pairs = []
    for bal in range(32):
        for y in range(4):
            for x in range(4):
                along_x = (bal % 2 == 0) == (phase == 1)
                to_y = y if along_x else (y + shift) % 4
                to_x = (x + shift) % 4 if along_x else x
                pairs.append(((4 * y + x) * 32 + bal, (4 * to_y + to_x) * 32 + bal))
    return pairs


def send(block, phase, shift):
    return lax.ppermute(block, MESH_AXES, plane_perm(phase, shift))


def swap_cores(block):
    return lax.ppermute(block, "bal", [(at, at ^ 1) for at in range(32)])


def pass_on(block):
    pairs = []
    for z in range(PLANES):
        pairs.append((2 * z, 2 * ((z + 1) % PLANES)))
        pairs.append((2 * z + 1, 2 * ((z - 1) % PLANES) + 1))
    return lax.ppermute(block, "bal", pairs)


def project_kernel(shares, place, *refs):
    count = len(shares)
    blocks = refs[:count]
    weight, q_gain, k_gain = refs[count : count + 3]
    q_out, kv_out, block_in, weight_in, gain_in, q_held, kv_held, arrive, leave = refs[-9:]
    first = place[0]
    second = place[1]
    first_step = place[2]
    second_step = place[3]
    half = 2 * PIECE

    copies = [
        pltpu.make_async_copy(weight, weight_in, arrive.at[count]),
        pltpu.make_async_copy(q_gain, gain_in.at[0], arrive.at[count + 1]),
        pltpu.make_async_copy(k_gain, gain_in.at[1], arrive.at[count + 2]),
    ]
    for at in range(count):
        copies.append(pltpu.make_async_copy(blocks[at], block_in.at[at], arrive.at[at]))
    for copy in copies:
        copy.start()
    for copy in copies[:3]:
        copy.wait()

    def normalize(values, gain):
        mean_square = jnp.mean(values * values, axis=-1, keepdims=True)
        return (values * lax.rsqrt(mean_square + 1e-06) * gain).astype(jnp.bfloat16)

    whole = jnp.concatenate([weight_in[at] for at in range(3)], axis=1)
    for copy in copies[3:]:
        copy.wait()
    rows = block_in[...].reshape(count * half, block_in.shape[2])
    proj = jnp.dot(rows, whole, preferred_element_type=jnp.float32)
    q_held[...] = normalize(proj[:, :HEAD], gain_in[0])
    kv_held[:, :HEAD] = normalize(proj[:, HEAD : 2 * HEAD], gain_in[1])
    kv_held[:, HEAD:] = proj[:, 2 * HEAD :].astype(jnp.bfloat16)
    for at, (shift, pieces) in enumerate(shares):
        for order, piece in enumerate(pieces):
            spot = ((first + piece) % 4) * first_step + ((second + shift) % 4) * second_step
            target = pl.ds(pl.multiple_of(spot * PIECE, PIECE), PIECE)
            source = pl.ds(at * half + order * PIECE, PIECE)
            pltpu.make_async_copy(q_held.at[source, :], q_out.at[target, :], leave.at[0]).start()
            pltpu.make_async_copy(kv_held.at[source, :], kv_out.at[target, :], leave.at[1]).start()
    pltpu.make_async_copy(q_held, q_held, leave.at[0]).wait()
    pltpu.make_async_copy(kv_held, kv_held, leave.at[1]).wait()


def project(shares, blocks, weight, q_gain, k_gain, place, begun=()):
    rows = 16 * PIECE
    count = len(blocks)
    done_rows = count * 2 * PIECE
    width = blocks[0].shape[1]
    anywhere = pl.BlockSpec(memory_space=pl.ANY)
    return pl.pallas_call(
        functools.partial(project_kernel, shares),
        out_shape=(
            jax.ShapeDtypeStruct((rows, HEAD), jnp.bfloat16),
            jax.ShapeDtypeStruct((rows, 2 * HEAD), jnp.bfloat16),
        ),
        in_specs=[SMEM] + [anywhere] * (count + 3 + len(begun)),
        out_specs=(anywhere, anywhere),
        scratch_shapes=[
            pltpu.VMEM((count, 2 * PIECE, width), jnp.bfloat16),
            pltpu.VMEM((3, width, HEAD), jnp.bfloat16),
            pltpu.VMEM((2, 1, HEAD), jnp.float32),
            pltpu.VMEM((done_rows, HEAD), jnp.bfloat16),
            pltpu.VMEM((done_rows, 2 * HEAD), jnp.bfloat16),
            pltpu.SemaphoreType.DMA((count + 3,)),
            pltpu.SemaphoreType.DMA((2,)),
        ],
        input_output_aliases={count + 4: 0, count + 5: 1} if begun else {},
        compiler_params=pltpu.CompilerParams(vmem_limit_bytes=16 * 1024 * 1024),
        name="project",
    )(place, *blocks, weight, q_gain, k_gain, *begun)


def attend_kernel(scale, place, lists, counts, mine, other, *refs):
    pieces = refs[:BLOCKS]
    out_mine, out_other, kv, ready = refs[BLOCKS:]
    ones = jnp.ones((GROUP * TILE, HEAD), jnp.bfloat16)
    slots = mine.shape[0]
    loads = [
        pltpu.make_async_copy(pieces[at], kv.at[pl.ds(at * slots, slots)], ready.at[at])
        for at in range(BLOCKS)
    ]
    for load in loads:
        load.start()
    for load in loads:
        load.wait()

    def attend_tiles(q, out, base):
        def one_slot(slot, _):
            query = q[slot]
            count = counts[0, base + slot]

            def turn(step, acc):
                picks = [lists[base + slot, step * GROUP + at] for at in range(GROUP)]
                keys = jnp.concatenate([kv[pick, :, :HEAD] for pick in picks], axis=0)
                values = jnp.concatenate([kv[pick, :, HEAD:] for pick in picks], axis=0)
                scores = lax.dot_general(
                    query, keys, (((1,), (1,)), ((), ())), preferred_element_type=jnp.float32
                )
                live = (count - step * GROUP) * TILE
                column = lax.broadcasted_iota(jnp.int32, scores.shape, 1)
                weights = jnp.where(column < live, jnp.exp2(scores * scale), 0.0)
                return acc + jnp.dot(
                    weights.astype(jnp.bfloat16),
                    jnp.concatenate((values, ones), axis=1),
                    preferred_element_type=jnp.float32,
                )

            turns = (count + GROUP - 1) // GROUP
            out[slot] = lax.fori_loop(0, turns, turn, jnp.zeros((TILE, 2 * HEAD), jnp.float32))
            return 0

        lax.fori_loop(0, slots, one_slot, 0)

    attend_tiles(other, out_other, (1 - place[4]) * slots)
    attend_tiles(mine, out_mine, place[4] * slots)


def attend(place, mine, other, pieces, lists, counts):
    scale = HEAD ** (-0.5) * LOG2E
    slots = mine.shape[0]
    sums = jax.ShapeDtypeStruct((slots, TILE, 2 * HEAD), jnp.float32)
    return pl.pallas_call(
        functools.partial(attend_kernel, scale),
        out_shape=(sums, sums),
        in_specs=[SMEM, SMEM, SMEM, VMEM, VMEM] + [pl.BlockSpec(memory_space=pl.ANY)] * BLOCKS,
        out_specs=(VMEM, VMEM),
        scratch_shapes=[
            pltpu.VMEM((BLOCKS * slots, TILE, 2 * HEAD), jnp.bfloat16),
            pltpu.SemaphoreType.DMA((BLOCKS,)),
        ],
        compiler_params=pltpu.CompilerParams(vmem_limit_bytes=24 * 1024 * 1024),
        name="attend",
    )(place, lists, counts, mine, other, *pieces)


def list_kernel(slots, place, tiles, counts, lists_out, counts_out):
    core = place[4]
    plane = place[5]
    half = PLANES // 2
    listed, rows = tiles.shape
    tile = tiles[...]
    bal = (tile * (65536 // slots + 1)) >> 16
    away = (((bal >> 1) - plane) * (2 * core - 1)) & (PLANES - 1)
    same = (bal & 1) == core
    entry = lax.broadcasted_iota(jnp.int32, (listed, rows), 0)
    least = jnp.where(same, 0, 1)
    most = jnp.where(same, half, half - 1)
    inside = (away >= least) & (away <= most) & (entry < counts[...])
    held = jnp.where(inside, 1.0, 0.0)
    pick = jnp.where(same, away, away + half) * slots + tile - bal * slots
    down = lax.broadcasted_iota(jnp.int32, (listed, listed), 0)
    along = lax.broadcasted_iota(jnp.int32, (listed, listed), 1)
    before = jnp.where(along < down, 1.0, 0.0)
    order = jnp.dot(before, held, preferred_element_type=jnp.float32)
    order = jnp.where(held > 0.0, order, -1.0).astype(jnp.int32)
    counts_out[...] = jnp.sum(held, axis=0, keepdims=True).astype(jnp.int32)
    for row in range(rows):
        hit = order[:, row : row + 1] == along
        placed = jnp.where(hit, pick[:, row : row + 1], 0)
        lists_out[row : row + 1, :] = jnp.sum(placed, axis=0, keepdims=True)


def local_lists(key_tiles, key_counts, place, slots):
    rows, listed = 2 * slots, key_tiles.shape[1]
    tiles = lax.dynamic_slice_in_dim(key_tiles.T, place[5] * rows, rows, 1)
    counts = lax.dynamic_slice_in_dim(key_counts, place[5] * rows, rows, 1)
    return pl.pallas_call(
        functools.partial(list_kernel, slots),
        out_shape=(
            jax.ShapeDtypeStruct((rows, listed), jnp.int32),
            jax.ShapeDtypeStruct((1, rows), jnp.int32),
        ),
        in_specs=[SMEM, VMEM, VMEM],
        out_specs=(VMEM, VMEM),
        compiler_params=pltpu.CompilerParams(vmem_limit_bytes=4 * 1024 * 1024),
        name="lists",
    )(place, tiles, counts)


def on_device(tokens, qkv_weight, q_gain, k_gain, key_tiles, key_counts):
    me_seq = lax.axis_index("seq")
    me_bal = lax.axis_index("bal")
    y, x = me_seq // 4, me_seq % 4
    core = me_bal % 2
    place = jnp.stack(
        (
            jnp.where(core == 0, x, y),
            jnp.where(core == 0, y, x),
            jnp.where(core == 0, 1, 4),
            jnp.where(core == 0, 4, 1),
            core,
            me_bal // 2,
        )
    ).astype(jnp.int32)
    slots = 16 * PIECE // TILE
    lists, counts = local_lists(key_tiles[0], key_counts, place, slots)

    before = send(tokens, 1, 1)
    after = send(tokens, 1, -1)
    across = send(tokens, 1, 2)
    low = jnp.concatenate((tokens, before), axis=0)
    before_low = send(low, 2, 1)
    high = jnp.concatenate((after, across), axis=0)
    after_high = send(high, 2, -1)
    after_low = send(low, 2, -1)
    before_high = send(high, 2, 1)
    across_low = send(before_low, 2, 1)
    across_high = send(after_high, 2, -1)

    weight = jnp.transpose(qkv_weight[:, 0], (1, 0, 2))
    low_pieces, high_pieces = (0, 3), (1, 2)
    begun = project(
        ((0, low_pieces), (0, high_pieces), (3, low_pieces), (1, high_pieces)),
        (low, high, before_low, after_high),
        weight,
        q_gain,
        k_gain,
        place,
    )
    begun = project(
        ((1, low_pieces), (3, high_pieces)),
        (after_low, before_high),
        weight,
        q_gain,
        k_gain,
        place,
        begun,
    )
    queries, pairs = project(
        ((2, low_pieces), (2, high_pieces)),
        (across_low, across_high),
        weight,
        q_gain,
        k_gain,
        place,
        begun,
    )
    same, other = [pairs, pass_on(pairs)], []
    moving = swap_cores(pairs)
    for step in range(1, PLANES // 2):
        moving = pass_on(moving)
        other.append(moving)
        same.append(pass_on(same[-1]))
        if step == 3:
            queries, moving = lax.optimization_barrier((queries, moving))
            other_queries = swap_cores(queries)

    def tiles(block):
        return block.reshape(slots, TILE, block.shape[1])

    pieces = [tiles(block) for block in same + other]
    kept, given = attend(place, tiles(queries), tiles(other_queries), pieces, lists, counts)
    sums = kept + swap_cores(given)
    result = (sums[:, :, :HEAD] / sums[:, :, HEAD:]).astype(jnp.bfloat16)
    return lax.all_to_all(
        result.reshape(slots * TILE, HEAD), "seq", split_axis=0, concat_axis=1, tiled=True
    )


def solution(mesh):
    placed = (
        P(("bal", "seq"), None),
        P(None, "seq", None, None),
        P("seq", None),
        P("seq", None),
        P("seq", None, None),
        P("seq", None),
    )
    return jax.shard_map(
        on_device, mesh=mesh, in_specs=placed, out_specs=P(("bal", "seq"), None), check_vma=False
    )
```

```python
import functools
import jax
import jax.numpy as jnp
from jax import lax
from jax.experimental import pallas as pl
from jax.experimental.pallas import tpu as pltpu
from jax.sharding import PartitionSpec as P

TILE = 128
HEAD = 128
PIECE = 48
PLANES = 16
UNROLL = 4
CALLS = ((0, 3),) + tuple((step, step + 1) for step in range(3, 9))
LOG2E = 1.4426950408889634
MESH_AXES = ("seq", "bal")
VMEM = pl.BlockSpec(memory_space=pltpu.VMEM)
SMEM = pl.BlockSpec(memory_space=pltpu.SMEM)


def plane_perm(phase, shift):
    pairs = []
    for bal in range(32):
        for y in range(4):
            for x in range(4):
                along_x = (bal % 2 == 0) == (phase == 1)
                to_y = y if along_x else (y + shift) % 4
                to_x = (x + shift) % 4 if along_x else x
                pairs.append(((4 * y + x) * 32 + bal, (4 * to_y + to_x) * 32 + bal))
    return pairs


def send(block, phase, shift):
    return lax.ppermute(block, MESH_AXES, plane_perm(phase, shift))


def swap_cores(block):
    return lax.ppermute(block, "bal", [(at, at ^ 1) for at in range(32)])


def pass_on(block, cores):
    pairs = []
    for z in range(PLANES):
        if 0 in cores:
            pairs.append((2 * z, 2 * ((z + 1) % PLANES)))
        if 1 in cores:
            pairs.append((2 * z + 1, 2 * ((z - 1) % PLANES) + 1))
    return lax.ppermute(block, "bal", pairs)


def project_kernel(shares, place, *refs):
    count = len(shares)
    blocks = refs[:count]
    weight, q_gain, k_gain = refs[count : count + 3]
    q_out, kv_out, rows_in, weight_in, gain_in, q_held, kv_held, arrive, leave = refs[-9:]
    first = place[0]
    second = place[1]
    first_step = place[2]
    second_step = place[3]

    copies = [
        pltpu.make_async_copy(weight, weight_in, arrive.at[count]),
        pltpu.make_async_copy(q_gain, gain_in.at[0], arrive.at[count + 1]),
        pltpu.make_async_copy(k_gain, gain_in.at[1], arrive.at[count + 2]),
    ]
    targets = []
    row = 0
    for at, (shift, pieces) in enumerate(shares):
        here = rows_in.at[pl.ds(row, len(pieces) * PIECE), :]
        copies.append(pltpu.make_async_copy(blocks[at], here, arrive.at[at]))
        for piece in pieces:
            spot = ((first + piece) % 4) * first_step + ((second + shift) % 4) * second_step
            target = pl.ds(pl.multiple_of(spot * PIECE, PIECE), PIECE)
            targets.append((pl.ds(row, PIECE), target))
            row += PIECE
    for copy in copies:
        copy.start()
    for copy in copies:
        copy.wait()

    def normalize(values, gain):
        mean_square = jnp.mean(values * values, axis=-1, keepdims=True)
        return (values * lax.rsqrt(mean_square + 1e-06) * gain).astype(jnp.bfloat16)

    whole = jnp.concatenate([weight_in[at] for at in range(3)], axis=1)
    proj = jnp.dot(rows_in[...], whole, preferred_element_type=jnp.float32)
    q_held[...] = normalize(proj[:, :HEAD], gain_in[0])
    kv_held[:, :HEAD] = normalize(proj[:, HEAD : 2 * HEAD], gain_in[1])
    kv_held[:, HEAD:] = proj[:, 2 * HEAD :].astype(jnp.bfloat16)
    for source, target in targets:
        pltpu.make_async_copy(q_held.at[source, :], q_out.at[target, :], leave.at[0]).start()
        pltpu.make_async_copy(kv_held.at[source, :], kv_out.at[target, :], leave.at[1]).start()
    pltpu.make_async_copy(q_held, q_held, leave.at[0]).wait()
    pltpu.make_async_copy(kv_held, kv_held, leave.at[1]).wait()


def project(shares, blocks, weight, q_gain, k_gain, place, begun=()):
    rows = 16 * PIECE
    count = len(blocks)
    rows_here = sum(len(pieces) for _, pieces in shares) * PIECE
    width = blocks[0].shape[1]
    anywhere = pl.BlockSpec(memory_space=pl.ANY)
    return pl.pallas_call(
        functools.partial(project_kernel, shares),
        out_shape=(
            jax.ShapeDtypeStruct((rows, HEAD), jnp.bfloat16),
            jax.ShapeDtypeStruct((rows, 2 * HEAD), jnp.bfloat16),
        ),
        in_specs=[SMEM] + [anywhere] * (count + 3 + len(begun)),
        out_specs=(anywhere, anywhere),
        scratch_shapes=[
            pltpu.VMEM((rows_here, width), jnp.bfloat16),
            pltpu.VMEM((3, width, HEAD), jnp.bfloat16),
            pltpu.VMEM((2, 1, HEAD), jnp.float32),
            pltpu.VMEM((rows_here, HEAD), jnp.bfloat16),
            pltpu.VMEM((rows_here, 2 * HEAD), jnp.bfloat16),
            pltpu.SemaphoreType.DMA((count + 3,)),
            pltpu.SemaphoreType.DMA((2,)),
        ],
        input_output_aliases={count + 4: 0, count + 5: 1} if begun else {},
        compiler_params=pltpu.CompilerParams(vmem_limit_bytes=16 * 1024 * 1024),
        name="project",
    )(place, *blocks, weight, q_gain, k_gain, *begun)


def attend_kernel(scale, first_call, last_call, call, blocks, place, pairs, counts, q, *refs):
    pieces = refs[:blocks]
    kv = refs[-1]
    slots = pieces[0].shape[0]
    rows = q.shape[0]
    if last_call:
        sums_in, kept, given, sums = refs[blocks : blocks + 4]
    elif first_call:
        sums = refs[blocks]
    else:
        sums_in, sums = refs[blocks : blocks + 2]
    for at in range(blocks):
        kv[at * slots : (at + 1) * slots] = pieces[at][...]
    if first_call:
        sums[...] = jnp.zeros_like(sums)
    else:
        sums[...] = sums_in[...]
    ones = jnp.ones((TILE, HEAD), jnp.bfloat16)

    def turn(step, _):
        for at in range(UNROLL):
            pair = pairs[call, step * UNROLL + at]
            row = pair >> 7
            tile = pair & 127
            scores = lax.dot_general(
                q[jnp.minimum(row, rows - 1)],
                kv[tile, :, :HEAD],
                (((1,), (1,)), ((), ())),
                preferred_element_type=jnp.float32,
            )
            weights = jnp.exp2(scores * scale).astype(jnp.bfloat16)
            values = jnp.concatenate((kv[tile, :, HEAD:], ones), axis=1)
            sums[row] += jnp.dot(weights, values, preferred_element_type=jnp.float32)
        return 0

    lax.fori_loop(0, (counts[0, call] + UNROLL - 1) // UNROLL, turn, 0)
    if last_call:
        core = place[4]
        for at in range(slots):
            kept[at] = sums[core * slots + at]
            given[at] = sums[(1 - core) * slots + at]


def attend(call, calls, place, pairs, counts, q, pieces, sums=None):
    scale = HEAD ** (-0.5) * LOG2E
    first_call, last_call = call == 0, call == calls - 1
    blocks, slots, rows = len(pieces), pieces[0].shape[0], q.shape[0]
    whole = jax.ShapeDtypeStruct((rows + 1, TILE, 2 * HEAD), jnp.float32)
    half = jax.ShapeDtypeStruct((slots, TILE, 2 * HEAD), jnp.float32)
    scratch = [pltpu.VMEM((blocks * slots, TILE, 2 * HEAD), jnp.bfloat16)]
    if last_call:
        scratch.insert(0, pltpu.VMEM(whole.shape, whole.dtype))
    more = () if first_call else (sums,)
    return pl.pallas_call(
        functools.partial(attend_kernel, scale, first_call, last_call, call, blocks),
        out_shape=(half, half) if last_call else whole,
        in_specs=[SMEM] * 3 + [VMEM] * (1 + blocks + len(more)),
        out_specs=(VMEM, VMEM) if last_call else VMEM,
        scratch_shapes=scratch,
        input_output_aliases={} if first_call or last_call else {4 + blocks: 0},
        compiler_params=pltpu.CompilerParams(vmem_limit_bytes=16 * 1024 * 1024),
        cost_estimate=pl.CostEstimate(
            flops=blocks * 10**9, bytes_accessed=blocks * 10**6, transcendentals=0
        ),
        name="attend",
    )(place, pairs, counts, q, *pieces, *more)


def list_kernel(slots, calls, place, tiles, counts, pairs_out, counts_out):
    core = place[4]
    plane = place[5]
    listed, rows = tiles.shape
    room = pairs_out.shape[1]
    tile = tiles[...]
    bal = (tile * (65536 // slots + 1)) >> 16
    away = (((bal >> 1) - plane) * (2 * core - 1)) & (PLANES - 1)
    same = (bal & 1) == core
    entry = lax.broadcasted_iota(jnp.int32, (listed, rows), 0)
    column = lax.broadcasted_iota(jnp.int32, (listed, rows), 1)
    least = jnp.where(same, 0, 1)
    most = PLANES // 2 - 1 + core
    inside = (away >= least) & (away <= most) & (entry < counts[...])
    down = lax.broadcasted_iota(jnp.int32, (listed, listed), 0)
    along = lax.broadcasted_iota(jnp.int32, (listed, listed), 1)
    before = jnp.where(along < down, 1.0, 0.0)
    down = lax.broadcasted_iota(jnp.int32, (rows, rows), 0)
    along = lax.broadcasted_iota(jnp.int32, (rows, rows), 1)
    ahead = jnp.where(down < along, 1.0, 0.0)
    spot = lax.broadcasted_iota(jnp.int32, (listed, room), 1)
    nothing = rows * TILE
    totals = []
    for call, (start, stop) in enumerate(calls):
        here = inside & (away >= start) & (away < stop)
        held = jnp.where(here, 1.0, 0.0)
        total = jnp.sum(held, axis=0, keepdims=True)
        order = jnp.dot(before, held, preferred_element_type=jnp.float32)
        order = order + jnp.dot(
            jnp.broadcast_to(total, (8, rows)), ahead, preferred_element_type=jnp.float32
        )[:1]
        order = jnp.where(held > 0.0, order, -1.0).astype(jnp.int32)
        skip = stop - start - max(start, 1)
        block = jnp.where(same, away - start, away + skip)
        pair = column * TILE + block * slots + tile - bal * slots - nothing
        placed = jnp.zeros((1, room), jnp.int32)
        for row in range(rows):
            hit = order[:, row : row + 1] == spot
            placed += jnp.sum(jnp.where(hit, pair[:, row : row + 1], 0), axis=0, keepdims=True)
        pairs_out[call : call + 1, :] = placed + nothing
        totals.append(jnp.sum(total, axis=1, keepdims=True).astype(jnp.int32))
    counts_out[...] = jnp.concatenate(totals, axis=1)


def list_pairs(calls, key_tiles, key_counts, place, slots):
    rows = 2 * slots
    tiles = lax.dynamic_slice_in_dim(key_tiles.T, place[5] * rows, rows, 1)
    counts = lax.dynamic_slice_in_dim(key_counts, place[5] * rows, rows, 1)
    most = max(2 * stop - start - max(start, 1) for start, stop in calls) * slots
    room = -(-rows * most // TILE) * TILE
    return pl.pallas_call(
        functools.partial(list_kernel, slots, calls),
        out_shape=(
            jax.ShapeDtypeStruct((len(calls), room), jnp.int32),
            jax.ShapeDtypeStruct((1, len(calls)), jnp.int32),
        ),
        in_specs=[SMEM, VMEM, VMEM],
        out_specs=(VMEM, VMEM),
        compiler_params=pltpu.CompilerParams(vmem_limit_bytes=4 * 1024 * 1024),
        name="lists",
    )(place, tiles, counts)


def on_device(tokens, qkv_weight, q_gain, k_gain, key_tiles, key_counts):
    me_seq = lax.axis_index("seq")
    me_bal = lax.axis_index("bal")
    y, x = me_seq // 4, me_seq % 4
    core = me_bal % 2
    place = jnp.stack(
        (
            jnp.where(core == 0, x, y),
            jnp.where(core == 0, y, x),
            jnp.where(core == 0, 1, 4),
            jnp.where(core == 0, 4, 1),
            core,
            me_bal // 2,
        )
    ).astype(jnp.int32)
    slots = 16 * PIECE // TILE
    pairs, counts = list_pairs(CALLS, key_tiles[0], key_counts, place, slots)

    before = send(tokens, 1, 1)
    after = send(tokens, 1, -1)
    across = send(tokens, 1, 2)
    low = jnp.concatenate((tokens, before), axis=0)
    before_low = send(low, 2, 1)
    high = jnp.concatenate((after, across), axis=0)
    after_high = send(high, 2, -1)
    after_low = send(low, 2, -1)
    before_high = send(high, 2, 1)
    across_low = send(before_low, 2, 1)
    across_high = send(after_high, 2, -1)

    weight = jnp.transpose(qkv_weight[:, 0], (1, 0, 2))
    low_pieces, high_pieces = (0, 3), (1, 2)
    begun = project(
        ((0, (0,)), (0, (3,)), (0, (1,)), (0, (2,)), (3, low_pieces), (1, high_pieces)),
        (tokens, before, after, across, before_low, after_high),
        weight,
        q_gain,
        k_gain,
        place,
    )
    begun = project(
        ((1, low_pieces), (3, high_pieces)),
        (after_low, before_high),
        weight,
        q_gain,
        k_gain,
        place,
        begun,
    )
    queries, keys_values = project(
        ((2, low_pieces), (2, high_pieces)),
        (across_low, across_high),
        weight,
        q_gain,
        k_gain,
        place,
        begun,
    )
    def tiles(block):
        return block.reshape(-1, TILE, block.shape[1])

    same, other, sums = [keys_values], [swap_cores(keys_values)], None
    for step in range(1, PLANES // 2 + 1):
        cores = (0, 1) if step < PLANES // 2 else (1,)
        same.append(pass_on(same[-1], cores))
        other.append(pass_on(other[-1], cores))
        if sums is not None:
            same[-1], sums = lax.optimization_barrier((same[-1], sums))
        if step == 1:
            queries, other[1] = lax.optimization_barrier((queries, other[1]))
            other_queries = swap_cores(queries)
        if step == 2:
            low_queries = jnp.where(core == 0, queries, other_queries)
            high_queries = jnp.where(core == 0, other_queries, queries)
            chip_queries = tiles(jnp.concatenate((low_queries, high_queries), axis=0))
            other[2], chip_queries = lax.optimization_barrier((other[2], chip_queries))
        call = step - CALLS[0][1] + 1
        if call >= 0:
            start, stop = CALLS[call]
            blocks = [tiles(block) for block in same[start:stop] + other[max(start, 1) : stop]]
            sums = attend(call, len(CALLS), place, pairs, counts, chip_queries, blocks, sums)
    kept, given = sums
    sums = kept + swap_cores(given)
    result = (sums[:, :, :HEAD] / sums[:, :, HEAD:]).astype(jnp.bfloat16)
    return lax.all_to_all(
        result.reshape(slots * TILE, HEAD), "seq", split_axis=0, concat_axis=1, tiled=True
    )


def solution(mesh):
    placed = (
        P(("bal", "seq"), None),
        P(None, "seq", None, None),
        P("seq", None),
        P("seq", None),
        P("seq", None, None),
        P("seq", None),
    )
    return jax.shard_map(
        on_device, mesh=mesh, in_specs=placed, out_specs=P(("bal", "seq"), None), check_vma=False
    )
```

```python
import functools
import jax
import jax.numpy as jnp
from jax import lax
from jax.experimental import pallas as pl
from jax.experimental.pallas import tpu as pltpu
from jax.sharding import PartitionSpec as P

TILE = 128
HEAD = 128
PIECE = 48
PLANES = 16
UNROLL = 8
CALLS = ((0, 3),) + tuple((step, step + 1) for step in range(3, 9))
LOG2E = 1.4426950408889634
MESH_AXES = ("seq", "bal")
VMEM = pl.BlockSpec(memory_space=pltpu.VMEM)
SMEM = pl.BlockSpec(memory_space=pltpu.SMEM)


def plane_perm(phase, shift):
    pairs = []
    for bal in range(32):
        for y in range(4):
            for x in range(4):
                along_x = (bal % 2 == 0) == (phase == 1)
                to_y = y if along_x else (y + shift) % 4
                to_x = (x + shift) % 4 if along_x else x
                pairs.append(((4 * y + x) * 32 + bal, (4 * to_y + to_x) * 32 + bal))
    return pairs


def send(block, phase, shift):
    return lax.ppermute(block, MESH_AXES, plane_perm(phase, shift))


def swap_cores(block):
    return lax.ppermute(block, "bal", [(at, at ^ 1) for at in range(32)])


def pass_on(block, cores):
    pairs = []
    for z in range(PLANES):
        if 0 in cores:
            pairs.append((2 * z, 2 * ((z + 1) % PLANES)))
        if 1 in cores:
            pairs.append((2 * z + 1, 2 * ((z - 1) % PLANES) + 1))
    return lax.ppermute(block, "bal", pairs)


def project_kernel(shares, place, *refs):
    count = len(shares)
    blocks = refs[:count]
    weight, q_gain, k_gain = refs[count : count + 3]
    q_out, kv_out, q_held, kv_held, leave = refs[-5:]
    first = place[0]
    second = place[1]
    first_step = place[2]
    second_step = place[3]

    def normalize(values, gain):
        mean_square = jnp.mean(values * values, axis=-1, keepdims=True)
        return (values * lax.rsqrt(mean_square + 1e-06) * gain).astype(jnp.bfloat16)

    rows = jnp.concatenate([block[...] for block in blocks], axis=0)
    whole = jnp.concatenate([weight[at] for at in range(3)], axis=1)
    proj = jnp.dot(rows, whole, preferred_element_type=jnp.float32)
    q_held[...] = normalize(proj[:, :HEAD], q_gain[...])
    kv_held[:, :HEAD] = normalize(proj[:, HEAD : 2 * HEAD], k_gain[...])
    kv_held[:, HEAD:] = proj[:, 2 * HEAD :].astype(jnp.bfloat16)
    row = 0
    for shift, pieces in shares:
        for piece in pieces:
            spot = ((first + piece) % 4) * first_step + ((second + shift) % 4) * second_step
            target = pl.ds(pl.multiple_of(spot * PIECE, PIECE), PIECE)
            source = pl.ds(row, PIECE)
            pltpu.make_async_copy(q_held.at[source, :], q_out.at[target, :], leave.at[0]).start()
            pltpu.make_async_copy(kv_held.at[source, :], kv_out.at[target, :], leave.at[1]).start()
            row += PIECE
    pltpu.make_async_copy(q_held, q_held, leave.at[0]).wait()
    pltpu.make_async_copy(kv_held, kv_held, leave.at[1]).wait()


def project(shares, blocks, weight, q_gain, k_gain, place, begun=()):
    rows = 16 * PIECE
    count = len(blocks)
    rows_here = sum(len(pieces) for _, pieces in shares) * PIECE
    anywhere = pl.BlockSpec(memory_space=pl.ANY)
    return pl.pallas_call(
        functools.partial(project_kernel, shares),
        out_shape=(
            jax.ShapeDtypeStruct((rows, HEAD), jnp.bfloat16),
            jax.ShapeDtypeStruct((rows, 2 * HEAD), jnp.bfloat16),
        ),
        in_specs=[SMEM] + [VMEM] * (count + 3) + [anywhere] * len(begun),
        out_specs=(anywhere, anywhere),
        scratch_shapes=[
            pltpu.VMEM((rows_here, HEAD), jnp.bfloat16),
            pltpu.VMEM((rows_here, 2 * HEAD), jnp.bfloat16),
            pltpu.SemaphoreType.DMA((2,)),
        ],
        input_output_aliases={count + 4: 0, count + 5: 1} if begun else {},
        compiler_params=pltpu.CompilerParams(vmem_limit_bytes=20 * 1024 * 1024),
        name="project",
    )(place, *blocks, weight, q_gain, k_gain, *begun)


def attend_kernel(scale, first_call, last_call, call, blocks, place, pairs, counts, q, *refs):
    pieces = refs[:blocks]
    kv = refs[-1]
    slots = pieces[0].shape[0]
    rows = q.shape[0]
    if last_call:
        sums_in, kept, given, sums = refs[blocks : blocks + 4]
    elif first_call:
        sums = refs[blocks]
    else:
        sums_in, sums = refs[blocks : blocks + 2]
    for at in range(blocks):
        kv[at * slots : (at + 1) * slots] = pieces[at][...]
    if first_call:
        sums[...] = jnp.zeros_like(sums)
    else:
        sums[...] = sums_in[...]
    ones = jnp.ones((TILE, HEAD), jnp.bfloat16)

    def turn(step, _):
        rows_here, scores, products = [], [], []
        for at in range(UNROLL):
            pair = pairs[call, step * UNROLL + at]
            rows_here.append((pair >> 7, pair & 127))
        for row, tile in rows_here:
            scores.append(
                lax.dot_general(
                    q[jnp.minimum(row, rows - 1)],
                    kv[tile, :, :HEAD],
                    (((1,), (1,)), ((), ())),
                    preferred_element_type=jnp.float32,
                )
            )
        for (row, tile), score in zip(rows_here, scores):
            weights = jnp.exp2(score * scale).astype(jnp.bfloat16)
            values = jnp.concatenate((kv[tile, :, HEAD:], ones), axis=1)
            products.append(jnp.dot(weights, values, preferred_element_type=jnp.float32))
        for (row, _), product in zip(rows_here, products):
            sums[row] += product
        return 0

    lax.fori_loop(0, (counts[0, call] + UNROLL - 1) // UNROLL, turn, 0)
    if last_call:
        core = place[4]
        for at in range(slots):
            kept[at] = sums[core * slots + at]
            given[at] = sums[(1 - core) * slots + at]


def attend(call, calls, place, pairs, counts, q, pieces, sums=None):
    scale = HEAD ** (-0.5) * LOG2E
    first_call, last_call = call == 0, call == calls - 1
    blocks, slots, rows = len(pieces), pieces[0].shape[0], q.shape[0]
    whole = jax.ShapeDtypeStruct((rows + 1, TILE, 2 * HEAD), jnp.float32)
    half = jax.ShapeDtypeStruct((slots, TILE, 2 * HEAD), jnp.float32)
    scratch = [pltpu.VMEM((blocks * slots, TILE, 2 * HEAD), jnp.bfloat16)]
    if last_call:
        scratch.insert(0, pltpu.VMEM(whole.shape, whole.dtype))
    more = () if first_call else (sums,)
    return pl.pallas_call(
        functools.partial(attend_kernel, scale, first_call, last_call, call, blocks),
        out_shape=(half, half) if last_call else whole,
        in_specs=[SMEM] * 3 + [VMEM] * (1 + blocks + len(more)),
        out_specs=(VMEM, VMEM) if last_call else VMEM,
        scratch_shapes=scratch,
        input_output_aliases={} if first_call or last_call else {4 + blocks: 0},
        compiler_params=pltpu.CompilerParams(vmem_limit_bytes=16 * 1024 * 1024),
        cost_estimate=pl.CostEstimate(
            flops=blocks * 10**9, bytes_accessed=blocks * 10**6, transcendentals=0
        ),
        name="attend",
    )(place, pairs, counts, q, *pieces, *more)


def call_room(start, stop, slots):
    pairs = 2 * slots * (2 * stop - start - max(start, 1)) * slots
    return -(-pairs // TILE) * TILE


def list_kernel(slots, calls, place, tiles, counts, pairs_out, counts_out):
    core = place[4]
    plane = place[5]
    listed, rows = tiles.shape
    tile = tiles[...]
    bal = (tile * (65536 // slots + 1)) >> 16
    away = (((bal >> 1) - plane) * (2 * core - 1)) & (PLANES - 1)
    same = (bal & 1) == core
    entry = lax.broadcasted_iota(jnp.int32, (listed, rows), 0)
    column = lax.broadcasted_iota(jnp.int32, (listed, rows), 1)
    least = jnp.where(same, 0, 1)
    most = PLANES // 2 - 1 + core
    inside = (away >= least) & (away <= most) & (entry < counts[...])
    down = lax.broadcasted_iota(jnp.int32, (listed, listed), 0)
    along = lax.broadcasted_iota(jnp.int32, (listed, listed), 1)
    before = jnp.where(along < down, 1.0, 0.0)
    down = lax.broadcasted_iota(jnp.int32, (rows, rows), 0)
    along = lax.broadcasted_iota(jnp.int32, (rows, rows), 1)
    ahead = jnp.where(down < along, 1.0, 0.0)
    nothing = rows * TILE
    totals = []
    for call, (start, stop) in enumerate(calls):
        here = inside & (away >= start) & (away < stop)
        held = jnp.where(here, 1.0, 0.0)
        total = jnp.sum(held, axis=0, keepdims=True)
        order = jnp.dot(before, held, preferred_element_type=jnp.float32)
        order = order + jnp.dot(
            jnp.broadcast_to(total, (8, rows)), ahead, preferred_element_type=jnp.float32
        )[:1]
        order = jnp.where(held > 0.0, order, -1.0).astype(jnp.int32)
        skip = stop - start - max(start, 1)
        block = jnp.where(same, away - start, away + skip)
        pair = column * TILE + block * slots + tile - bal * slots - nothing
        room = call_room(start, stop, slots)
        spot = lax.broadcasted_iota(jnp.int32, (listed, room), 1)
        placed = jnp.zeros((1, room), jnp.int32)
        for row in range(rows):
            hit = order[:, row : row + 1] == spot
            placed += jnp.sum(jnp.where(hit, pair[:, row : row + 1], 0), axis=0, keepdims=True)
        pairs_out[call : call + 1, :room] = placed + nothing
        totals.append(jnp.sum(total, axis=1, keepdims=True).astype(jnp.int32))
    counts_out[...] = jnp.concatenate(totals, axis=1)


def list_pairs(calls, key_tiles, key_counts, place, slots):
    rows = 2 * slots
    tiles = lax.dynamic_slice_in_dim(key_tiles.T, place[5] * rows, rows, 1)
    counts = lax.dynamic_slice_in_dim(key_counts, place[5] * rows, rows, 1)
    room = max(call_room(start, stop, slots) for start, stop in calls)
    return pl.pallas_call(
        functools.partial(list_kernel, slots, calls),
        out_shape=(
            jax.ShapeDtypeStruct((len(calls), room), jnp.int32),
            jax.ShapeDtypeStruct((1, len(calls)), jnp.int32),
        ),
        in_specs=[SMEM, VMEM, VMEM],
        out_specs=(VMEM, VMEM),
        compiler_params=pltpu.CompilerParams(vmem_limit_bytes=4 * 1024 * 1024),
        name="lists",
    )(place, tiles, counts)


def on_device(tokens, qkv_weight, q_gain, k_gain, key_tiles, key_counts):
    me_seq = lax.axis_index("seq")
    me_bal = lax.axis_index("bal")
    y, x = me_seq // 4, me_seq % 4
    core = me_bal % 2
    place = jnp.stack(
        (
            jnp.where(core == 0, x, y),
            jnp.where(core == 0, y, x),
            jnp.where(core == 0, 1, 4),
            jnp.where(core == 0, 4, 1),
            core,
            me_bal // 2,
        )
    ).astype(jnp.int32)
    slots = 16 * PIECE // TILE
    pairs, counts = list_pairs(CALLS, key_tiles[0], key_counts, place, slots)

    before = send(tokens, 1, 1)
    after = send(tokens, 1, -1)
    across = send(tokens, 1, 2)
    low = jnp.concatenate((tokens, before), axis=0)
    before_low = send(low, 2, 1)
    high = jnp.concatenate((after, across), axis=0)
    after_high = send(high, 2, -1)
    after_low = send(low, 2, -1)
    before_high = send(high, 2, 1)
    across_low = send(before_low, 2, 1)
    across_high = send(after_high, 2, -1)

    weight = jnp.transpose(qkv_weight[:, 0], (1, 0, 2))
    low_pieces, high_pieces = (0, 3), (1, 2)
    begun = project(
        ((0, (0,)), (0, (3,)), (0, (1,)), (0, (2,)), (3, low_pieces), (1, high_pieces)),
        (tokens, before, after, across, before_low, after_high),
        weight,
        q_gain,
        k_gain,
        place,
    )
    begun = project(
        ((1, low_pieces), (3, high_pieces)),
        (after_low, before_high),
        weight,
        q_gain,
        k_gain,
        place,
        begun,
    )
    begun, (pairs, counts) = lax.optimization_barrier((begun, (pairs, counts)))
    queries, keys_values = project(
        ((2, low_pieces), (2, high_pieces)),
        (across_low, across_high),
        weight,
        q_gain,
        k_gain,
        place,
        begun,
    )
    def tiles(block):
        return block.reshape(-1, TILE, block.shape[1])

    same, other, sums = [keys_values], [swap_cores(keys_values)], None
    for step in range(1, PLANES // 2 + 1):
        cores = (0, 1) if step < PLANES // 2 else (1,)
        same.append(pass_on(same[-1], cores))
        other.append(pass_on(other[-1], cores))
        if sums is not None:
            same[-1], sums = lax.optimization_barrier((same[-1], sums))
        if step == 1:
            queries, other[1] = lax.optimization_barrier((queries, other[1]))
            other_queries = swap_cores(queries)
        if step == 2:
            low_queries = jnp.where(core == 0, queries, other_queries)
            high_queries = jnp.where(core == 0, other_queries, queries)
            chip_queries = tiles(jnp.concatenate((low_queries, high_queries), axis=0))
            other[2], chip_queries = lax.optimization_barrier((other[2], chip_queries))
        call = step - CALLS[0][1] + 1
        if call >= 0:
            start, stop = CALLS[call]
            blocks = [tiles(block) for block in same[start:stop] + other[max(start, 1) : stop]]
            sums = attend(call, len(CALLS), place, pairs, counts, chip_queries, blocks, sums)
    kept, given = sums
    sums = kept + swap_cores(given)
    result = (sums[:, :, :HEAD] / sums[:, :, HEAD:]).astype(jnp.bfloat16)
    return lax.all_to_all(
        result.reshape(slots * TILE, HEAD), "seq", split_axis=0, concat_axis=1, tiled=True
    )


def solution(mesh):
    placed = (
        P(("bal", "seq"), None),
        P(None, "seq", None, None),
        P("seq", None),
        P("seq", None),
        P("seq", None, None),
        P("seq", None),
    )
    return jax.shard_map(
        on_device, mesh=mesh, in_specs=placed, out_specs=P(("bal", "seq"), None), check_vma=False
    )
```

```python
import functools
import jax
import jax.numpy as jnp
from jax import lax
from jax.experimental import pallas as pl
from jax.experimental.pallas import tpu as pltpu
from jax.sharding import PartitionSpec as P

TILE = 128
HEAD = 128
PIECE = 48
PLANES = 16
UNROLL = 8
CALLS = ((0, 3),) + tuple((step, step + 1) for step in range(3, 9))
LOG2E = 1.4426950408889634
MESH_AXES = ("seq", "bal")
VMEM = pl.BlockSpec(memory_space=pltpu.VMEM)
SMEM = pl.BlockSpec(memory_space=pltpu.SMEM)


def plane_perm(phase, shift):
    pairs = []
    for bal in range(32):
        for y in range(4):
            for x in range(4):
                along_x = (bal % 2 == 0) == (phase == 1)
                to_y = y if along_x else (y + shift) % 4
                to_x = (x + shift) % 4 if along_x else x
                pairs.append(((4 * y + x) * 32 + bal, (4 * to_y + to_x) * 32 + bal))
    return pairs


def send(block, phase, shift):
    return lax.ppermute(block, MESH_AXES, plane_perm(phase, shift))


def join_kernel(upper, lower, out, done):
    rows = upper.shape[0]
    copies = [
        pltpu.make_async_copy(upper, out.at[pl.ds(0, rows), :], done.at[0]),
        pltpu.make_async_copy(lower, out.at[pl.ds(rows, rows), :], done.at[1]),
    ]
    for copy in copies:
        copy.start()
    for copy in copies:
        copy.wait()


def join(upper, lower):
    rows, width = upper.shape
    anywhere = pl.BlockSpec(memory_space=pl.ANY)
    return pl.pallas_call(
        join_kernel,
        out_shape=jax.ShapeDtypeStruct((2 * rows, width), upper.dtype),
        in_specs=[anywhere, anywhere],
        out_specs=anywhere,
        scratch_shapes=[pltpu.SemaphoreType.DMA((2,))],
        compiler_params=pltpu.CompilerParams(vmem_limit_bytes=1024 * 1024),
        name="join",
    )(upper, lower)


def swap_cores(block):
    return lax.ppermute(block, "bal", [(at, at ^ 1) for at in range(32)])


def pass_on(block, cores):
    pairs = []
    for z in range(PLANES):
        if 0 in cores:
            pairs.append((2 * z, 2 * ((z + 1) % PLANES)))
        if 1 in cores:
            pairs.append((2 * z + 1, 2 * ((z - 1) % PLANES) + 1))
    return lax.ppermute(block, "bal", pairs)


def project_kernel(shares, place, *refs):
    count = len(shares)
    blocks = refs[:count]
    weight, gains = refs[count : count + 2]
    q_out, kv_out, q_held, kv_held, leave = refs[-5:]
    first = place[0]
    second = place[1]
    first_step = place[2]
    second_step = place[3]

    def normalize(values, gain):
        mean_square = jnp.mean(values * values, axis=-1, keepdims=True)
        return (values * lax.rsqrt(mean_square + 1e-06) * gain).astype(jnp.bfloat16)

    rows = jnp.concatenate([block[...] for block in blocks], axis=0)
    whole = jnp.concatenate([weight[at] for at in range(3)], axis=1)
    proj = jnp.dot(rows, whole, preferred_element_type=jnp.float32)
    q_held[...] = normalize(proj[:, :HEAD], gains[0:1, :])
    kv_held[:, :HEAD] = normalize(proj[:, HEAD : 2 * HEAD], gains[1:2, :])
    kv_held[:, HEAD:] = proj[:, 2 * HEAD :].astype(jnp.bfloat16)
    row = 0
    for shift, pieces in shares:
        for piece in pieces:
            spot = ((first + piece) % 4) * first_step + ((second + shift) % 4) * second_step
            target = pl.ds(pl.multiple_of(spot * PIECE, PIECE), PIECE)
            source = pl.ds(row, PIECE)
            pltpu.make_async_copy(q_held.at[source, :], q_out.at[target, :], leave.at[0]).start()
            pltpu.make_async_copy(kv_held.at[source, :], kv_out.at[target, :], leave.at[1]).start()
            row += PIECE
    pltpu.make_async_copy(q_held, q_held, leave.at[0]).wait()
    pltpu.make_async_copy(kv_held, kv_held, leave.at[1]).wait()


def project(shares, blocks, weight, gains, place, begun=()):
    rows = 16 * PIECE
    count = len(blocks)
    rows_here = sum(len(pieces) for _, pieces in shares) * PIECE
    anywhere = pl.BlockSpec(memory_space=pl.ANY)
    return pl.pallas_call(
        functools.partial(project_kernel, shares),
        out_shape=(
            jax.ShapeDtypeStruct((rows, HEAD), jnp.bfloat16),
            jax.ShapeDtypeStruct((rows, 2 * HEAD), jnp.bfloat16),
        ),
        in_specs=[SMEM] + [VMEM] * (count + 2) + [anywhere] * len(begun),
        out_specs=(anywhere, anywhere),
        scratch_shapes=[
            pltpu.VMEM((rows_here, HEAD), jnp.bfloat16),
            pltpu.VMEM((rows_here, 2 * HEAD), jnp.bfloat16),
            pltpu.SemaphoreType.DMA((2,)),
        ],
        input_output_aliases={count + 3: 0, count + 4: 1} if begun else {},
        compiler_params=pltpu.CompilerParams(vmem_limit_bytes=20 * 1024 * 1024),
        name="project",
    )(place, *blocks, weight, gains, *begun)


def attend_kernel(scale, first_call, last_call, call, blocks, place, pairs, counts, q, *refs):
    pieces = refs[:blocks]
    kv = refs[-1]
    slots = pieces[0].shape[0]
    rows = q.shape[0]
    if last_call:
        sums_in, kept, given, sums = refs[blocks : blocks + 4]
    elif first_call:
        sums = refs[blocks]
    else:
        sums_in, sums = refs[blocks : blocks + 2]
    for at in range(blocks):
        kv[at * slots : (at + 1) * slots] = pieces[at][...]
    if first_call:
        sums[...] = jnp.zeros_like(sums)
    else:
        sums[...] = sums_in[...]
    ones = jnp.ones((TILE, HEAD), jnp.bfloat16)

    def turn(step, _):
        rows_here, scores, products = [], [], []
        for at in range(UNROLL):
            pair = pairs[call, step * UNROLL + at]
            rows_here.append((pair >> 7, pair & 127))
        for row, tile in rows_here:
            scores.append(
                lax.dot_general(
                    q[jnp.minimum(row, rows - 1)],
                    kv[tile, :, :HEAD],
                    (((1,), (1,)), ((), ())),
                    preferred_element_type=jnp.float32,
                )
            )
        for (row, tile), score in zip(rows_here, scores):
            weights = jnp.exp2(score * scale).astype(jnp.bfloat16)
            values = jnp.concatenate((kv[tile, :, HEAD:], ones), axis=1)
            products.append(jnp.dot(weights, values, preferred_element_type=jnp.float32))
        for (row, _), product in zip(rows_here, products):
            sums[row] += product
        return 0

    lax.fori_loop(0, (counts[0, call] + UNROLL - 1) // UNROLL, turn, 0)
    if last_call:
        core = place[4]
        for at in range(slots):
            kept[at] = sums[core * slots + at]
            given[at] = sums[(1 - core) * slots + at]


def attend(call, calls, place, pairs, counts, q, pieces, sums=None):
    scale = HEAD ** (-0.5) * LOG2E
    first_call, last_call = call == 0, call == calls - 1
    blocks, slots, rows = len(pieces), pieces[0].shape[0], q.shape[0]
    whole = jax.ShapeDtypeStruct((rows + 1, TILE, 2 * HEAD), jnp.float32)
    half = jax.ShapeDtypeStruct((slots, TILE, 2 * HEAD), jnp.float32)
    scratch = [pltpu.VMEM((blocks * slots, TILE, 2 * HEAD), jnp.bfloat16)]
    if last_call:
        scratch.insert(0, pltpu.VMEM(whole.shape, whole.dtype))
    more = () if first_call else (sums,)
    return pl.pallas_call(
        functools.partial(attend_kernel, scale, first_call, last_call, call, blocks),
        out_shape=(half, half) if last_call else whole,
        in_specs=[SMEM] * 3 + [VMEM] * (1 + blocks + len(more)),
        out_specs=(VMEM, VMEM) if last_call else VMEM,
        scratch_shapes=scratch,
        input_output_aliases={} if first_call or last_call else {4 + blocks: 0},
        compiler_params=pltpu.CompilerParams(vmem_limit_bytes=16 * 1024 * 1024),
        cost_estimate=pl.CostEstimate(
            flops=blocks * 10**9, bytes_accessed=blocks * 10**6, transcendentals=0
        ),
        name="attend",
    )(place, pairs, counts, q, *pieces, *more)


def call_room(start, stop, slots):
    pairs = 2 * slots * (2 * stop - start - max(start, 1)) * slots
    return -(-pairs // TILE) * TILE


def list_kernel(slots, calls, place, tiles, counts, pairs_out, counts_out):
    core = place[4]
    plane = place[5]
    listed, rows = tiles.shape
    tile = tiles[...]
    bal = (tile * (65536 // slots + 1)) >> 16
    away = (((bal >> 1) - plane) * (2 * core - 1)) & (PLANES - 1)
    same = (bal & 1) == core
    entry = lax.broadcasted_iota(jnp.int32, (listed, rows), 0)
    column = lax.broadcasted_iota(jnp.int32, (listed, rows), 1)
    least = jnp.where(same, 0, 1)
    most = PLANES // 2 - 1 + core
    inside = (away >= least) & (away <= most) & (entry < counts[...])
    down = lax.broadcasted_iota(jnp.int32, (listed, listed), 0)
    along = lax.broadcasted_iota(jnp.int32, (listed, listed), 1)
    before = jnp.where(along < down, 1.0, 0.0)
    down = lax.broadcasted_iota(jnp.int32, (rows, rows), 0)
    along = lax.broadcasted_iota(jnp.int32, (rows, rows), 1)
    ahead = jnp.where(down < along, 1.0, 0.0)
    nothing = rows * TILE
    totals = []
    for call, (start, stop) in enumerate(calls):
        here = inside & (away >= start) & (away < stop)
        held = jnp.where(here, 1.0, 0.0)
        total = jnp.sum(held, axis=0, keepdims=True)
        order = jnp.dot(before, held, preferred_element_type=jnp.float32)
        order = order + jnp.dot(
            jnp.broadcast_to(total, (8, rows)), ahead, preferred_element_type=jnp.float32
        )[:1]
        order = jnp.where(held > 0.0, order, -1.0).astype(jnp.int32)
        skip = stop - start - max(start, 1)
        block = jnp.where(same, away - start, away + skip)
        pair = column * TILE + block * slots + tile - bal * slots - nothing
        room = call_room(start, stop, slots)
        spot = lax.broadcasted_iota(jnp.int32, (listed, room), 1)
        placed = jnp.zeros((1, room), jnp.int32)
        for row in range(rows):
            hit = order[:, row : row + 1] == spot
            placed += jnp.sum(jnp.where(hit, pair[:, row : row + 1], 0), axis=0, keepdims=True)
        pairs_out[call : call + 1, :room] = placed + nothing
        totals.append(jnp.sum(total, axis=1, keepdims=True).astype(jnp.int32))
    counts_out[...] = jnp.concatenate(totals, axis=1)


def list_pairs(calls, key_tiles, key_counts, place, slots):
    rows = 2 * slots
    tiles = lax.dynamic_slice_in_dim(key_tiles.T, place[5] * rows, rows, 1)
    counts = lax.dynamic_slice_in_dim(key_counts, place[5] * rows, rows, 1)
    room = max(call_room(start, stop, slots) for start, stop in calls)
    return pl.pallas_call(
        functools.partial(list_kernel, slots, calls),
        out_shape=(
            jax.ShapeDtypeStruct((len(calls), room), jnp.int32),
            jax.ShapeDtypeStruct((1, len(calls)), jnp.int32),
        ),
        in_specs=[SMEM, VMEM, VMEM],
        out_specs=(VMEM, VMEM),
        compiler_params=pltpu.CompilerParams(vmem_limit_bytes=4 * 1024 * 1024),
        name="lists",
    )(place, tiles, counts)


def on_device(tokens, qkv_weight, q_gain, k_gain, key_tiles, key_counts):
    me_seq = lax.axis_index("seq")
    me_bal = lax.axis_index("bal")
    y, x = me_seq // 4, me_seq % 4
    core = me_bal % 2
    place = jnp.stack(
        (
            jnp.where(core == 0, x, y),
            jnp.where(core == 0, y, x),
            jnp.where(core == 0, 1, 4),
            jnp.where(core == 0, 4, 1),
            core,
            me_bal // 2,
        )
    ).astype(jnp.int32)
    slots = 16 * PIECE // TILE
    before = send(tokens, 1, 1)
    after = send(tokens, 1, -1)
    across = send(tokens, 1, 2)
    low = join(tokens, before)
    before_low = send(low, 2, 1)
    high = join(after, across)
    after_high = send(high, 2, -1)
    after_low = send(low, 2, -1)
    before_high = send(high, 2, 1)
    across_low = send(before_low, 2, 1)
    across_high = send(after_high, 2, -1)

    gains = jnp.concatenate((q_gain, k_gain), axis=0)
    weight = jnp.transpose(qkv_weight[:, 0], (1, 0, 2))
    low_pieces, high_pieces = (0, 3), (1, 2)
    begun = project(
        ((0, low_pieces), (0, high_pieces), (3, low_pieces), (1, high_pieces)),
        (low, high, before_low, after_high),
        weight,
        gains,
        place,
    )
    begun = project(
        ((1, low_pieces), (3, high_pieces)),
        (after_low, before_high),
        weight,
        gains,
        place,
        begun,
    )
    queries, keys_values = project(
        ((2, low_pieces), (2, high_pieces)),
        (across_low, across_high),
        weight,
        gains,
        place,
        begun,
    )
    def tiles(block):
        return block.reshape(-1, TILE, block.shape[1])

    same, other, sums = [keys_values], [swap_cores(keys_values)], None
    for step in range(1, PLANES // 2 + 1):
        cores = (0, 1) if step < PLANES // 2 else (1,)
        same.append(pass_on(same[-1], cores))
        other.append(pass_on(other[-1], cores))
        if sums is not None:
            same[-1], sums = lax.optimization_barrier((same[-1], sums))
        if step == 1:
            key_tiles, other[0] = lax.optimization_barrier((key_tiles, other[0]))
            pairs, counts = list_pairs(CALLS, key_tiles[0], key_counts, place, slots)
            same[1], pairs, counts = lax.optimization_barrier((same[1], pairs, counts))
            queries, other[1] = lax.optimization_barrier((queries, other[1]))
            other_queries = swap_cores(queries)
        if step == 2:
            low_queries = jnp.where(core == 0, queries, other_queries)
            high_queries = jnp.where(core == 0, other_queries, queries)
            chip_queries = tiles(jnp.concatenate((low_queries, high_queries), axis=0))
            other[2], chip_queries = lax.optimization_barrier((other[2], chip_queries))
        call = step - CALLS[0][1] + 1
        if call >= 0:
            start, stop = CALLS[call]
            blocks = [tiles(block) for block in same[start:stop] + other[max(start, 1) : stop]]
            sums = attend(call, len(CALLS), place, pairs, counts, chip_queries, blocks, sums)
    kept, given = sums
    sums = kept + swap_cores(given)
    result = (sums[:, :, :HEAD] / sums[:, :, HEAD:]).astype(jnp.bfloat16)
    return lax.all_to_all(
        result.reshape(slots * TILE, HEAD), "seq", split_axis=0, concat_axis=1, tiled=True
    )


def solution(mesh):
    placed = (
        P(("bal", "seq"), None),
        P(None, "seq", None, None),
        P("seq", None),
        P("seq", None),
        P("seq", None, None),
        P("seq", None),
    )
    return jax.shard_map(
        on_device, mesh=mesh, in_specs=placed, out_specs=P(("bal", "seq"), None), check_vma=False
    )
```

```python
import functools
import jax
import jax.numpy as jnp
from jax import lax
from jax.experimental import pallas as pl
from jax.experimental.pallas import tpu as pltpu
from jax.sharding import PartitionSpec as P

TILE = 128
HEAD = 128
PIECE = 48
PLANES = 16
UNROLL = 8
CALLS = ((0, 3),) + tuple((step, step + 1) for step in range(3, 9))
LOG2E = 1.4426950408889634
MESH_AXES = ("seq", "bal")
VMEM = pl.BlockSpec(memory_space=pltpu.VMEM)
SMEM = pl.BlockSpec(memory_space=pltpu.SMEM)


def plane_perm(phase, shift):
    pairs = []
    for bal in range(32):
        for y in range(4):
            for x in range(4):
                along_x = (bal % 2 == 0) == (phase == 1)
                to_y = y if along_x else (y + shift) % 4
                to_x = (x + shift) % 4 if along_x else x
                pairs.append(((4 * y + x) * 32 + bal, (4 * to_y + to_x) * 32 + bal))
    return pairs


def send(block, phase, shift):
    return lax.ppermute(block, MESH_AXES, plane_perm(phase, shift))


def join_kernel(upper, lower, out, done):
    rows = upper.shape[0]
    copies = [
        pltpu.make_async_copy(upper, out.at[pl.ds(0, rows), :], done.at[0]),
        pltpu.make_async_copy(lower, out.at[pl.ds(rows, rows), :], done.at[1]),
    ]
    for copy in copies:
        copy.start()
    for copy in copies:
        copy.wait()


def join(upper, lower):
    rows, width = upper.shape
    anywhere = pl.BlockSpec(memory_space=pl.ANY)
    return pl.pallas_call(
        join_kernel,
        out_shape=jax.ShapeDtypeStruct((2 * rows, width), upper.dtype),
        in_specs=[anywhere, anywhere],
        out_specs=anywhere,
        scratch_shapes=[pltpu.SemaphoreType.DMA((2,))],
        compiler_params=pltpu.CompilerParams(vmem_limit_bytes=1024 * 1024),
        name="join",
    )(upper, lower)


def swap_cores(block):
    return lax.ppermute(block, "bal", [(at, at ^ 1) for at in range(32)])


def pass_on(block, cores):
    pairs = []
    for z in range(PLANES):
        if 0 in cores:
            pairs.append((2 * z, 2 * ((z + 1) % PLANES)))
        if 1 in cores:
            pairs.append((2 * z + 1, 2 * ((z - 1) % PLANES) + 1))
    return lax.ppermute(block, "bal", pairs)


def project_kernel(shares, place, *refs):
    count = len(shares)
    blocks = refs[:count]
    weight, gains = refs[count : count + 2]
    q_out, kv_out, q_held, kv_held, leave = refs[-5:]
    first = place[0]
    second = place[1]
    first_step = place[2]
    second_step = place[3]

    def normalize(values, gain):
        mean_square = jnp.mean(values * values, axis=-1, keepdims=True)
        return (values * lax.rsqrt(mean_square + 1e-06) * gain).astype(jnp.bfloat16)

    rows = jnp.concatenate([block[...] for block in blocks], axis=0)
    whole = jnp.concatenate([weight[at] for at in range(3)], axis=1)
    proj = jnp.dot(rows, whole, preferred_element_type=jnp.float32)
    q_held[...] = normalize(proj[:, :HEAD], gains[0:1, :])
    kv_held[:, :HEAD] = normalize(proj[:, HEAD : 2 * HEAD], gains[1:2, :])
    kv_held[:, HEAD:] = proj[:, 2 * HEAD :].astype(jnp.bfloat16)
    row = 0
    for shift, pieces in shares:
        for piece in pieces:
            spot = ((first + piece) % 4) * first_step + ((second + shift) % 4) * second_step
            target = pl.ds(pl.multiple_of(spot * PIECE, PIECE), PIECE)
            source = pl.ds(row, PIECE)
            pltpu.make_async_copy(q_held.at[source, :], q_out.at[target, :], leave.at[0]).start()
            pltpu.make_async_copy(kv_held.at[source, :], kv_out.at[target, :], leave.at[1]).start()
            row += PIECE
    pltpu.make_async_copy(q_held, q_held, leave.at[0]).wait()
    pltpu.make_async_copy(kv_held, kv_held, leave.at[1]).wait()


def project(shares, blocks, weight, gains, place, begun=()):
    rows = 16 * PIECE
    count = len(blocks)
    rows_here = sum(len(pieces) for _, pieces in shares) * PIECE
    anywhere = pl.BlockSpec(memory_space=pl.ANY)
    return pl.pallas_call(
        functools.partial(project_kernel, shares),
        out_shape=(
            jax.ShapeDtypeStruct((rows, HEAD), jnp.bfloat16),
            jax.ShapeDtypeStruct((rows, 2 * HEAD), jnp.bfloat16),
        ),
        in_specs=[SMEM] + [VMEM] * (count + 2) + [anywhere] * len(begun),
        out_specs=(anywhere, anywhere),
        scratch_shapes=[
            pltpu.VMEM((rows_here, HEAD), jnp.bfloat16),
            pltpu.VMEM((rows_here, 2 * HEAD), jnp.bfloat16),
            pltpu.SemaphoreType.DMA((2,)),
        ],
        input_output_aliases={count + 3: 0, count + 4: 1} if begun else {},
        compiler_params=pltpu.CompilerParams(vmem_limit_bytes=20 * 1024 * 1024),
        name="project",
    )(place, *blocks, weight, gains, *begun)


def attend_kernel(scale, first_call, last_call, call, blocks, place, pairs, counts, q, *refs):
    pieces = refs[:blocks]
    kv = refs[-1]
    slots = pieces[0].shape[0]
    rows = q.shape[0]
    if last_call:
        sums_in, kept, given, sums = refs[blocks : blocks + 4]
    elif first_call:
        sums = refs[blocks]
    else:
        sums_in, sums = refs[blocks : blocks + 2]
    for at in range(blocks):
        kv[at * slots : (at + 1) * slots] = pieces[at][...]
    if first_call:
        sums[...] = jnp.zeros_like(sums)
    else:
        sums[...] = sums_in[...]
    ones = jnp.ones((TILE, HEAD), jnp.bfloat16)

    def turn(step, _):
        rows_here, scores, products = [], [], []
        for at in range(UNROLL):
            pair = pairs[call, step * UNROLL + at]
            rows_here.append((pair >> 7, pair & 127))
        for row, tile in rows_here:
            scores.append(
                lax.dot_general(
                    q[jnp.minimum(row, rows - 1)],
                    kv[tile, :, :HEAD],
                    (((1,), (1,)), ((), ())),
                    preferred_element_type=jnp.float32,
                )
            )
        for (row, tile), score in zip(rows_here, scores):
            weights = jnp.exp2(score * scale).astype(jnp.bfloat16)
            values = jnp.concatenate((kv[tile, :, HEAD:], ones), axis=1)
            products.append(jnp.dot(weights, values, preferred_element_type=jnp.float32))
        for (row, _), product in zip(rows_here, products):
            sums[row] += product
        return 0

    lax.fori_loop(0, (counts[0, call] + UNROLL - 1) // UNROLL, turn, 0)
    if last_call:
        core = place[4]
        for at in range(slots):
            kept[at] = sums[core * slots + at]
            given[at] = sums[(1 - core) * slots + at]


def attend(call, calls, place, pairs, counts, q, pieces, sums=None):
    scale = HEAD ** (-0.5) * LOG2E
    first_call, last_call = call == 0, call == calls - 1
    blocks, slots, rows = len(pieces), pieces[0].shape[0], q.shape[0]
    whole = jax.ShapeDtypeStruct((rows + 1, TILE, 2 * HEAD), jnp.float32)
    half = jax.ShapeDtypeStruct((slots, TILE, 2 * HEAD), jnp.float32)
    scratch = [pltpu.VMEM((blocks * slots, TILE, 2 * HEAD), jnp.bfloat16)]
    if last_call:
        scratch.insert(0, pltpu.VMEM(whole.shape, whole.dtype))
    more = () if first_call else (sums,)
    return pl.pallas_call(
        functools.partial(attend_kernel, scale, first_call, last_call, call, blocks),
        out_shape=(half, half) if last_call else whole,
        in_specs=[SMEM] * 3 + [VMEM] * (1 + blocks + len(more)),
        out_specs=(VMEM, VMEM) if last_call else VMEM,
        scratch_shapes=scratch,
        input_output_aliases={} if first_call or last_call else {4 + blocks: 0},
        compiler_params=pltpu.CompilerParams(vmem_limit_bytes=16 * 1024 * 1024),
        cost_estimate=pl.CostEstimate(
            flops=blocks * 10**9, bytes_accessed=blocks * 10**6, transcendentals=0
        ),
        name="attend",
    )(place, pairs, counts, q, *pieces, *more)


def call_room(start, stop, slots):
    pairs = 2 * slots * (2 * stop - start - max(start, 1)) * slots
    return -(-pairs // TILE) * TILE


def list_kernel(slots, calls, place, tiles, counts, pairs_out, counts_out):
    core = place[4]
    plane = place[5]
    listed, rows = tiles.shape
    tile = tiles[...]
    bal = (tile * (65536 // slots + 1)) >> 16
    away = (((bal >> 1) - plane) * (2 * core - 1)) & (PLANES - 1)
    same = (bal & 1) == core
    entry = lax.broadcasted_iota(jnp.int32, (listed, rows), 0)
    column = lax.broadcasted_iota(jnp.int32, (listed, rows), 1)
    least = jnp.where(same, 0, 1)
    most = PLANES // 2 - 1 + core
    inside = (away >= least) & (away <= most) & (entry < counts[...])
    down = lax.broadcasted_iota(jnp.int32, (listed, listed), 0)
    along = lax.broadcasted_iota(jnp.int32, (listed, listed), 1)
    before = jnp.where(along < down, 1.0, 0.0)
    down = lax.broadcasted_iota(jnp.int32, (rows, rows), 0)
    along = lax.broadcasted_iota(jnp.int32, (rows, rows), 1)
    ahead = jnp.where(down < along, 1.0, 0.0)
    nothing = rows * TILE
    totals = []
    for call, (start, stop) in enumerate(calls):
        here = inside & (away >= start) & (away < stop)
        held = jnp.where(here, 1.0, 0.0)
        total = jnp.sum(held, axis=0, keepdims=True)
        order = jnp.dot(before, held, preferred_element_type=jnp.float32)
        order = order + jnp.dot(
            jnp.broadcast_to(total, (8, rows)), ahead, preferred_element_type=jnp.float32
        )[:1]
        order = jnp.where(held > 0.0, order, -1.0).astype(jnp.int32)
        skip = stop - start - max(start, 1)
        block = jnp.where(same, away - start, away + skip)
        pair = column * TILE + block * slots + tile - bal * slots - nothing
        room = call_room(start, stop, slots)
        spot = lax.broadcasted_iota(jnp.int32, (listed, room), 1)
        placed = jnp.zeros((1, room), jnp.int32)
        for row in range(rows):
            hit = order[:, row : row + 1] == spot
            placed += jnp.sum(jnp.where(hit, pair[:, row : row + 1], 0), axis=0, keepdims=True)
        pairs_out[call : call + 1, :room] = placed + nothing
        totals.append(jnp.sum(total, axis=1, keepdims=True).astype(jnp.int32))
    counts_out[...] = jnp.concatenate(totals, axis=1)


def list_pairs(calls, key_tiles, key_counts, place, slots):
    rows = 2 * slots
    tiles = lax.dynamic_slice_in_dim(key_tiles.T, place[5] * rows, rows, 1)
    counts = lax.dynamic_slice_in_dim(key_counts, place[5] * rows, rows, 1)
    room = max(call_room(start, stop, slots) for start, stop in calls)
    return pl.pallas_call(
        functools.partial(list_kernel, slots, calls),
        out_shape=(
            jax.ShapeDtypeStruct((len(calls), room), jnp.int32),
            jax.ShapeDtypeStruct((1, len(calls)), jnp.int32),
        ),
        in_specs=[SMEM, VMEM, VMEM],
        out_specs=(VMEM, VMEM),
        compiler_params=pltpu.CompilerParams(vmem_limit_bytes=4 * 1024 * 1024),
        name="lists",
    )(place, tiles, counts)


def on_device(tokens, qkv_weight, q_gain, k_gain, key_tiles, key_counts):
    me_seq = lax.axis_index("seq")
    me_bal = lax.axis_index("bal")
    y, x = me_seq // 4, me_seq % 4
    core = me_bal % 2
    place = jnp.stack(
        (
            jnp.where(core == 0, x, y),
            jnp.where(core == 0, y, x),
            jnp.where(core == 0, 1, 4),
            jnp.where(core == 0, 4, 1),
            core,
            me_bal // 2,
        )
    ).astype(jnp.int32)
    slots = 16 * PIECE // TILE
    before = send(tokens, 1, 1)
    after = send(tokens, 1, -1)
    low = join(tokens, before)
    low, late = lax.optimization_barrier((low, tokens))
    across = send(late, 1, 2)
    before_low = send(low, 2, 1)
    after_low = send(low, 2, -1)
    before_low, after_low = lax.optimization_barrier((before_low, after_low))
    high = join(after, across)
    after_high = send(high, 2, -1)
    before_high = send(high, 2, 1)
    across_low = send(before_low, 2, 1)
    across_high = send(after_high, 2, -1)

    gains = jnp.concatenate((q_gain, k_gain), axis=0)
    weight = jnp.transpose(qkv_weight[:, 0], (1, 0, 2))
    low_pieces, high_pieces = (0, 3), (1, 2)
    begun = project(
        ((0, low_pieces), (0, high_pieces), (3, low_pieces), (1, high_pieces)),
        (low, high, before_low, after_high),
        weight,
        gains,
        place,
    )
    begun = project(
        ((1, low_pieces), (3, high_pieces)),
        (after_low, before_high),
        weight,
        gains,
        place,
        begun,
    )
    queries, keys_values = project(
        ((2, low_pieces), (2, high_pieces)),
        (across_low, across_high),
        weight,
        gains,
        place,
        begun,
    )
    def tiles(block):
        return block.reshape(-1, TILE, block.shape[1])

    same, other, sums = [keys_values], [swap_cores(keys_values)], None
    for step in range(1, PLANES // 2 + 1):
        cores = (0, 1) if step < PLANES // 2 else (1,)
        same.append(pass_on(same[-1], cores))
        other.append(pass_on(other[-1], cores))
        if sums is not None:
            same[-1], sums = lax.optimization_barrier((same[-1], sums))
        if step == 1:
            key_tiles, other[0] = lax.optimization_barrier((key_tiles, other[0]))
            pairs, counts = list_pairs(CALLS, key_tiles[0], key_counts, place, slots)
            same[1], pairs, counts = lax.optimization_barrier((same[1], pairs, counts))
            queries, other[0] = lax.optimization_barrier((queries, other[0]))
            other_queries = swap_cores(queries)
            same[1], other_queries = lax.optimization_barrier((same[1], other_queries))
        if step == 2:
            low_queries = jnp.where(core == 0, queries, other_queries)
            high_queries = jnp.where(core == 0, other_queries, queries)
            chip_queries = tiles(jnp.concatenate((low_queries, high_queries), axis=0))
            other[2], chip_queries = lax.optimization_barrier((other[2], chip_queries))
        call = step - CALLS[0][1] + 1
        if call >= 0:
            start, stop = CALLS[call]
            blocks = [tiles(block) for block in same[start:stop] + other[max(start, 1) : stop]]
            sums = attend(call, len(CALLS), place, pairs, counts, chip_queries, blocks, sums)
    kept, given = sums
    sums = kept + swap_cores(given)
    result = (sums[:, :, :HEAD] / sums[:, :, HEAD:]).astype(jnp.bfloat16)
    return lax.all_to_all(
        result.reshape(slots * TILE, HEAD), "seq", split_axis=0, concat_axis=1, tiled=True
    )


def solution(mesh):
    placed = (
        P(("bal", "seq"), None),
        P(None, "seq", None, None),
        P("seq", None),
        P("seq", None),
        P("seq", None, None),
        P("seq", None),
    )
    return jax.shard_map(
        on_device, mesh=mesh, in_specs=placed, out_specs=P(("bal", "seq"), None), check_vma=False
    )
```

```python
import functools
import jax
import jax.numpy as jnp
from jax import lax
from jax.experimental import pallas as pl
from jax.experimental.pallas import tpu as pltpu
from jax.sharding import PartitionSpec as P

TILE = 128
HEAD = 128
PIECE = 48
PLANES = 16
UNROLL = 8
CALLS = ((0, 3),) + tuple((step, step + 1) for step in range(3, 9))
LOG2E = 1.4426950408889634
MESH_AXES = ("seq", "bal")
VMEM = pl.BlockSpec(memory_space=pltpu.VMEM)
SMEM = pl.BlockSpec(memory_space=pltpu.SMEM)


def plane_perm(phase, shift):
    pairs = []
    for bal in range(32):
        for y in range(4):
            for x in range(4):
                along_x = (bal % 2 == 0) == (phase == 1)
                to_y = y if along_x else (y + shift) % 4
                to_x = (x + shift) % 4 if along_x else x
                pairs.append(((4 * y + x) * 32 + bal, (4 * to_y + to_x) * 32 + bal))
    return pairs


def send(block, phase, shift):
    return lax.ppermute(block, MESH_AXES, plane_perm(phase, shift))


def join_kernel(upper, lower, out, done):
    rows = upper.shape[0]
    copies = [
        pltpu.make_async_copy(upper, out.at[pl.ds(0, rows), :], done.at[0]),
        pltpu.make_async_copy(lower, out.at[pl.ds(rows, rows), :], done.at[1]),
    ]
    for copy in copies:
        copy.start()
    for copy in copies:
        copy.wait()


def join(upper, lower):
    rows, width = upper.shape
    anywhere = pl.BlockSpec(memory_space=pl.ANY)
    return pl.pallas_call(
        join_kernel,
        out_shape=jax.ShapeDtypeStruct((2 * rows, width), upper.dtype),
        in_specs=[anywhere, anywhere],
        out_specs=anywhere,
        scratch_shapes=[pltpu.SemaphoreType.DMA((2,))],
        compiler_params=pltpu.CompilerParams(vmem_limit_bytes=1024 * 1024),
        name="join",
    )(upper, lower)


def swap_cores(block):
    return lax.ppermute(block, "bal", [(at, at ^ 1) for at in range(32)])


def pass_on(block, cores):
    pairs = []
    for z in range(PLANES):
        if 0 in cores:
            pairs.append((2 * z, 2 * ((z + 1) % PLANES)))
        if 1 in cores:
            pairs.append((2 * z + 1, 2 * ((z - 1) % PLANES) + 1))
    return lax.ppermute(block, "bal", pairs)


def project_kernel(shares, place, *refs):
    count = len(shares)
    blocks = refs[:count]
    weight, gains = refs[count : count + 2]
    q_out, kv_out, q_held, kv_held, leave = refs[-5:]
    first = place[0]
    second = place[1]
    first_step = place[2]
    second_step = place[3]

    def normalize(values, gain):
        mean_square = jnp.mean(values * values, axis=-1, keepdims=True)
        return (values * lax.rsqrt(mean_square + 1e-06) * gain).astype(jnp.bfloat16)

    rows = jnp.concatenate([block[...] for block in blocks], axis=0)
    whole = jnp.concatenate([weight[at] for at in range(3)], axis=1)
    proj = jnp.dot(rows, whole, preferred_element_type=jnp.float32)
    q_held[...] = normalize(proj[:, :HEAD], gains[0:1, :])
    kv_held[:, :HEAD] = normalize(proj[:, HEAD : 2 * HEAD], gains[1:2, :])
    kv_held[:, HEAD:] = proj[:, 2 * HEAD :].astype(jnp.bfloat16)
    row = 0
    for shift, pieces in shares:
        for piece in pieces:
            spot = ((first + piece) % 4) * first_step + ((second + shift) % 4) * second_step
            target = pl.ds(pl.multiple_of(spot * PIECE, PIECE), PIECE)
            source = pl.ds(row, PIECE)
            pltpu.make_async_copy(q_held.at[source, :], q_out.at[target, :], leave.at[0]).start()
            pltpu.make_async_copy(kv_held.at[source, :], kv_out.at[target, :], leave.at[1]).start()
            row += PIECE
    pltpu.make_async_copy(q_held, q_held, leave.at[0]).wait()
    pltpu.make_async_copy(kv_held, kv_held, leave.at[1]).wait()


def project(shares, blocks, weight, gains, place, begun=()):
    rows = 16 * PIECE
    count = len(blocks)
    rows_here = sum(len(pieces) for _, pieces in shares) * PIECE
    anywhere = pl.BlockSpec(memory_space=pl.ANY)
    return pl.pallas_call(
        functools.partial(project_kernel, shares),
        out_shape=(
            jax.ShapeDtypeStruct((rows, HEAD), jnp.bfloat16),
            jax.ShapeDtypeStruct((rows, 2 * HEAD), jnp.bfloat16),
        ),
        in_specs=[SMEM] + [VMEM] * (count + 2) + [anywhere] * len(begun),
        out_specs=(anywhere, anywhere),
        scratch_shapes=[
            pltpu.VMEM((rows_here, HEAD), jnp.bfloat16),
            pltpu.VMEM((rows_here, 2 * HEAD), jnp.bfloat16),
            pltpu.SemaphoreType.DMA((2,)),
        ],
        input_output_aliases={count + 3: 0, count + 4: 1} if begun else {},
        compiler_params=pltpu.CompilerParams(vmem_limit_bytes=20 * 1024 * 1024),
        name="project",
    )(place, *blocks, weight, gains, *begun)


def attend_kernel(scale, first_call, last_call, call, blocks, place, pairs, counts, q, *refs):
    pieces = refs[:blocks]
    kv = refs[-1]
    slots = pieces[0].shape[0]
    rows = q.shape[0]
    if last_call:
        sums_in, kept, given, sums = refs[blocks : blocks + 4]
    elif first_call:
        sums = refs[blocks]
    else:
        sums_in, sums = refs[blocks : blocks + 2]
    for at in range(blocks):
        kv[at * slots : (at + 1) * slots] = pieces[at][...]
    if first_call:
        sums[...] = jnp.zeros_like(sums)
    else:
        sums[...] = sums_in[...]
    ones = jnp.ones((TILE, HEAD), jnp.bfloat16)

    def turn(step, _):
        rows_here, scores, products = [], [], []
        for at in range(UNROLL):
            pair = pairs[call, step * UNROLL + at]
            rows_here.append((pair >> 7, pair & 127))
        for row, tile in rows_here:
            scores.append(
                lax.dot_general(
                    q[jnp.minimum(row, rows - 1)],
                    kv[tile, :, :HEAD],
                    (((1,), (1,)), ((), ())),
                    preferred_element_type=jnp.float32,
                )
            )
        for (row, tile), score in zip(rows_here, scores):
            weights = jnp.exp2(score * scale).astype(jnp.bfloat16)
            values = jnp.concatenate((kv[tile, :, HEAD:], ones), axis=1)
            products.append(jnp.dot(weights, values, preferred_element_type=jnp.float32))
        for (row, _), product in zip(rows_here, products):
            sums[row] += product
        return 0

    lax.fori_loop(0, (counts[0, call] + UNROLL - 1) // UNROLL, turn, 0)
    if last_call:
        core = place[4]
        for at in range(slots):
            kept[at] = sums[core * slots + at]
            given[at] = sums[(1 - core) * slots + at]


def attend(call, calls, place, pairs, counts, q, pieces, sums=None):
    scale = HEAD ** (-0.5) * LOG2E
    first_call, last_call = call == 0, call == calls - 1
    blocks, slots, rows = len(pieces), pieces[0].shape[0], q.shape[0]
    whole = jax.ShapeDtypeStruct((rows + 1, TILE, 2 * HEAD), jnp.float32)
    half = jax.ShapeDtypeStruct((slots, TILE, 2 * HEAD), jnp.float32)
    scratch = [pltpu.VMEM((blocks * slots, TILE, 2 * HEAD), jnp.bfloat16)]
    if last_call:
        scratch.insert(0, pltpu.VMEM(whole.shape, whole.dtype))
    more = () if first_call else (sums,)
    return pl.pallas_call(
        functools.partial(attend_kernel, scale, first_call, last_call, call, blocks),
        out_shape=(half, half) if last_call else whole,
        in_specs=[SMEM] * 3 + [VMEM] * (1 + blocks + len(more)),
        out_specs=(VMEM, VMEM) if last_call else VMEM,
        scratch_shapes=scratch,
        input_output_aliases={} if first_call or last_call else {4 + blocks: 0},
        compiler_params=pltpu.CompilerParams(vmem_limit_bytes=16 * 1024 * 1024),
        cost_estimate=pl.CostEstimate(
            flops=blocks * 10**9, bytes_accessed=blocks * 10**6, transcendentals=0
        ),
        name="attend",
    )(place, pairs, counts, q, *pieces, *more)


def call_room(start, stop, slots):
    pairs = 2 * slots * (2 * stop - start - max(start, 1)) * slots
    return -(-pairs // TILE) * TILE


def list_kernel(slots, calls, place, tiles, counts, pairs_out, counts_out):
    core = place[4]
    plane = place[5]
    listed, rows = tiles.shape
    tile = tiles[...]
    bal = (tile * (65536 // slots + 1)) >> 16
    away = (((bal >> 1) - plane) * (2 * core - 1)) & (PLANES - 1)
    same = (bal & 1) == core
    entry = lax.broadcasted_iota(jnp.int32, (listed, rows), 0)
    column = lax.broadcasted_iota(jnp.int32, (listed, rows), 1)
    least = jnp.where(same, 0, 1)
    most = PLANES // 2 - 1 + core
    inside = (away >= least) & (away <= most) & (entry < counts[...])
    down = lax.broadcasted_iota(jnp.int32, (listed, listed), 0)
    along = lax.broadcasted_iota(jnp.int32, (listed, listed), 1)
    before = jnp.where(along < down, 1.0, 0.0)
    down = lax.broadcasted_iota(jnp.int32, (rows, rows), 0)
    along = lax.broadcasted_iota(jnp.int32, (rows, rows), 1)
    ahead = jnp.where(down < along, 1.0, 0.0)
    nothing = rows * TILE
    totals = []
    for call, (start, stop) in enumerate(calls):
        here = inside & (away >= start) & (away < stop)
        held = jnp.where(here, 1.0, 0.0)
        total = jnp.sum(held, axis=0, keepdims=True)
        order = jnp.dot(before, held, preferred_element_type=jnp.float32)
        order = order + jnp.dot(
            jnp.broadcast_to(total, (8, rows)), ahead, preferred_element_type=jnp.float32
        )[:1]
        order = jnp.where(held > 0.0, order, -1.0).astype(jnp.int32)
        skip = stop - start - max(start, 1)
        block = jnp.where(same, away - start, away + skip)
        pair = column * TILE + block * slots + tile - bal * slots - nothing
        room = call_room(start, stop, slots)
        spot = lax.broadcasted_iota(jnp.int32, (listed, room), 1)
        placed = jnp.zeros((1, room), jnp.int32)
        for row in range(rows):
            hit = order[:, row : row + 1] == spot
            placed += jnp.sum(jnp.where(hit, pair[:, row : row + 1], 0), axis=0, keepdims=True)
        pairs_out[call : call + 1, :room] = placed + nothing
        totals.append(jnp.sum(total, axis=1, keepdims=True).astype(jnp.int32))
    counts_out[...] = jnp.concatenate(totals, axis=1)


def list_pairs(calls, key_tiles, key_counts, place, slots):
    rows = 2 * slots
    tiles = lax.dynamic_slice_in_dim(key_tiles.T, place[5] * rows, rows, 1)
    counts = lax.dynamic_slice_in_dim(key_counts, place[5] * rows, rows, 1)
    room = max(call_room(start, stop, slots) for start, stop in calls)
    return pl.pallas_call(
        functools.partial(list_kernel, slots, calls),
        out_shape=(
            jax.ShapeDtypeStruct((len(calls), room), jnp.int32),
            jax.ShapeDtypeStruct((1, len(calls)), jnp.int32),
        ),
        in_specs=[SMEM, VMEM, VMEM],
        out_specs=(VMEM, VMEM),
        compiler_params=pltpu.CompilerParams(vmem_limit_bytes=4 * 1024 * 1024),
        name="lists",
    )(place, tiles, counts)


def on_device(tokens, qkv_weight, q_gain, k_gain, key_tiles, key_counts):
    me_seq = lax.axis_index("seq")
    me_bal = lax.axis_index("bal")
    y, x = me_seq // 4, me_seq % 4
    core = me_bal % 2
    place = jnp.stack(
        (
            jnp.where(core == 0, x, y),
            jnp.where(core == 0, y, x),
            jnp.where(core == 0, 1, 4),
            jnp.where(core == 0, 4, 1),
            core,
            me_bal // 2,
        )
    ).astype(jnp.int32)
    slots = 16 * PIECE // TILE
    before = send(tokens, 1, 1)
    across = send(tokens, 1, 2)
    after = send(tokens, 1, -1)
    low = join(tokens, before)
    gains = jnp.concatenate((q_gain, k_gain), axis=0)
    weight = jnp.transpose(qkv_weight[:, 0], (1, 0, 2))
    low, gains, across, after = lax.optimization_barrier((low, gains, across, after))
    high = join(across, after)
    after_high = send(high, 2, -1)
    before_low = send(low, 2, 1)
    before_high = send(high, 2, 1)
    after_low = send(low, 2, -1)
    across_low = send(before_low, 2, 1)
    across_high = send(after_high, 2, -1)

    low_pieces, high_pieces = (0, 3), (2, 1)
    begun = project(
        ((0, low_pieces), (0, high_pieces), (3, low_pieces), (1, high_pieces)),
        (low, high, before_low, after_high),
        weight,
        gains,
        place,
    )
    begun = project(
        ((1, low_pieces), (3, high_pieces)),
        (after_low, before_high),
        weight,
        gains,
        place,
        begun,
    )
    queries, keys_values = project(
        ((2, low_pieces), (2, high_pieces)),
        (across_low, across_high),
        weight,
        gains,
        place,
        begun,
    )
    def tiles(block):
        return block.reshape(-1, TILE, block.shape[1])

    same, other, sums = [keys_values], [swap_cores(keys_values)], None
    for step in range(1, PLANES // 2 + 1):
        cores = (0, 1) if step < PLANES // 2 else (1,)
        same.append(pass_on(same[-1], cores))
        other.append(pass_on(other[-1], cores))
        if sums is not None:
            same[-1], sums = lax.optimization_barrier((same[-1], sums))
        if step == 1:
            key_tiles, other[0] = lax.optimization_barrier((key_tiles, other[0]))
            pairs, counts = list_pairs(CALLS, key_tiles[0], key_counts, place, slots)
            same[1], pairs, counts = lax.optimization_barrier((same[1], pairs, counts))
            queries, other[0] = lax.optimization_barrier((queries, other[0]))
            other_queries = swap_cores(queries)
            same[1], other_queries = lax.optimization_barrier((same[1], other_queries))
        if step == 2:
            low_queries = jnp.where(core == 0, queries, other_queries)
            high_queries = jnp.where(core == 0, other_queries, queries)
            chip_queries = tiles(jnp.concatenate((low_queries, high_queries), axis=0))
            other[2], chip_queries = lax.optimization_barrier((other[2], chip_queries))
        call = step - CALLS[0][1] + 1
        if call >= 0:
            start, stop = CALLS[call]
            blocks = [tiles(block) for block in same[start:stop] + other[max(start, 1) : stop]]
            sums = attend(call, len(CALLS), place, pairs, counts, chip_queries, blocks, sums)
    kept, given = sums
    sums = kept + swap_cores(given)
    result = (sums[:, :, :HEAD] / sums[:, :, HEAD:]).astype(jnp.bfloat16)
    return lax.all_to_all(
        result.reshape(slots * TILE, HEAD), "seq", split_axis=0, concat_axis=1, tiled=True
    )


def solution(mesh):
    placed = (
        P(("bal", "seq"), None),
        P(None, "seq", None, None),
        P("seq", None),
        P("seq", None),
        P("seq", None, None),
        P("seq", None),
    )
    return jax.shard_map(
        on_device, mesh=mesh, in_specs=placed, out_specs=P(("bal", "seq"), None), check_vma=False
    )
```

```python
import functools
import jax
import jax.numpy as jnp
from jax import lax
from jax.experimental import pallas as pl
from jax.experimental.pallas import tpu as pltpu
from jax.sharding import PartitionSpec as P

TILE = 128
HEAD = 128
PIECE = 48
PLANES = 16
UNROLL = 8
CALLS = ((0, 3),) + tuple((step, step + 1) for step in range(3, 9))
LOG2E = 1.4426950408889634
MESH_AXES = ("seq", "bal")
VMEM = pl.BlockSpec(memory_space=pltpu.VMEM)
SMEM = pl.BlockSpec(memory_space=pltpu.SMEM)


def plane_perm(phase, shift):
    pairs = []
    for bal in range(32):
        for y in range(4):
            for x in range(4):
                along_x = (bal % 2 == 0) == (phase == 1)
                to_y = y if along_x else (y + shift) % 4
                to_x = (x + shift) % 4 if along_x else x
                pairs.append(((4 * y + x) * 32 + bal, (4 * to_y + to_x) * 32 + bal))
    return pairs


def send(block, phase, shift):
    return lax.ppermute(block, MESH_AXES, plane_perm(phase, shift))


def join_kernel(starts, *refs):
    parts = refs[: len(starts)]
    out, done = refs[-2:]
    copies = []
    for at, start in enumerate(starts):
        here = out.at[pl.ds(start, parts[at].shape[0]), :]
        copies.append(pltpu.make_async_copy(parts[at], here, done.at[at]))
    for copy in copies:
        copy.start()
    for copy in copies:
        copy.wait()


def join(rows, starts, parts, begun=()):
    anywhere = pl.BlockSpec(memory_space=pl.ANY)
    return pl.pallas_call(
        functools.partial(join_kernel, starts),
        out_shape=jax.ShapeDtypeStruct((rows, parts[0].shape[1]), parts[0].dtype),
        in_specs=[anywhere] * (len(parts) + len(begun)),
        out_specs=anywhere,
        scratch_shapes=[pltpu.SemaphoreType.DMA((len(parts),))],
        input_output_aliases={len(parts): 0} if begun else {},
        compiler_params=pltpu.CompilerParams(vmem_limit_bytes=1024 * 1024),
        name="join",
    )(*parts, *begun)


def swap_cores(block):
    return lax.ppermute(block, "bal", [(at, at ^ 1) for at in range(32)])


def pass_on(block, cores):
    pairs = []
    for z in range(PLANES):
        if 0 in cores:
            pairs.append((2 * z, 2 * ((z + 1) % PLANES)))
        if 1 in cores:
            pairs.append((2 * z + 1, 2 * ((z - 1) % PLANES) + 1))
    return lax.ppermute(block, "bal", pairs)


def project_kernel(shares, place, *refs):
    count = len(shares)
    blocks = refs[:count]
    weight, gains = refs[count : count + 2]
    q_out, kv_out, q_held, kv_held, leave = refs[-5:]
    first = place[0]
    second = place[1]
    first_step = place[2]
    second_step = place[3]

    def normalize(values, gain):
        mean_square = jnp.mean(values * values, axis=-1, keepdims=True)
        return (values * lax.rsqrt(mean_square + 1e-06) * gain).astype(jnp.bfloat16)

    rows = jnp.concatenate([block[...] for block in blocks], axis=0)
    whole = jnp.concatenate([weight[at] for at in range(3)], axis=1)
    proj = jnp.dot(rows, whole, preferred_element_type=jnp.float32)
    q_held[...] = normalize(proj[:, :HEAD], gains[0:1, :])
    kv_held[:, :HEAD] = normalize(proj[:, HEAD : 2 * HEAD], gains[1:2, :])
    kv_held[:, HEAD:] = proj[:, 2 * HEAD :].astype(jnp.bfloat16)
    row = 0
    for shift, pieces in shares:
        for piece in pieces:
            spot = ((first + piece) % 4) * first_step + ((second + shift) % 4) * second_step
            target = pl.ds(pl.multiple_of(spot * PIECE, PIECE), PIECE)
            source = pl.ds(row, PIECE)
            pltpu.make_async_copy(q_held.at[source, :], q_out.at[target, :], leave.at[0]).start()
            pltpu.make_async_copy(kv_held.at[source, :], kv_out.at[target, :], leave.at[1]).start()
            row += PIECE
    pltpu.make_async_copy(q_held, q_held, leave.at[0]).wait()
    pltpu.make_async_copy(kv_held, kv_held, leave.at[1]).wait()


def project(shares, blocks, weight, gains, place, begun=()):
    rows = 16 * PIECE
    count = len(blocks)
    rows_here = sum(len(pieces) for _, pieces in shares) * PIECE
    anywhere = pl.BlockSpec(memory_space=pl.ANY)
    return pl.pallas_call(
        functools.partial(project_kernel, shares),
        out_shape=(
            jax.ShapeDtypeStruct((rows, HEAD), jnp.bfloat16),
            jax.ShapeDtypeStruct((rows, 2 * HEAD), jnp.bfloat16),
        ),
        in_specs=[SMEM] + [VMEM] * (count + 2) + [anywhere] * len(begun),
        out_specs=(anywhere, anywhere),
        scratch_shapes=[
            pltpu.VMEM((rows_here, HEAD), jnp.bfloat16),
            pltpu.VMEM((rows_here, 2 * HEAD), jnp.bfloat16),
            pltpu.SemaphoreType.DMA((2,)),
        ],
        input_output_aliases={count + 3: 0, count + 4: 1} if begun else {},
        compiler_params=pltpu.CompilerParams(vmem_limit_bytes=20 * 1024 * 1024),
        name="project",
    )(place, *blocks, weight, gains, *begun)


def attend_kernel(scale, first_call, last_call, call, blocks, place, pairs, counts, q, *refs):
    pieces = refs[:blocks]
    kv = refs[-1]
    slots = pieces[0].shape[0]
    rows = q.shape[0]
    if last_call:
        sums_in, kept, given, sums = refs[blocks : blocks + 4]
    elif first_call:
        sums = refs[blocks]
    else:
        sums_in, sums = refs[blocks : blocks + 2]
    for at in range(blocks):
        kv[at * slots : (at + 1) * slots] = pieces[at][...]
    if first_call:
        sums[...] = jnp.zeros_like(sums)
    else:
        sums[...] = sums_in[...]
    ones = jnp.ones((TILE, HEAD), jnp.bfloat16)

    def turn(step, _):
        rows_here, scores, products = [], [], []
        for at in range(UNROLL):
            pair = pairs[call, step * UNROLL + at]
            rows_here.append((pair >> 7, pair & 127))
        for row, tile in rows_here:
            scores.append(
                lax.dot_general(
                    q[jnp.minimum(row, rows - 1)],
                    kv[tile, :, :HEAD],
                    (((1,), (1,)), ((), ())),
                    preferred_element_type=jnp.float32,
                )
            )
        for (row, tile), score in zip(rows_here, scores):
            weights = jnp.exp2(score * scale).astype(jnp.bfloat16)
            values = jnp.concatenate((kv[tile, :, HEAD:], ones), axis=1)
            products.append(jnp.dot(weights, values, preferred_element_type=jnp.float32))
        for (row, _), product in zip(rows_here, products):
            sums[row] += product
        return 0

    lax.fori_loop(0, (counts[0, call] + UNROLL - 1) // UNROLL, turn, 0)
    if last_call:
        core = place[4]
        for at in range(slots):
            kept[at] = sums[core * slots + at]
            given[at] = sums[(1 - core) * slots + at]


def attend(call, calls, place, pairs, counts, q, pieces, sums=None):
    scale = HEAD ** (-0.5) * LOG2E
    first_call, last_call = call == 0, call == calls - 1
    blocks, slots, rows = len(pieces), pieces[0].shape[0], q.shape[0]
    whole = jax.ShapeDtypeStruct((rows + 1, TILE, 2 * HEAD), jnp.float32)
    half = jax.ShapeDtypeStruct((slots, TILE, 2 * HEAD), jnp.float32)
    scratch = [pltpu.VMEM((blocks * slots, TILE, 2 * HEAD), jnp.bfloat16)]
    if last_call:
        scratch.insert(0, pltpu.VMEM(whole.shape, whole.dtype))
    more = () if first_call else (sums,)
    return pl.pallas_call(
        functools.partial(attend_kernel, scale, first_call, last_call, call, blocks),
        out_shape=(half, half) if last_call else whole,
        in_specs=[SMEM] * 3 + [VMEM] * (1 + blocks + len(more)),
        out_specs=(VMEM, VMEM) if last_call else VMEM,
        scratch_shapes=scratch,
        input_output_aliases={} if first_call or last_call else {4 + blocks: 0},
        compiler_params=pltpu.CompilerParams(vmem_limit_bytes=16 * 1024 * 1024),
        cost_estimate=pl.CostEstimate(
            flops=blocks * 10**9, bytes_accessed=blocks * 10**6, transcendentals=0
        ),
        name="attend",
    )(place, pairs, counts, q, *pieces, *more)


def call_room(start, stop, slots):
    pairs = 2 * slots * (2 * stop - start - max(start, 1)) * slots
    return -(-pairs // TILE) * TILE


def list_kernel(slots, calls, place, tiles, counts, pairs_out, counts_out):
    core = place[4]
    plane = place[5]
    listed, rows = tiles.shape
    tile = tiles[...]
    bal = (tile * (65536 // slots + 1)) >> 16
    away = (((bal >> 1) - plane) * (2 * core - 1)) & (PLANES - 1)
    same = (bal & 1) == core
    entry = lax.broadcasted_iota(jnp.int32, (listed, rows), 0)
    column = lax.broadcasted_iota(jnp.int32, (listed, rows), 1)
    least = jnp.where(same, 0, 1)
    most = PLANES // 2 - 1 + core
    inside = (away >= least) & (away <= most) & (entry < counts[...])
    down = lax.broadcasted_iota(jnp.int32, (listed, listed), 0)
    along = lax.broadcasted_iota(jnp.int32, (listed, listed), 1)
    before = jnp.where(along < down, 1.0, 0.0)
    down = lax.broadcasted_iota(jnp.int32, (rows, rows), 0)
    along = lax.broadcasted_iota(jnp.int32, (rows, rows), 1)
    ahead = jnp.where(down < along, 1.0, 0.0)
    nothing = rows * TILE
    totals = []
    for call, (start, stop) in enumerate(calls):
        here = inside & (away >= start) & (away < stop)
        held = jnp.where(here, 1.0, 0.0)
        total = jnp.sum(held, axis=0, keepdims=True)
        order = jnp.dot(before, held, preferred_element_type=jnp.float32)
        order = order + jnp.dot(
            jnp.broadcast_to(total, (8, rows)), ahead, preferred_element_type=jnp.float32
        )[:1]
        order = jnp.where(held > 0.0, order, -1.0).astype(jnp.int32)
        skip = stop - start - max(start, 1)
        block = jnp.where(same, away - start, away + skip)
        pair = column * TILE + block * slots + tile - bal * slots - nothing
        room = call_room(start, stop, slots)
        spot = lax.broadcasted_iota(jnp.int32, (listed, room), 1)
        placed = jnp.zeros((1, room), jnp.int32)
        for row in range(rows):
            hit = order[:, row : row + 1] == spot
            placed += jnp.sum(jnp.where(hit, pair[:, row : row + 1], 0), axis=0, keepdims=True)
        pairs_out[call : call + 1, :room] = placed + nothing
        totals.append(jnp.sum(total, axis=1, keepdims=True).astype(jnp.int32))
    counts_out[...] = jnp.concatenate(totals, axis=1)


def list_pairs(calls, key_tiles, key_counts, place, slots):
    rows = 2 * slots
    tiles = lax.dynamic_slice_in_dim(key_tiles.T, place[5] * rows, rows, 1)
    counts = lax.dynamic_slice_in_dim(key_counts, place[5] * rows, rows, 1)
    room = max(call_room(start, stop, slots) for start, stop in calls)
    return pl.pallas_call(
        functools.partial(list_kernel, slots, calls),
        out_shape=(
            jax.ShapeDtypeStruct((len(calls), room), jnp.int32),
            jax.ShapeDtypeStruct((1, len(calls)), jnp.int32),
        ),
        in_specs=[SMEM, VMEM, VMEM],
        out_specs=(VMEM, VMEM),
        compiler_params=pltpu.CompilerParams(vmem_limit_bytes=4 * 1024 * 1024),
        name="lists",
    )(place, tiles, counts)


def on_device(tokens, qkv_weight, q_gain, k_gain, key_tiles, key_counts):
    me_seq = lax.axis_index("seq")
    me_bal = lax.axis_index("bal")
    y, x = me_seq // 4, me_seq % 4
    core = me_bal % 2
    place = jnp.stack(
        (
            jnp.where(core == 0, x, y),
            jnp.where(core == 0, y, x),
            jnp.where(core == 0, 1, 4),
            jnp.where(core == 0, 4, 1),
            core,
            me_bal // 2,
        )
    ).astype(jnp.int32)
    slots = 16 * PIECE // TILE
    before = send(tokens, 1, 1)
    after = send(tokens, 1, -1)
    across = send(tokens, 1, 2)
    gains = jnp.concatenate((q_gain, k_gain), axis=0)
    weight = jnp.transpose(qkv_weight[:, 0], (1, 0, 2))
    own = join(2 * PIECE, (0,), (tokens,))
    after, own, gains = lax.optimization_barrier((after, own, gains))
    high = join(2 * PIECE, (0, PIECE), (after, across))
    after_high = send(high, 2, -1)
    low = join(2 * PIECE, (PIECE,), (before,), (own,))
    before_low = send(low, 2, 1)
    before_high = send(high, 2, 1)
    after_low = send(low, 2, -1)
    across_low = send(before_low, 2, 1)
    across_high = send(after_high, 2, -1)

    low_pieces, high_pieces = (0, 3), (1, 2)
    begun = project(
        ((0, low_pieces), (0, high_pieces), (3, low_pieces), (1, high_pieces)),
        (low, high, before_low, after_high),
        weight,
        gains,
        place,
    )
    begun = project(
        ((1, low_pieces), (3, high_pieces)),
        (after_low, before_high),
        weight,
        gains,
        place,
        begun,
    )
    queries, keys_values = project(
        ((2, low_pieces), (2, high_pieces)),
        (across_low, across_high),
        weight,
        gains,
        place,
        begun,
    )
    def tiles(block):
        return block.reshape(-1, TILE, block.shape[1])

    same, other, sums = [keys_values], [swap_cores(keys_values)], None
    for step in range(1, PLANES // 2 + 1):
        cores = (0, 1) if step < PLANES // 2 else (1,)
        same.append(pass_on(same[-1], cores))
        other.append(pass_on(other[-1], cores))
        if sums is not None:
            same[-1], sums = lax.optimization_barrier((same[-1], sums))
        if step == 1:
            queries, other[0] = lax.optimization_barrier((queries, other[0]))
            other_queries = swap_cores(queries)
            same[1], other_queries = lax.optimization_barrier((same[1], other_queries))
        if step == 2:
            key_tiles, other[1] = lax.optimization_barrier((key_tiles, other[1]))
            pairs, counts = list_pairs(CALLS, key_tiles[0], key_counts, place, slots)
            same[2], pairs, counts = lax.optimization_barrier((same[2], pairs, counts))
            low_queries = jnp.where(core == 0, queries, other_queries)
            high_queries = jnp.where(core == 0, other_queries, queries)
            chip_queries = tiles(jnp.concatenate((low_queries, high_queries), axis=0))
            other[2], chip_queries = lax.optimization_barrier((other[2], chip_queries))
        call = step - CALLS[0][1] + 1
        if call >= 0:
            start, stop = CALLS[call]
            blocks = [tiles(block) for block in same[start:stop] + other[max(start, 1) : stop]]
            sums = attend(call, len(CALLS), place, pairs, counts, chip_queries, blocks, sums)
    kept, given = sums
    sums = kept + swap_cores(given)
    result = (sums[:, :, :HEAD] / sums[:, :, HEAD:]).astype(jnp.bfloat16)
    return lax.all_to_all(
        result.reshape(slots * TILE, HEAD), "seq", split_axis=0, concat_axis=1, tiled=True
    )


def solution(mesh):
    placed = (
        P(("bal", "seq"), None),
        P(None, "seq", None, None),
        P("seq", None),
        P("seq", None),
        P("seq", None, None),
        P("seq", None),
    )
    return jax.shard_map(
        on_device, mesh=mesh, in_specs=placed, out_specs=P(("bal", "seq"), None), check_vma=False
    )
```

```python
import functools
import jax
import jax.numpy as jnp
from jax import lax
from jax.experimental import pallas as pl
from jax.experimental.pallas import tpu as pltpu
from jax.sharding import PartitionSpec as P

TILE = 128
HEAD = 128
PIECE = 48
PLANES = 16
UNROLL = 8
CALLS = ((0, 3),) + tuple((step, step + 1) for step in range(3, 9))
LOG2E = 1.4426950408889634
MESH_AXES = ("seq", "bal")
VMEM = pl.BlockSpec(memory_space=pltpu.VMEM)
SMEM = pl.BlockSpec(memory_space=pltpu.SMEM)


def plane_perm(phase, shift):
    pairs = []
    for bal in range(32):
        for y in range(4):
            for x in range(4):
                along_x = (bal % 2 == 0) == (phase == 1)
                to_y = y if along_x else (y + shift) % 4
                to_x = (x + shift) % 4 if along_x else x
                pairs.append(((4 * y + x) * 32 + bal, (4 * to_y + to_x) * 32 + bal))
    return pairs


def send(block, phase, shift):
    return lax.ppermute(block, MESH_AXES, plane_perm(phase, shift))


def join_kernel(starts, *refs):
    parts = refs[: len(starts)]
    out, done = refs[-2:]
    copies = []
    for at, start in enumerate(starts):
        here = out.at[pl.ds(start, parts[at].shape[0]), :]
        copies.append(pltpu.make_async_copy(parts[at], here, done.at[at]))
    for copy in copies:
        copy.start()
    for copy in copies:
        copy.wait()


def join(rows, starts, parts, begun=()):
    anywhere = pl.BlockSpec(memory_space=pl.ANY)
    return pl.pallas_call(
        functools.partial(join_kernel, starts),
        out_shape=jax.ShapeDtypeStruct((rows, parts[0].shape[1]), parts[0].dtype),
        in_specs=[anywhere] * (len(parts) + len(begun)),
        out_specs=anywhere,
        scratch_shapes=[pltpu.SemaphoreType.DMA((len(parts),))],
        input_output_aliases={len(parts): 0} if begun else {},
        compiler_params=pltpu.CompilerParams(vmem_limit_bytes=1024 * 1024),
        name="join",
    )(*parts, *begun)


def swap_cores(block):
    return lax.ppermute(block, "bal", [(at, at ^ 1) for at in range(32)])


def pass_on(block, cores):
    pairs = []
    for z in range(PLANES):
        if 0 in cores:
            pairs.append((2 * z, 2 * ((z + 1) % PLANES)))
        if 1 in cores:
            pairs.append((2 * z + 1, 2 * ((z - 1) % PLANES) + 1))
    return lax.ppermute(block, "bal", pairs)


def project_kernel(shares, place, *refs):
    count = len(shares)
    blocks = refs[:count]
    weight, gains = refs[count : count + 2]
    q_out, kv_out, q_held, kv_held, leave = refs[-5:]
    first = place[0]
    second = place[1]
    first_step = place[2]
    second_step = place[3]

    def normalize(values, gain):
        mean_square = jnp.mean(values * values, axis=-1, keepdims=True)
        return (values * lax.rsqrt(mean_square + 1e-06) * gain).astype(jnp.bfloat16)

    rows = jnp.concatenate([block[...] for block in blocks], axis=0)
    whole = jnp.concatenate([weight[at] for at in range(3)], axis=1)
    proj = jnp.dot(rows, whole, preferred_element_type=jnp.float32)
    q_held[...] = normalize(proj[:, :HEAD], gains[0:1, :])
    kv_held[:, :HEAD] = normalize(proj[:, HEAD : 2 * HEAD], gains[1:2, :])
    kv_held[:, HEAD:] = proj[:, 2 * HEAD :].astype(jnp.bfloat16)
    row = 0
    for shift, pieces in shares:
        for piece in pieces:
            spot = ((first + piece) % 4) * first_step + ((second + shift) % 4) * second_step
            target = pl.ds(pl.multiple_of(spot * PIECE, PIECE), PIECE)
            source = pl.ds(row, PIECE)
            pltpu.make_async_copy(q_held.at[source, :], q_out.at[target, :], leave.at[0]).start()
            pltpu.make_async_copy(kv_held.at[source, :], kv_out.at[target, :], leave.at[1]).start()
            row += PIECE
    pltpu.make_async_copy(q_held, q_held, leave.at[0]).wait()
    pltpu.make_async_copy(kv_held, kv_held, leave.at[1]).wait()


def project(shares, blocks, weight, gains, place, begun=()):
    rows = 16 * PIECE
    count = len(blocks)
    rows_here = sum(len(pieces) for _, pieces in shares) * PIECE
    anywhere = pl.BlockSpec(memory_space=pl.ANY)
    return pl.pallas_call(
        functools.partial(project_kernel, shares),
        out_shape=(
            jax.ShapeDtypeStruct((rows, HEAD), jnp.bfloat16),
            jax.ShapeDtypeStruct((rows, 2 * HEAD), jnp.bfloat16),
        ),
        in_specs=[SMEM] + [VMEM] * (count + 2) + [anywhere] * len(begun),
        out_specs=(anywhere, anywhere),
        scratch_shapes=[
            pltpu.VMEM((rows_here, HEAD), jnp.bfloat16),
            pltpu.VMEM((rows_here, 2 * HEAD), jnp.bfloat16),
            pltpu.SemaphoreType.DMA((2,)),
        ],
        input_output_aliases={count + 3: 0, count + 4: 1} if begun else {},
        compiler_params=pltpu.CompilerParams(vmem_limit_bytes=20 * 1024 * 1024),
        name="project",
    )(place, *blocks, weight, gains, *begun)


def attend_kernel(scale, first_call, last_call, call, blocks, place, pairs, counts, q, *refs):
    pieces = refs[:blocks]
    kv = refs[-1]
    rows = q.shape[0]
    slots = rows // 2
    if last_call:
        sums_in, kept, given, sums = refs[blocks : blocks + 4]
    elif first_call:
        sums = refs[blocks]
    else:
        sums_in, sums = refs[blocks : blocks + 2]
    start = 0
    for piece in pieces:
        kv[start : start + piece.shape[0]] = piece[...]
        start += piece.shape[0]
    if first_call:
        sums[...] = jnp.zeros_like(sums)
    else:
        sums[...] = sums_in[...]
    ones = jnp.ones((TILE, HEAD), jnp.bfloat16)

    def turn(step, _):
        rows_here, scores, products = [], [], []
        for at in range(UNROLL):
            pair = pairs[call, step * UNROLL + at]
            rows_here.append((pair >> 7, pair & 127))
        for row, tile in rows_here:
            scores.append(
                lax.dot_general(
                    q[jnp.minimum(row, rows - 1)],
                    kv[tile, :, :HEAD],
                    (((1,), (1,)), ((), ())),
                    preferred_element_type=jnp.float32,
                )
            )
        for (row, tile), score in zip(rows_here, scores):
            weights = jnp.exp2(score * scale).astype(jnp.bfloat16)
            values = jnp.concatenate((kv[tile, :, HEAD:], ones), axis=1)
            products.append(jnp.dot(weights, values, preferred_element_type=jnp.float32))
        for (row, _), product in zip(rows_here, products):
            sums[row] += product
        return 0

    lax.fori_loop(0, (counts[0, call] + UNROLL - 1) // UNROLL, turn, 0)
    if last_call:
        core = place[4]
        for at in range(slots):
            kept[at] = sums[core * slots + at]
            given[at] = sums[(1 - core) * slots + at]


def attend(call, calls, place, pairs, counts, q, pieces, sums=None):
    scale = HEAD ** (-0.5) * LOG2E
    first_call, last_call = call == 0, call == calls - 1
    blocks, rows = len(pieces), q.shape[0]
    slots = rows // 2
    held = sum(piece.shape[0] for piece in pieces)
    whole = jax.ShapeDtypeStruct((rows + 1, TILE, 2 * HEAD), jnp.float32)
    half = jax.ShapeDtypeStruct((slots, TILE, 2 * HEAD), jnp.float32)
    scratch = [pltpu.VMEM((held, TILE, 2 * HEAD), jnp.bfloat16)]
    if last_call:
        scratch.insert(0, pltpu.VMEM(whole.shape, whole.dtype))
    more = () if first_call else (sums,)
    return pl.pallas_call(
        functools.partial(attend_kernel, scale, first_call, last_call, call, blocks),
        out_shape=(half, half) if last_call else whole,
        in_specs=[SMEM] * 3 + [VMEM] * (1 + blocks + len(more)),
        out_specs=(VMEM, VMEM) if last_call else VMEM,
        scratch_shapes=scratch,
        input_output_aliases={} if first_call or last_call else {4 + blocks: 0},
        compiler_params=pltpu.CompilerParams(vmem_limit_bytes=16 * 1024 * 1024),
        cost_estimate=pl.CostEstimate(
            flops=blocks * 10**9, bytes_accessed=blocks * 10**6, transcendentals=0
        ),
        name="attend",
    )(place, pairs, counts, q, *pieces, *more)


def call_room(start, stop, slots):
    pairs = 2 * slots * (2 * stop - start - max(start, 1)) * slots
    return -(-pairs // TILE) * TILE


def list_kernel(slots, calls, place, tiles, counts, pairs_out, counts_out):
    core = place[4]
    plane = place[5]
    listed, rows = tiles.shape
    tile = tiles[...]
    bal = (tile * (65536 // slots + 1)) >> 16
    away = (((bal >> 1) - plane) * (2 * core - 1)) & (PLANES - 1)
    same = (bal & 1) == core
    entry = lax.broadcasted_iota(jnp.int32, (listed, rows), 0)
    column = lax.broadcasted_iota(jnp.int32, (listed, rows), 1)
    least = jnp.where(same, 0, 1)
    last, half = PLANES // 2, slots // 2
    order_in = tile - bal * slots
    far = away == last
    low_tile = jnp.where(far, jnp.where(same, 0, half), 0)
    high_tile = jnp.where(far, jnp.where(same, half + half * core, slots * core), slots)
    moved = jnp.where(far, jnp.where(same, slots - slots * core, -half), 0)
    inside = (away >= least) & (away <= last) & (entry < counts[...])
    inside = inside & (order_in >= low_tile) & (order_in < high_tile)
    down = lax.broadcasted_iota(jnp.int32, (listed, listed), 0)
    along = lax.broadcasted_iota(jnp.int32, (listed, listed), 1)
    before = jnp.where(along < down, 1.0, 0.0)
    down = lax.broadcasted_iota(jnp.int32, (rows, rows), 0)
    along = lax.broadcasted_iota(jnp.int32, (rows, rows), 1)
    ahead = jnp.where(down < along, 1.0, 0.0)
    nothing = rows * TILE
    totals = []
    for call, (start, stop) in enumerate(calls):
        here = inside & (away >= start) & (away < stop)
        held = jnp.where(here, 1.0, 0.0)
        total = jnp.sum(held, axis=0, keepdims=True)
        order = jnp.dot(before, held, preferred_element_type=jnp.float32)
        order = order + jnp.dot(
            jnp.broadcast_to(total, (8, rows)), ahead, preferred_element_type=jnp.float32
        )[:1]
        order = jnp.where(held > 0.0, order, -1.0).astype(jnp.int32)
        skip = stop - start - max(start, 1)
        block = jnp.where(same, away - start, away + skip)
        pair = column * TILE + block * slots + order_in + moved - nothing
        room = call_room(start, stop, slots)
        spot = lax.broadcasted_iota(jnp.int32, (listed, room), 1)
        placed = jnp.zeros((1, room), jnp.int32)
        for row in range(rows):
            hit = order[:, row : row + 1] == spot
            placed += jnp.sum(jnp.where(hit, pair[:, row : row + 1], 0), axis=0, keepdims=True)
        pairs_out[call : call + 1, :room] = placed + nothing
        totals.append(jnp.sum(total, axis=1, keepdims=True).astype(jnp.int32))
    counts_out[...] = jnp.concatenate(totals, axis=1)


def list_pairs(calls, key_tiles, key_counts, place, slots):
    rows = 2 * slots
    tiles = lax.dynamic_slice_in_dim(key_tiles.T, place[5] * rows, rows, 1)
    counts = lax.dynamic_slice_in_dim(key_counts, place[5] * rows, rows, 1)
    room = max(call_room(start, stop, slots) for start, stop in calls)
    return pl.pallas_call(
        functools.partial(list_kernel, slots, calls),
        out_shape=(
            jax.ShapeDtypeStruct((len(calls), room), jnp.int32),
            jax.ShapeDtypeStruct((1, len(calls)), jnp.int32),
        ),
        in_specs=[SMEM, VMEM, VMEM],
        out_specs=(VMEM, VMEM),
        compiler_params=pltpu.CompilerParams(vmem_limit_bytes=4 * 1024 * 1024),
        name="lists",
    )(place, tiles, counts)


def on_device(tokens, qkv_weight, q_gain, k_gain, key_tiles, key_counts):
    me_seq = lax.axis_index("seq")
    me_bal = lax.axis_index("bal")
    y, x = me_seq // 4, me_seq % 4
    core = me_bal % 2
    place = jnp.stack(
        (
            jnp.where(core == 0, x, y),
            jnp.where(core == 0, y, x),
            jnp.where(core == 0, 1, 4),
            jnp.where(core == 0, 4, 1),
            core,
            me_bal // 2,
        )
    ).astype(jnp.int32)
    slots = 16 * PIECE // TILE
    before = send(tokens, 1, 1)
    after = send(tokens, 1, -1)
    across = send(tokens, 1, 2)
    gains = jnp.concatenate((q_gain, k_gain), axis=0)
    weight = jnp.transpose(qkv_weight[:, 0], (1, 0, 2))
    own = join(2 * PIECE, (0,), (tokens,))
    after, own, gains = lax.optimization_barrier((after, own, gains))
    high = join(2 * PIECE, (0, PIECE), (after, across))
    after_high = send(high, 2, -1)
    low = join(2 * PIECE, (PIECE,), (before,), (own,))
    before_low = send(low, 2, 1)
    before_high = send(high, 2, 1)
    after_low = send(low, 2, -1)
    across_low = send(before_low, 2, 1)
    across_high = send(after_high, 2, -1)

    low_pieces, high_pieces = (0, 3), (1, 2)
    begun = project(
        ((0, low_pieces), (0, high_pieces), (3, low_pieces), (1, high_pieces)),
        (low, high, before_low, after_high),
        weight,
        gains,
        place,
    )
    begun = project(
        ((1, low_pieces), (3, high_pieces)),
        (after_low, before_high),
        weight,
        gains,
        place,
        begun,
    )
    queries, keys_values = project(
        ((2, low_pieces), (2, high_pieces)),
        (across_low, across_high),
        weight,
        gains,
        place,
        begun,
    )
    def tiles(block):
        return block.reshape(-1, TILE, block.shape[1])

    same, other, sums = [keys_values], [swap_cores(keys_values)], None
    for step in range(1, PLANES // 2 + 1):
        if step < PLANES // 2:
            same.append(pass_on(same[-1], (0, 1)))
            other.append(pass_on(other[-1], (0, 1)))
        else:
            half = keys_values.shape[0] // 2
            same.append(pass_on(same[-1], (1,)))
            share = jnp.where(core == 0, same[step - 1][:half], other[step - 1][half:])
            other.append(pass_on(share, (0, 1)))
        if sums is not None:
            same[-1], sums = lax.optimization_barrier((same[-1], sums))
        if step == 1:
            queries, other[0] = lax.optimization_barrier((queries, other[0]))
            other_queries = swap_cores(queries)
            same[1], other_queries = lax.optimization_barrier((same[1], other_queries))
        if step == 2:
            key_tiles, other[1] = lax.optimization_barrier((key_tiles, other[1]))
            pairs, counts = list_pairs(CALLS, key_tiles[0], key_counts, place, slots)
            same[2], pairs, counts = lax.optimization_barrier((same[2], pairs, counts))
            low_queries = jnp.where(core == 0, queries, other_queries)
            high_queries = jnp.where(core == 0, other_queries, queries)
            chip_queries = tiles(jnp.concatenate((low_queries, high_queries), axis=0))
            other[2], chip_queries = lax.optimization_barrier((other[2], chip_queries))
        call = step - CALLS[0][1] + 1
        if call >= 0:
            start, stop = CALLS[call]
            blocks = [tiles(block) for block in same[start:stop] + other[max(start, 1) : stop]]
            sums = attend(call, len(CALLS), place, pairs, counts, chip_queries, blocks, sums)
    kept, given = sums
    sums = kept + swap_cores(given)
    result = (sums[:, :, :HEAD] / sums[:, :, HEAD:]).astype(jnp.bfloat16)
    return lax.all_to_all(
        result.reshape(slots * TILE, HEAD), "seq", split_axis=0, concat_axis=1, tiled=True
    )


def solution(mesh):
    placed = (
        P(("bal", "seq"), None),
        P(None, "seq", None, None),
        P("seq", None),
        P("seq", None),
        P("seq", None, None),
        P("seq", None),
    )
    return jax.shard_map(
        on_device, mesh=mesh, in_specs=placed, out_specs=P(("bal", "seq"), None), check_vma=False
    )
```

```python
import functools
import jax
import jax.numpy as jnp
from jax import lax
from jax.experimental import pallas as pl
from jax.experimental.pallas import tpu as pltpu
from jax.sharding import PartitionSpec as P

TILE = 128
HEAD = 128
PIECE = 48
PLANES = 16
UNROLL = 8
CALLS = ((0, 3, None),) + tuple((step, step + 1, None) for step in range(3, 8))
CALLS += ((8, 9, "other"), (8, 9, "own"))
LOG2E = 1.4426950408889634
MESH_AXES = ("seq", "bal")
VMEM = pl.BlockSpec(memory_space=pltpu.VMEM)
SMEM = pl.BlockSpec(memory_space=pltpu.SMEM)


def plane_perm(phase, shift):
    pairs = []
    for bal in range(32):
        for y in range(4):
            for x in range(4):
                along_x = (bal % 2 == 0) == (phase == 1)
                to_y = y if along_x else (y + shift) % 4
                to_x = (x + shift) % 4 if along_x else x
                pairs.append(((4 * y + x) * 32 + bal, (4 * to_y + to_x) * 32 + bal))
    return pairs


def send(block, phase, shift):
    return lax.ppermute(block, MESH_AXES, plane_perm(phase, shift))


def join_kernel(starts, *refs):
    parts = refs[: len(starts)]
    out, done = refs[-2:]
    copies = []
    for at, start in enumerate(starts):
        here = out.at[pl.ds(start, parts[at].shape[0]), :]
        copies.append(pltpu.make_async_copy(parts[at], here, done.at[at]))
    for copy in copies:
        copy.start()
    for copy in copies:
        copy.wait()


def join(rows, starts, parts, begun=()):
    anywhere = pl.BlockSpec(memory_space=pl.ANY)
    return pl.pallas_call(
        functools.partial(join_kernel, starts),
        out_shape=jax.ShapeDtypeStruct((rows, parts[0].shape[1]), parts[0].dtype),
        in_specs=[anywhere] * (len(parts) + len(begun)),
        out_specs=anywhere,
        scratch_shapes=[pltpu.SemaphoreType.DMA((len(parts),))],
        input_output_aliases={len(parts): 0} if begun else {},
        compiler_params=pltpu.CompilerParams(vmem_limit_bytes=1024 * 1024),
        name="join",
    )(*parts, *begun)


def swap_cores(block):
    return lax.ppermute(block, "bal", [(at, at ^ 1) for at in range(32)])


def pass_on(block, cores):
    pairs = []
    for z in range(PLANES):
        if 0 in cores:
            pairs.append((2 * z, 2 * ((z + 1) % PLANES)))
        if 1 in cores:
            pairs.append((2 * z + 1, 2 * ((z - 1) % PLANES) + 1))
    return lax.ppermute(block, "bal", pairs)


def project_kernel(shares, place, *refs):
    count = len(shares)
    blocks = refs[:count]
    weight, gains = refs[count : count + 2]
    q_out, kv_out, q_held, kv_held, leave = refs[-5:]
    first = place[0]
    second = place[1]
    first_step = place[2]
    second_step = place[3]

    def normalize(values, gain):
        mean_square = jnp.mean(values * values, axis=-1, keepdims=True)
        return (values * lax.rsqrt(mean_square + 1e-06) * gain).astype(jnp.bfloat16)

    rows = jnp.concatenate([block[...] for block in blocks], axis=0)
    whole = jnp.concatenate([weight[at] for at in range(3)], axis=1)
    proj = jnp.dot(rows, whole, preferred_element_type=jnp.float32)
    q_held[...] = normalize(proj[:, :HEAD], gains[0:1, :])
    kv_held[:, :HEAD] = normalize(proj[:, HEAD : 2 * HEAD], gains[1:2, :])
    kv_held[:, HEAD:] = proj[:, 2 * HEAD :].astype(jnp.bfloat16)
    row = 0
    for shift, pieces in shares:
        for piece in pieces:
            spot = ((first + piece) % 4) * first_step + ((second + shift) % 4) * second_step
            target = pl.ds(pl.multiple_of(spot * PIECE, PIECE), PIECE)
            source = pl.ds(row, PIECE)
            pltpu.make_async_copy(q_held.at[source, :], q_out.at[target, :], leave.at[0]).start()
            pltpu.make_async_copy(kv_held.at[source, :], kv_out.at[target, :], leave.at[1]).start()
            row += PIECE
    pltpu.make_async_copy(q_held, q_held, leave.at[0]).wait()
    pltpu.make_async_copy(kv_held, kv_held, leave.at[1]).wait()


def project(shares, blocks, weight, gains, place, begun=()):
    rows = 16 * PIECE
    count = len(blocks)
    rows_here = sum(len(pieces) for _, pieces in shares) * PIECE
    anywhere = pl.BlockSpec(memory_space=pl.ANY)
    return pl.pallas_call(
        functools.partial(project_kernel, shares),
        out_shape=(
            jax.ShapeDtypeStruct((rows, HEAD), jnp.bfloat16),
            jax.ShapeDtypeStruct((rows, 2 * HEAD), jnp.bfloat16),
        ),
        in_specs=[SMEM] + [VMEM] * (count + 2) + [anywhere] * len(begun),
        out_specs=(anywhere, anywhere),
        scratch_shapes=[
            pltpu.VMEM((rows_here, HEAD), jnp.bfloat16),
            pltpu.VMEM((rows_here, 2 * HEAD), jnp.bfloat16),
            pltpu.SemaphoreType.DMA((2,)),
        ],
        input_output_aliases={count + 3: 0, count + 4: 1} if begun else {},
        compiler_params=pltpu.CompilerParams(vmem_limit_bytes=20 * 1024 * 1024),
        name="project",
    )(place, *blocks, weight, gains, *begun)


def attend_kernel(scale, call, part, blocks, place, pairs, counts, q, *refs):
    pieces = refs[:blocks]
    sums, kv = refs[-2:]
    slots = pieces[0].shape[0]
    rows = q.shape[0]
    for at in range(blocks):
        kv[at * slots : (at + 1) * slots] = pieces[at][...]
    if call == 0:
        sums[...] = jnp.zeros_like(sums)
    elif part is None:
        sums[...] = refs[blocks][...]
    else:
        base = (place[4] if part == "own" else 1 - place[4]) * slots
        for at in range(slots):
            sums[at] = refs[blocks][base + at]
    ones = jnp.ones((TILE, HEAD), jnp.bfloat16)

    def turn(step, _):
        rows_here, scores, products = [], [], []
        for at in range(UNROLL):
            pair = pairs[call, step * UNROLL + at]
            rows_here.append((pair >> 7, pair & 127))
        for row, tile in rows_here:
            scores.append(
                lax.dot_general(
                    q[jnp.minimum(row, rows - 1)],
                    kv[tile, :, :HEAD],
                    (((1,), (1,)), ((), ())),
                    preferred_element_type=jnp.float32,
                )
            )
        for (row, tile), score in zip(rows_here, scores):
            weights = jnp.exp2(score * scale).astype(jnp.bfloat16)
            values = jnp.concatenate((kv[tile, :, HEAD:], ones), axis=1)
            products.append(jnp.dot(weights, values, preferred_element_type=jnp.float32))
        for (row, _), product in zip(rows_here, products):
            if part is not None:
                row = jnp.where(row == rows, slots, row - base)
            sums[row] += product
        return 0

    lax.fori_loop(0, (counts[0, call] + UNROLL - 1) // UNROLL, turn, 0)
    if part is not None:
        refs[-3][...] = sums[:slots]


def attend(call, place, pairs, counts, q, pieces, sums=None):
    scale = HEAD ** (-0.5) * LOG2E
    part = CALLS[call][2]
    blocks, slots, rows = len(pieces), pieces[0].shape[0], q.shape[0]
    scratch = [pltpu.VMEM((blocks * slots, TILE, 2 * HEAD), jnp.bfloat16)]
    rows_out = rows + 1
    if part is not None:
        rows_out = slots
        scratch.insert(0, pltpu.VMEM((slots + 1, TILE, 2 * HEAD), jnp.float32))
    more = () if call == 0 else (sums,)
    return pl.pallas_call(
        functools.partial(attend_kernel, scale, call, part, blocks),
        out_shape=jax.ShapeDtypeStruct((rows_out, TILE, 2 * HEAD), jnp.float32),
        in_specs=[SMEM] * 3 + [VMEM] * (1 + blocks + len(more)),
        out_specs=VMEM,
        scratch_shapes=scratch,
        input_output_aliases={4 + blocks: 0} if call > 0 and part is None else {},
        compiler_params=pltpu.CompilerParams(vmem_limit_bytes=16 * 1024 * 1024),
        cost_estimate=pl.CostEstimate(
            flops=blocks * 10**9, bytes_accessed=blocks * 10**6, transcendentals=0
        ),
        name="attend",
    )(place, pairs, counts, q, *pieces, *more)


def call_room(start, stop, slots):
    pairs = 2 * slots * (2 * stop - start - max(start, 1)) * slots
    return -(-pairs // TILE) * TILE


def list_kernel(slots, calls, place, tiles, counts, pairs_out, counts_out):
    core = place[4]
    plane = place[5]
    listed, rows = tiles.shape
    tile = tiles[...]
    bal = (tile * (65536 // slots + 1)) >> 16
    away = (((bal >> 1) - plane) * (2 * core - 1)) & (PLANES - 1)
    same = (bal & 1) == core
    entry = lax.broadcasted_iota(jnp.int32, (listed, rows), 0)
    column = lax.broadcasted_iota(jnp.int32, (listed, rows), 1)
    least = jnp.where(same, 0, 1)
    most = PLANES // 2 - 1 + core
    inside = (away >= least) & (away <= most) & (entry < counts[...])
    down = lax.broadcasted_iota(jnp.int32, (listed, listed), 0)
    along = lax.broadcasted_iota(jnp.int32, (listed, listed), 1)
    before = jnp.where(along < down, 1.0, 0.0)
    down = lax.broadcasted_iota(jnp.int32, (rows, rows), 0)
    along = lax.broadcasted_iota(jnp.int32, (rows, rows), 1)
    ahead = jnp.where(down < along, 1.0, 0.0)
    nothing = rows * TILE
    totals = []
    theirs = jnp.where(column >= slots, 1 - core, core)
    for call, (start, stop, part) in enumerate(calls):
        here = inside & (away >= start) & (away < stop)
        if part is not None:
            here = here & (theirs == (0 if part == "own" else 1))
        held = jnp.where(here, 1.0, 0.0)
        total = jnp.sum(held, axis=0, keepdims=True)
        order = jnp.dot(before, held, preferred_element_type=jnp.float32)
        order = order + jnp.dot(
            jnp.broadcast_to(total, (8, rows)), ahead, preferred_element_type=jnp.float32
        )[:1]
        order = jnp.where(held > 0.0, order, -1.0).astype(jnp.int32)
        skip = stop - start - max(start, 1)
        block = jnp.where(same, away - start, away + skip)
        pair = column * TILE + block * slots + tile - bal * slots - nothing
        room = call_room(start, stop, slots)
        spot = lax.broadcasted_iota(jnp.int32, (listed, room), 1)
        placed = jnp.zeros((1, room), jnp.int32)
        for row in range(rows):
            hit = order[:, row : row + 1] == spot
            placed += jnp.sum(jnp.where(hit, pair[:, row : row + 1], 0), axis=0, keepdims=True)
        pairs_out[call : call + 1, :room] = placed + nothing
        totals.append(jnp.sum(total, axis=1, keepdims=True).astype(jnp.int32))
    counts_out[...] = jnp.concatenate(totals, axis=1)


def list_pairs(calls, key_tiles, key_counts, place, slots):
    rows = 2 * slots
    tiles = lax.dynamic_slice_in_dim(key_tiles.T, place[5] * rows, rows, 1)
    counts = lax.dynamic_slice_in_dim(key_counts, place[5] * rows, rows, 1)
    room = max(call_room(start, stop, slots) for start, stop, _ in calls)
    return pl.pallas_call(
        functools.partial(list_kernel, slots, calls),
        out_shape=(
            jax.ShapeDtypeStruct((len(calls), room), jnp.int32),
            jax.ShapeDtypeStruct((1, len(calls)), jnp.int32),
        ),
        in_specs=[SMEM, VMEM, VMEM],
        out_specs=(VMEM, VMEM),
        compiler_params=pltpu.CompilerParams(vmem_limit_bytes=12 * 1024 * 1024),
        name="lists",
    )(place, tiles, counts)


def on_device(tokens, qkv_weight, q_gain, k_gain, key_tiles, key_counts):
    me_seq = lax.axis_index("seq")
    me_bal = lax.axis_index("bal")
    y, x = me_seq // 4, me_seq % 4
    core = me_bal % 2
    place = jnp.stack(
        (
            jnp.where(core == 0, x, y),
            jnp.where(core == 0, y, x),
            jnp.where(core == 0, 1, 4),
            jnp.where(core == 0, 4, 1),
            core,
            me_bal // 2,
        )
    ).astype(jnp.int32)
    slots = 16 * PIECE // TILE
    before = send(tokens, 1, 1)
    after = send(tokens, 1, -1)
    across = send(tokens, 1, 2)
    gains = jnp.concatenate((q_gain, k_gain), axis=0)
    weight = jnp.transpose(qkv_weight[:, 0], (1, 0, 2))
    own = join(2 * PIECE, (0,), (tokens,))
    after, own, gains = lax.optimization_barrier((after, own, gains))
    high = join(2 * PIECE, (0, PIECE), (after, across))
    after_high = send(high, 2, -1)
    low = join(2 * PIECE, (PIECE,), (before,), (own,))
    before_low = send(low, 2, 1)
    before_high = send(high, 2, 1)
    after_low = send(low, 2, -1)
    across_low = send(before_low, 2, 1)
    across_high = send(after_high, 2, -1)

    low_pieces, high_pieces = (0, 3), (1, 2)
    begun = project(
        ((0, low_pieces), (0, high_pieces), (3, low_pieces), (1, high_pieces)),
        (low, high, before_low, after_high),
        weight,
        gains,
        place,
    )
    begun = project(
        ((1, low_pieces), (3, high_pieces)),
        (after_low, before_high),
        weight,
        gains,
        place,
        begun,
    )
    queries, keys_values = project(
        ((2, low_pieces), (2, high_pieces)),
        (across_low, across_high),
        weight,
        gains,
        place,
        begun,
    )
    def tiles(block):
        return block.reshape(-1, TILE, block.shape[1])

    same, other, sums = [keys_values], [swap_cores(keys_values)], None
    for step in range(1, PLANES // 2 + 1):
        cores = (0, 1) if step < PLANES // 2 else (1,)
        same.append(pass_on(same[-1], cores))
        other.append(pass_on(other[-1], cores))
        if sums is not None:
            same[-1], sums = lax.optimization_barrier((same[-1], sums))
        if step == 1:
            queries, other[0] = lax.optimization_barrier((queries, other[0]))
            other_queries = swap_cores(queries)
            same[1], other_queries = lax.optimization_barrier((same[1], other_queries))
        if step == 2:
            key_tiles, other[1] = lax.optimization_barrier((key_tiles, other[1]))
            pairs, counts = list_pairs(CALLS, key_tiles[0], key_counts, place, slots)
            same[2], pairs, counts = lax.optimization_barrier((same[2], pairs, counts))
            low_queries = jnp.where(core == 0, queries, other_queries)
            high_queries = jnp.where(core == 0, other_queries, queries)
            chip_queries = tiles(jnp.concatenate((low_queries, high_queries), axis=0))
            other[2], chip_queries = lax.optimization_barrier((other[2], chip_queries))
        call = step - CALLS[0][1] + 1
        if call >= 0:
            start, stop, part = CALLS[call]
            blocks = [tiles(block) for block in same[start:stop] + other[max(start, 1) : stop]]
            if part is None:
                sums = attend(call, place, pairs, counts, chip_queries, blocks, sums)
    given = swap_cores(attend(call, place, pairs, counts, chip_queries, blocks, sums))
    kept = attend(call + 1, place, pairs, counts, chip_queries, blocks, sums)
    sums = kept + given
    result = (sums[:, :, :HEAD] / sums[:, :, HEAD:]).astype(jnp.bfloat16)
    return lax.all_to_all(
        result.reshape(slots * TILE, HEAD), "seq", split_axis=0, concat_axis=1, tiled=True
    )


def solution(mesh):
    placed = (
        P(("bal", "seq"), None),
        P(None, "seq", None, None),
        P("seq", None),
        P("seq", None),
        P("seq", None, None),
        P("seq", None),
    )
    return jax.shard_map(
        on_device, mesh=mesh, in_specs=placed, out_specs=P(("bal", "seq"), None), check_vma=False
    )
```

```python
import functools
import jax
import jax.numpy as jnp
from jax import lax
from jax.experimental import pallas as pl
from jax.experimental.pallas import tpu as pltpu
from jax.sharding import PartitionSpec as P

TILE = 128
HEAD = 128
PIECE = 48
PLANES = 16
UNROLL = 8
CALLS = ((0, 3, None, None),) + tuple((step, step + 1, None, None) for step in range(3, 8))
CALLS += ((8, 9, None, "same"), (8, 9, "other", "other"), (8, 9, "own", "other"))
LOG2E = 1.4426950408889634
MESH_AXES = ("seq", "bal")
VMEM = pl.BlockSpec(memory_space=pltpu.VMEM)
SMEM = pl.BlockSpec(memory_space=pltpu.SMEM)


def plane_perm(phase, shift):
    pairs = []
    for bal in range(32):
        for y in range(4):
            for x in range(4):
                along_x = (bal % 2 == 0) == (phase == 1)
                to_y = y if along_x else (y + shift) % 4
                to_x = (x + shift) % 4 if along_x else x
                pairs.append(((4 * y + x) * 32 + bal, (4 * to_y + to_x) * 32 + bal))
    return pairs


def send(block, phase, shift):
    return lax.ppermute(block, MESH_AXES, plane_perm(phase, shift))


def join_kernel(starts, *refs):
    parts = refs[: len(starts)]
    out, done = refs[-2:]
    copies = []
    for at, start in enumerate(starts):
        here = out.at[pl.ds(start, parts[at].shape[0]), :]
        copies.append(pltpu.make_async_copy(parts[at], here, done.at[at]))
    for copy in copies:
        copy.start()
    for copy in copies:
        copy.wait()


def join(rows, starts, parts, begun=()):
    anywhere = pl.BlockSpec(memory_space=pl.ANY)
    return pl.pallas_call(
        functools.partial(join_kernel, starts),
        out_shape=jax.ShapeDtypeStruct((rows, parts[0].shape[1]), parts[0].dtype),
        in_specs=[anywhere] * (len(parts) + len(begun)),
        out_specs=anywhere,
        scratch_shapes=[pltpu.SemaphoreType.DMA((len(parts),))],
        input_output_aliases={len(parts): 0} if begun else {},
        compiler_params=pltpu.CompilerParams(vmem_limit_bytes=1024 * 1024),
        name="join",
    )(*parts, *begun)


def swap_cores(block):
    return lax.ppermute(block, "bal", [(at, at ^ 1) for at in range(32)])


def pass_on(block, cores):
    pairs = []
    for z in range(PLANES):
        if 0 in cores:
            pairs.append((2 * z, 2 * ((z + 1) % PLANES)))
        if 1 in cores:
            pairs.append((2 * z + 1, 2 * ((z - 1) % PLANES) + 1))
    return lax.ppermute(block, "bal", pairs)


def project_kernel(shares, place, *refs):
    count = len(shares)
    blocks = refs[:count]
    weight, gains = refs[count : count + 2]
    q_out, kv_out, q_held, kv_held, leave = refs[-5:]
    first = place[0]
    second = place[1]
    first_step = place[2]
    second_step = place[3]

    def normalize(values, gain):
        mean_square = jnp.mean(values * values, axis=-1, keepdims=True)
        return (values * lax.rsqrt(mean_square + 1e-06) * gain).astype(jnp.bfloat16)

    rows = jnp.concatenate([block[...] for block in blocks], axis=0)
    whole = jnp.concatenate([weight[at] for at in range(3)], axis=1)
    proj = jnp.dot(rows, whole, preferred_element_type=jnp.float32)
    q_held[...] = normalize(proj[:, :HEAD], gains[0:1, :])
    kv_held[:, :HEAD] = normalize(proj[:, HEAD : 2 * HEAD], gains[1:2, :])
    kv_held[:, HEAD:] = proj[:, 2 * HEAD :].astype(jnp.bfloat16)
    row = 0
    for shift, pieces in shares:
        for piece in pieces:
            spot = ((first + piece) % 4) * first_step + ((second + shift) % 4) * second_step
            target = pl.ds(pl.multiple_of(spot * PIECE, PIECE), PIECE)
            source = pl.ds(row, PIECE)
            pltpu.make_async_copy(q_held.at[source, :], q_out.at[target, :], leave.at[0]).start()
            pltpu.make_async_copy(kv_held.at[source, :], kv_out.at[target, :], leave.at[1]).start()
            row += PIECE
    pltpu.make_async_copy(q_held, q_held, leave.at[0]).wait()
    pltpu.make_async_copy(kv_held, kv_held, leave.at[1]).wait()


def project(shares, blocks, weight, gains, place, begun=()):
    rows = 16 * PIECE
    count = len(blocks)
    rows_here = sum(len(pieces) for _, pieces in shares) * PIECE
    anywhere = pl.BlockSpec(memory_space=pl.ANY)
    return pl.pallas_call(
        functools.partial(project_kernel, shares),
        out_shape=(
            jax.ShapeDtypeStruct((rows, HEAD), jnp.bfloat16),
            jax.ShapeDtypeStruct((rows, 2 * HEAD), jnp.bfloat16),
        ),
        in_specs=[SMEM] + [VMEM] * (count + 2) + [anywhere] * len(begun),
        out_specs=(anywhere, anywhere),
        scratch_shapes=[
            pltpu.VMEM((rows_here, HEAD), jnp.bfloat16),
            pltpu.VMEM((rows_here, 2 * HEAD), jnp.bfloat16),
            pltpu.SemaphoreType.DMA((2,)),
        ],
        input_output_aliases={count + 3: 0, count + 4: 1} if begun else {},
        compiler_params=pltpu.CompilerParams(vmem_limit_bytes=20 * 1024 * 1024),
        name="project",
    )(place, *blocks, weight, gains, *begun)


def attend_kernel(scale, call, part, blocks, place, pairs, counts, q, *refs):
    pieces = refs[:blocks]
    sums, kv = refs[-2:]
    slots = pieces[0].shape[0]
    rows = q.shape[0]
    for at in range(blocks):
        kv[at * slots : (at + 1) * slots] = pieces[at][...]
    if call == 0:
        sums[...] = jnp.zeros_like(sums)
    elif part is None:
        sums[...] = refs[blocks][...]
    else:
        base = (place[4] if part == "own" else 1 - place[4]) * slots
        for at in range(slots):
            sums[at] = refs[blocks][base + at]
    ones = jnp.ones((TILE, HEAD), jnp.bfloat16)

    def turn(step, _):
        rows_here, scores, products = [], [], []
        for at in range(UNROLL):
            pair = pairs[call, step * UNROLL + at]
            rows_here.append((pair >> 7, pair & 127))
        for row, tile in rows_here:
            scores.append(
                lax.dot_general(
                    q[jnp.minimum(row, rows - 1)],
                    kv[tile, :, :HEAD],
                    (((1,), (1,)), ((), ())),
                    preferred_element_type=jnp.float32,
                )
            )
        for (row, tile), score in zip(rows_here, scores):
            weights = jnp.exp2(score * scale).astype(jnp.bfloat16)
            values = jnp.concatenate((kv[tile, :, HEAD:], ones), axis=1)
            products.append(jnp.dot(weights, values, preferred_element_type=jnp.float32))
        for (row, _), product in zip(rows_here, products):
            if part is not None:
                row = jnp.where(row == rows, slots, row - base)
            sums[row] += product
        return 0

    lax.fori_loop(0, (counts[0, call] + UNROLL - 1) // UNROLL, turn, 0)
    if part is not None:
        refs[-3][...] = sums[:slots]


def attend(call, place, pairs, counts, q, pieces, sums=None):
    scale = HEAD ** (-0.5) * LOG2E
    part = CALLS[call][2]
    blocks, slots, rows = len(pieces), pieces[0].shape[0], q.shape[0]
    scratch = [pltpu.VMEM((blocks * slots, TILE, 2 * HEAD), jnp.bfloat16)]
    rows_out = rows + 1
    if part is not None:
        rows_out = slots
        scratch.insert(0, pltpu.VMEM((slots + 1, TILE, 2 * HEAD), jnp.float32))
    more = () if call == 0 else (sums,)
    return pl.pallas_call(
        functools.partial(attend_kernel, scale, call, part, blocks),
        out_shape=jax.ShapeDtypeStruct((rows_out, TILE, 2 * HEAD), jnp.float32),
        in_specs=[SMEM] * 3 + [VMEM] * (1 + blocks + len(more)),
        out_specs=VMEM,
        scratch_shapes=scratch,
        input_output_aliases={4 + blocks: 0} if call > 0 and part is None else {},
        compiler_params=pltpu.CompilerParams(vmem_limit_bytes=16 * 1024 * 1024),
        cost_estimate=pl.CostEstimate(
            flops=blocks * 10**9, bytes_accessed=blocks * 10**6, transcendentals=0
        ),
        name="attend",
    )(place, pairs, counts, q, *pieces, *more)


def call_room(start, stop, slots):
    pairs = 2 * slots * (2 * stop - start - max(start, 1)) * slots
    return -(-pairs // TILE) * TILE


def list_kernel(slots, calls, place, tiles, counts, pairs_out, counts_out):
    core = place[4]
    plane = place[5]
    listed, rows = tiles.shape
    tile = tiles[...]
    bal = (tile * (65536 // slots + 1)) >> 16
    away = (((bal >> 1) - plane) * (2 * core - 1)) & (PLANES - 1)
    same = (bal & 1) == core
    entry = lax.broadcasted_iota(jnp.int32, (listed, rows), 0)
    column = lax.broadcasted_iota(jnp.int32, (listed, rows), 1)
    least = jnp.where(same, 0, 1)
    most = PLANES // 2 - 1 + core
    inside = (away >= least) & (away <= most) & (entry < counts[...])
    down = lax.broadcasted_iota(jnp.int32, (listed, listed), 0)
    along = lax.broadcasted_iota(jnp.int32, (listed, listed), 1)
    before = jnp.where(along < down, 1.0, 0.0)
    down = lax.broadcasted_iota(jnp.int32, (rows, rows), 0)
    along = lax.broadcasted_iota(jnp.int32, (rows, rows), 1)
    ahead = jnp.where(down < along, 1.0, 0.0)
    nothing = rows * TILE
    totals = []
    theirs = jnp.where(column >= slots, 1 - core, core)
    crossed = jnp.where(same, 0, 1)
    for call, (start, stop, part, kind) in enumerate(calls):
        here = inside & (away >= start) & (away < stop)
        if part is not None:
            here = here & (theirs == (0 if part == "own" else 1))
        if kind is not None:
            here = here & (crossed == (0 if kind == "same" else 1))
        held = jnp.where(here, 1.0, 0.0)
        total = jnp.sum(held, axis=0, keepdims=True)
        order = jnp.dot(before, held, preferred_element_type=jnp.float32)
        order = order + jnp.dot(
            jnp.broadcast_to(total, (8, rows)), ahead, preferred_element_type=jnp.float32
        )[:1]
        order = jnp.where(held > 0.0, order, -1.0).astype(jnp.int32)
        skip = stop - start - max(start, 1) if kind is None else -start
        block = jnp.where(same, away - start, away + skip)
        pair = column * TILE + block * slots + tile - bal * slots - nothing
        room = call_room(start, stop, slots)
        spot = lax.broadcasted_iota(jnp.int32, (listed, room), 1)
        placed = jnp.zeros((1, room), jnp.int32)
        for row in range(rows):
            hit = order[:, row : row + 1] == spot
            placed += jnp.sum(jnp.where(hit, pair[:, row : row + 1], 0), axis=0, keepdims=True)
        pairs_out[call : call + 1, :room] = placed + nothing
        totals.append(jnp.sum(total, axis=1, keepdims=True).astype(jnp.int32))
    counts_out[...] = jnp.concatenate(totals, axis=1)


def list_pairs(calls, key_tiles, key_counts, place, slots):
    rows = 2 * slots
    tiles = lax.dynamic_slice_in_dim(key_tiles.T, place[5] * rows, rows, 1)
    counts = lax.dynamic_slice_in_dim(key_counts, place[5] * rows, rows, 1)
    room = max(call_room(start, stop, slots) for start, stop, _, _ in calls)
    return pl.pallas_call(
        functools.partial(list_kernel, slots, calls),
        out_shape=(
            jax.ShapeDtypeStruct((len(calls), room), jnp.int32),
            jax.ShapeDtypeStruct((1, len(calls)), jnp.int32),
        ),
        in_specs=[SMEM, VMEM, VMEM],
        out_specs=(VMEM, VMEM),
        compiler_params=pltpu.CompilerParams(vmem_limit_bytes=16 * 1024 * 1024),
        name="lists",
    )(place, tiles, counts)


def on_device(tokens, qkv_weight, q_gain, k_gain, key_tiles, key_counts):
    me_seq = lax.axis_index("seq")
    me_bal = lax.axis_index("bal")
    y, x = me_seq // 4, me_seq % 4
    core = me_bal % 2
    place = jnp.stack(
        (
            jnp.where(core == 0, x, y),
            jnp.where(core == 0, y, x),
            jnp.where(core == 0, 1, 4),
            jnp.where(core == 0, 4, 1),
            core,
            me_bal // 2,
        )
    ).astype(jnp.int32)
    slots = 16 * PIECE // TILE
    before = send(tokens, 1, 1)
    after = send(tokens, 1, -1)
    across = send(tokens, 1, 2)
    gains = jnp.concatenate((q_gain, k_gain), axis=0)
    weight = jnp.transpose(qkv_weight[:, 0], (1, 0, 2))
    own = join(2 * PIECE, (0,), (tokens,))
    after, own, gains = lax.optimization_barrier((after, own, gains))
    high = join(2 * PIECE, (0, PIECE), (after, across))
    after_high = send(high, 2, -1)
    low = join(2 * PIECE, (PIECE,), (before,), (own,))
    before_low = send(low, 2, 1)
    before_high = send(high, 2, 1)
    after_low = send(low, 2, -1)
    across_low = send(before_low, 2, 1)
    across_high = send(after_high, 2, -1)

    low_pieces, high_pieces = (0, 3), (1, 2)
    begun = project(
        ((0, low_pieces), (0, high_pieces), (3, low_pieces), (1, high_pieces)),
        (low, high, before_low, after_high),
        weight,
        gains,
        place,
    )
    begun = project(
        ((1, low_pieces), (3, high_pieces)),
        (after_low, before_high),
        weight,
        gains,
        place,
        begun,
    )
    queries, keys_values = project(
        ((2, low_pieces), (2, high_pieces)),
        (across_low, across_high),
        weight,
        gains,
        place,
        begun,
    )
    def tiles(block):
        return block.reshape(-1, TILE, block.shape[1])

    same, other, sums = [keys_values], [swap_cores(keys_values)], None
    for step in range(1, PLANES // 2 + 1):
        cores = (0, 1) if step < PLANES // 2 else (1,)
        same.append(pass_on(same[-1], cores))
        other.append(pass_on(other[-1], cores))
        if sums is not None:
            same[-1], sums = lax.optimization_barrier((same[-1], sums))
        if step == 1:
            queries, other[0] = lax.optimization_barrier((queries, other[0]))
            other_queries = swap_cores(queries)
            same[1], other_queries = lax.optimization_barrier((same[1], other_queries))
        if step == 2:
            key_tiles, other[1] = lax.optimization_barrier((key_tiles, other[1]))
            pairs, counts = list_pairs(CALLS, key_tiles[0], key_counts, place, slots)
            same[2], pairs, counts = lax.optimization_barrier((same[2], pairs, counts))
            low_queries = jnp.where(core == 0, queries, other_queries)
            high_queries = jnp.where(core == 0, other_queries, queries)
            chip_queries = tiles(jnp.concatenate((low_queries, high_queries), axis=0))
            other[2], chip_queries = lax.optimization_barrier((other[2], chip_queries))
        for call, (start, stop, part, kind) in enumerate(CALLS):
            if stop != step + 1:
                continue
            blocks = [] if kind == "other" else same[start:stop]
            blocks = blocks + ([] if kind == "same" else other[max(start, 1) : stop])
            blocks = [tiles(block) for block in blocks]
            done = attend(call, place, pairs, counts, chip_queries, blocks, sums)
            if part is None:
                sums = done
            elif part == "other":
                given = swap_cores(done)
            else:
                kept = done
    sums = kept + given
    result = (sums[:, :, :HEAD] / sums[:, :, HEAD:]).astype(jnp.bfloat16)
    return lax.all_to_all(
        result.reshape(slots * TILE, HEAD), "seq", split_axis=0, concat_axis=1, tiled=True
    )


def solution(mesh):
    placed = (
        P(("bal", "seq"), None),
        P(None, "seq", None, None),
        P("seq", None),
        P("seq", None),
        P("seq", None, None),
        P("seq", None),
    )
    return jax.shard_map(
        on_device, mesh=mesh, in_specs=placed, out_specs=P(("bal", "seq"), None), check_vma=False
    )
```

```python
import functools
import jax
import jax.numpy as jnp
from jax import lax
from jax.experimental import pallas as pl
from jax.experimental.pallas import tpu as pltpu
from jax.sharding import PartitionSpec as P

TILE = 128
HEAD = 128
PIECE = 48
PLANES = 16
UNROLL = 8
CALLS = ((0, 3, None),) + tuple((step, step + 1, None) for step in range(3, 8))
CALLS += ((8, 9, "other"), (8, 9, "own"))
LOG2E = 1.4426950408889634
MESH_AXES = ("seq", "bal")
VMEM = pl.BlockSpec(memory_space=pltpu.VMEM)
SMEM = pl.BlockSpec(memory_space=pltpu.SMEM)


def plane_perm(phase, shift):
    pairs = []
    for bal in range(32):
        for y in range(4):
            for x in range(4):
                along_x = (bal % 2 == 0) == (phase == 1)
                to_y = y if along_x else (y + shift) % 4
                to_x = (x + shift) % 4 if along_x else x
                pairs.append(((4 * y + x) * 32 + bal, (4 * to_y + to_x) * 32 + bal))
    return pairs


def send(block, phase, shift):
    return lax.ppermute(block, MESH_AXES, plane_perm(phase, shift))


def join_kernel(starts, *refs):
    parts = refs[: len(starts)]
    out, done = refs[-2:]
    copies = []
    for at, start in enumerate(starts):
        here = out.at[pl.ds(start, parts[at].shape[0]), :]
        copies.append(pltpu.make_async_copy(parts[at], here, done.at[at]))
    for copy in copies:
        copy.start()
    for copy in copies:
        copy.wait()


def join(rows, starts, parts, begun=()):
    anywhere = pl.BlockSpec(memory_space=pl.ANY)
    return pl.pallas_call(
        functools.partial(join_kernel, starts),
        out_shape=jax.ShapeDtypeStruct((rows, parts[0].shape[1]), parts[0].dtype),
        in_specs=[anywhere] * (len(parts) + len(begun)),
        out_specs=anywhere,
        scratch_shapes=[pltpu.SemaphoreType.DMA((len(parts),))],
        input_output_aliases={len(parts): 0} if begun else {},
        compiler_params=pltpu.CompilerParams(vmem_limit_bytes=1024 * 1024),
        name="join",
    )(*parts, *begun)


def swap_cores(block):
    return lax.ppermute(block, "bal", [(at, at ^ 1) for at in range(32)])


def pass_on(block, cores):
    pairs = []
    for z in range(PLANES):
        if 0 in cores:
            pairs.append((2 * z, 2 * ((z + 1) % PLANES)))
        if 1 in cores:
            pairs.append((2 * z + 1, 2 * ((z - 1) % PLANES) + 1))
    return lax.ppermute(block, "bal", pairs)


def project_kernel(shares, place, *refs):
    count = len(shares)
    blocks = refs[:count]
    weight, gains = refs[count : count + 2]
    q_out, kv_out, q_held, kv_held, leave = refs[-5:]
    first = place[0]
    second = place[1]
    first_step = place[2]
    second_step = place[3]

    def normalize(values, gain):
        mean_square = jnp.mean(values * values, axis=-1, keepdims=True)
        return (values * lax.rsqrt(mean_square + 1e-06) * gain).astype(jnp.bfloat16)

    rows = jnp.concatenate([block[...] for block in blocks], axis=0)
    whole = jnp.concatenate([weight[at] for at in range(3)], axis=1)
    proj = jnp.dot(rows, whole, preferred_element_type=jnp.float32)
    q_held[...] = normalize(proj[:, :HEAD], gains[0:1, :])
    kv_held[:, :HEAD] = normalize(proj[:, HEAD : 2 * HEAD], gains[1:2, :])
    kv_held[:, HEAD:] = proj[:, 2 * HEAD :].astype(jnp.bfloat16)
    row = 0
    for shift, pieces in shares:
        for piece in pieces:
            spot = ((first + piece) % 4) * first_step + ((second + shift) % 4) * second_step
            target = pl.ds(pl.multiple_of(spot * PIECE, PIECE), PIECE)
            source = pl.ds(row, PIECE)
            pltpu.make_async_copy(q_held.at[source, :], q_out.at[target, :], leave.at[0]).start()
            pltpu.make_async_copy(kv_held.at[source, :], kv_out.at[target, :], leave.at[1]).start()
            row += PIECE
    pltpu.make_async_copy(q_held, q_held, leave.at[0]).wait()
    pltpu.make_async_copy(kv_held, kv_held, leave.at[1]).wait()


def project(shares, blocks, weight, gains, place, begun=()):
    rows = 16 * PIECE
    count = len(blocks)
    rows_here = sum(len(pieces) for _, pieces in shares) * PIECE
    anywhere = pl.BlockSpec(memory_space=pl.ANY)
    return pl.pallas_call(
        functools.partial(project_kernel, shares),
        out_shape=(
            jax.ShapeDtypeStruct((rows, HEAD), jnp.bfloat16),
            jax.ShapeDtypeStruct((rows, 2 * HEAD), jnp.bfloat16),
        ),
        in_specs=[SMEM] + [VMEM] * (count + 2) + [anywhere] * len(begun),
        out_specs=(anywhere, anywhere),
        scratch_shapes=[
            pltpu.VMEM((rows_here, HEAD), jnp.bfloat16),
            pltpu.VMEM((rows_here, 2 * HEAD), jnp.bfloat16),
            pltpu.SemaphoreType.DMA((2,)),
        ],
        input_output_aliases={count + 3: 0, count + 4: 1} if begun else {},
        compiler_params=pltpu.CompilerParams(vmem_limit_bytes=20 * 1024 * 1024),
        name="project",
    )(place, *blocks, weight, gains, *begun)


def attend_kernel(scale, call, part, blocks, place, pairs, counts, q, *refs):
    pieces = refs[:blocks]
    sums, kv = refs[-2:]
    slots = pieces[0].shape[0]
    rows = q.shape[0]
    for at in range(blocks):
        kv[at * slots : (at + 1) * slots] = pieces[at][...]
    if call == 0:
        sums[...] = jnp.zeros_like(sums)
    elif part is None:
        sums[...] = refs[blocks][...]
    else:
        base = (place[4] if part == "own" else 1 - place[4]) * slots
        for at in range(slots):
            sums[at] = refs[blocks][base + at]
    ones = jnp.ones((TILE, HEAD), jnp.bfloat16)

    def turn(step, _):
        rows_here, scores, products = [], [], []
        for at in range(UNROLL):
            pair = pairs[call, step * UNROLL + at]
            rows_here.append((pair >> 7, pair & 127))
        for row, tile in rows_here:
            scores.append(
                lax.dot_general(
                    q[jnp.minimum(row, rows - 1)],
                    kv[tile, :, :HEAD],
                    (((1,), (1,)), ((), ())),
                    preferred_element_type=jnp.float32,
                )
            )
        for (row, tile), score in zip(rows_here, scores):
            weights = jnp.exp2(score * scale).astype(jnp.bfloat16)
            values = jnp.concatenate((kv[tile, :, HEAD:], ones), axis=1)
            products.append(jnp.dot(weights, values, preferred_element_type=jnp.float32))
        for (row, _), product in zip(rows_here, products):
            if part is not None:
                row = jnp.where(row == rows, slots, row - base)
            sums[row] += product
        return 0

    lax.fori_loop(0, (counts[0, call] + UNROLL - 1) // UNROLL, turn, 0)
    if part is not None:
        refs[-3][...] = sums[:slots].astype(refs[-3].dtype)


def attend(call, place, pairs, counts, q, pieces, sums=None):
    scale = HEAD ** (-0.5) * LOG2E
    part = CALLS[call][2]
    blocks, slots, rows = len(pieces), pieces[0].shape[0], q.shape[0]
    scratch = [pltpu.VMEM((blocks * slots, TILE, 2 * HEAD), jnp.bfloat16)]
    rows_out = rows + 1
    if part is not None:
        rows_out = slots
        scratch.insert(0, pltpu.VMEM((slots + 1, TILE, 2 * HEAD), jnp.float32))
    more = () if call == 0 else (sums,)
    return pl.pallas_call(
        functools.partial(attend_kernel, scale, call, part, blocks),
        out_shape=jax.ShapeDtypeStruct(
            (rows_out, TILE, 2 * HEAD), jnp.bfloat16 if part == "other" else jnp.float32
        ),
        in_specs=[SMEM] * 3 + [VMEM] * (1 + blocks + len(more)),
        out_specs=VMEM,
        scratch_shapes=scratch,
        input_output_aliases={4 + blocks: 0} if call > 0 and part is None else {},
        compiler_params=pltpu.CompilerParams(vmem_limit_bytes=16 * 1024 * 1024),
        cost_estimate=pl.CostEstimate(
            flops=blocks * 10**9, bytes_accessed=blocks * 10**6, transcendentals=0
        ),
        name="attend",
    )(place, pairs, counts, q, *pieces, *more)


def call_room(start, stop, slots):
    pairs = 2 * slots * (2 * stop - start - max(start, 1)) * slots
    return -(-pairs // TILE) * TILE


def list_kernel(slots, calls, place, tiles, counts, pairs_out, counts_out):
    core = place[4]
    plane = place[5]
    listed, rows = tiles.shape
    tile = tiles[...]
    bal = (tile * (65536 // slots + 1)) >> 16
    away = (((bal >> 1) - plane) * (2 * core - 1)) & (PLANES - 1)
    same = (bal & 1) == core
    entry = lax.broadcasted_iota(jnp.int32, (listed, rows), 0)
    column = lax.broadcasted_iota(jnp.int32, (listed, rows), 1)
    least = jnp.where(same, 0, 1)
    most = PLANES // 2 - 1 + core
    inside = (away >= least) & (away <= most) & (entry < counts[...])
    down = lax.broadcasted_iota(jnp.int32, (listed, listed), 0)
    along = lax.broadcasted_iota(jnp.int32, (listed, listed), 1)
    before = jnp.where(along < down, 1.0, 0.0)
    down = lax.broadcasted_iota(jnp.int32, (rows, rows), 0)
    along = lax.broadcasted_iota(jnp.int32, (rows, rows), 1)
    ahead = jnp.where(down < along, 1.0, 0.0)
    nothing = rows * TILE
    totals = []
    theirs = jnp.where(column >= slots, 1 - core, core)
    for call, (start, stop, part) in enumerate(calls):
        here = inside & (away >= start) & (away < stop)
        if part is not None:
            here = here & (theirs == (0 if part == "own" else 1))
        held = jnp.where(here, 1.0, 0.0)
        total = jnp.sum(held, axis=0, keepdims=True)
        order = jnp.dot(before, held, preferred_element_type=jnp.float32)
        order = order + jnp.dot(
            jnp.broadcast_to(total, (8, rows)), ahead, preferred_element_type=jnp.float32
        )[:1]
        order = jnp.where(held > 0.0, order, -1.0).astype(jnp.int32)
        skip = stop - start - max(start, 1)
        block = jnp.where(same, away - start, away + skip)
        pair = column * TILE + block * slots + tile - bal * slots - nothing
        room = call_room(start, stop, slots)
        spot = lax.broadcasted_iota(jnp.int32, (listed, room), 1)
        placed = jnp.zeros((1, room), jnp.int32)
        for row in range(rows):
            hit = order[:, row : row + 1] == spot
            placed += jnp.sum(jnp.where(hit, pair[:, row : row + 1], 0), axis=0, keepdims=True)
        pairs_out[call : call + 1, :room] = placed + nothing
        totals.append(jnp.sum(total, axis=1, keepdims=True).astype(jnp.int32))
    counts_out[...] = jnp.concatenate(totals, axis=1)


def list_pairs(calls, key_tiles, key_counts, place, slots):
    rows = 2 * slots
    tiles = lax.dynamic_slice_in_dim(key_tiles.T, place[5] * rows, rows, 1)
    counts = lax.dynamic_slice_in_dim(key_counts, place[5] * rows, rows, 1)
    room = max(call_room(start, stop, slots) for start, stop, _ in calls)
    return pl.pallas_call(
        functools.partial(list_kernel, slots, calls),
        out_shape=(
            jax.ShapeDtypeStruct((len(calls), room), jnp.int32),
            jax.ShapeDtypeStruct((1, len(calls)), jnp.int32),
        ),
        in_specs=[SMEM, VMEM, VMEM],
        out_specs=(VMEM, VMEM),
        compiler_params=pltpu.CompilerParams(vmem_limit_bytes=12 * 1024 * 1024),
        name="lists",
    )(place, tiles, counts)


def on_device(tokens, qkv_weight, q_gain, k_gain, key_tiles, key_counts):
    me_seq = lax.axis_index("seq")
    me_bal = lax.axis_index("bal")
    y, x = me_seq // 4, me_seq % 4
    core = me_bal % 2
    place = jnp.stack(
        (
            jnp.where(core == 0, x, y),
            jnp.where(core == 0, y, x),
            jnp.where(core == 0, 1, 4),
            jnp.where(core == 0, 4, 1),
            core,
            me_bal // 2,
        )
    ).astype(jnp.int32)
    slots = 16 * PIECE // TILE
    before = send(tokens, 1, 1)
    after = send(tokens, 1, -1)
    across = send(tokens, 1, 2)
    gains = jnp.concatenate((q_gain, k_gain), axis=0)
    weight = jnp.transpose(qkv_weight[:, 0], (1, 0, 2))
    own = join(2 * PIECE, (0,), (tokens,))
    after, own, gains = lax.optimization_barrier((after, own, gains))
    high = join(2 * PIECE, (0, PIECE), (after, across))
    after_high = send(high, 2, -1)
    low = join(2 * PIECE, (PIECE,), (before,), (own,))
    before_low = send(low, 2, 1)
    before_high = send(high, 2, 1)
    after_low = send(low, 2, -1)
    across_low = send(before_low, 2, 1)
    across_high = send(after_high, 2, -1)

    low_pieces, high_pieces = (0, 3), (1, 2)
    begun = project(
        ((0, low_pieces), (0, high_pieces), (3, low_pieces), (1, high_pieces)),
        (low, high, before_low, after_high),
        weight,
        gains,
        place,
    )
    begun = project(
        ((1, low_pieces), (3, high_pieces)),
        (after_low, before_high),
        weight,
        gains,
        place,
        begun,
    )
    queries, keys_values = project(
        ((2, low_pieces), (2, high_pieces)),
        (across_low, across_high),
        weight,
        gains,
        place,
        begun,
    )
    def tiles(block):
        return block.reshape(-1, TILE, block.shape[1])

    same, other, sums = [keys_values], [swap_cores(keys_values)], None
    for step in range(1, PLANES // 2 + 1):
        cores = (0, 1) if step < PLANES // 2 else (1,)
        same.append(pass_on(same[-1], cores))
        other.append(pass_on(other[-1], cores))
        if sums is not None:
            same[-1], sums = lax.optimization_barrier((same[-1], sums))
        if step == 1:
            queries, other[0] = lax.optimization_barrier((queries, other[0]))
            other_queries = swap_cores(queries)
            same[1], other_queries = lax.optimization_barrier((same[1], other_queries))
        if step == 2:
            key_tiles, other[1] = lax.optimization_barrier((key_tiles, other[1]))
            pairs, counts = list_pairs(CALLS, key_tiles[0], key_counts, place, slots)
            same[2], pairs, counts = lax.optimization_barrier((same[2], pairs, counts))
            low_queries = jnp.where(core == 0, queries, other_queries)
            high_queries = jnp.where(core == 0, other_queries, queries)
            chip_queries = tiles(jnp.concatenate((low_queries, high_queries), axis=0))
            other[2], chip_queries = lax.optimization_barrier((other[2], chip_queries))
        call = step - CALLS[0][1] + 1
        if call >= 0:
            start, stop, part = CALLS[call]
            blocks = [tiles(block) for block in same[start:stop] + other[max(start, 1) : stop]]
            if part is None:
                sums = attend(call, place, pairs, counts, chip_queries, blocks, sums)
    given = swap_cores(attend(call, place, pairs, counts, chip_queries, blocks, sums))
    kept = attend(call + 1, place, pairs, counts, chip_queries, blocks, sums)
    sums = kept + given.astype(jnp.float32)
    result = (sums[:, :, :HEAD] / sums[:, :, HEAD:]).astype(jnp.bfloat16)
    return lax.all_to_all(
        result.reshape(slots * TILE, HEAD), "seq", split_axis=0, concat_axis=1, tiled=True
    )


def solution(mesh):
    placed = (
        P(("bal", "seq"), None),
        P(None, "seq", None, None),
        P("seq", None),
        P("seq", None),
        P("seq", None, None),
        P("seq", None),
    )
    return jax.shard_map(
        on_device, mesh=mesh, in_specs=placed, out_specs=P(("bal", "seq"), None), check_vma=False
    )
```

```python
import functools
import jax
import jax.numpy as jnp
from jax import lax
from jax.experimental import pallas as pl
from jax.experimental.pallas import tpu as pltpu
from jax.sharding import PartitionSpec as P

TILE = 128
HEAD = 128
PIECE = 48
PLANES = 16
UNROLL = 8
CALLS = ((0, 3, None),) + tuple((step, step + 1, None) for step in range(3, 8))
CALLS += ((8, 9, "other"), (8, 9, "own"))
LOG2E = 1.4426950408889634
MESH_AXES = ("seq", "bal")
VMEM = pl.BlockSpec(memory_space=pltpu.VMEM)
SMEM = pl.BlockSpec(memory_space=pltpu.SMEM)


def plane_perm(phase, shift):
    pairs = []
    for bal in range(32):
        for y in range(4):
            for x in range(4):
                along_x = (bal % 2 == 0) == (phase == 1)
                to_y = y if along_x else (y + shift) % 4
                to_x = (x + shift) % 4 if along_x else x
                pairs.append(((4 * y + x) * 32 + bal, (4 * to_y + to_x) * 32 + bal))
    return pairs


def send(block, phase, shift):
    return lax.ppermute(block, MESH_AXES, plane_perm(phase, shift))


def join_kernel(starts, *refs):
    parts = refs[: len(starts)]
    out, done = refs[-2:]
    copies = []
    for at, start in enumerate(starts):
        here = out.at[pl.ds(start, parts[at].shape[0]), :]
        copies.append(pltpu.make_async_copy(parts[at], here, done.at[at]))
    for copy in copies:
        copy.start()
    for copy in copies:
        copy.wait()


def join(rows, starts, parts, begun=()):
    anywhere = pl.BlockSpec(memory_space=pl.ANY)
    return pl.pallas_call(
        functools.partial(join_kernel, starts),
        out_shape=jax.ShapeDtypeStruct((rows, parts[0].shape[1]), parts[0].dtype),
        in_specs=[anywhere] * (len(parts) + len(begun)),
        out_specs=anywhere,
        scratch_shapes=[pltpu.SemaphoreType.DMA((len(parts),))],
        input_output_aliases={len(parts): 0} if begun else {},
        compiler_params=pltpu.CompilerParams(vmem_limit_bytes=1024 * 1024),
        name="join",
    )(*parts, *begun)


def swap_cores(block):
    return lax.ppermute(block, "bal", [(at, at ^ 1) for at in range(32)])


def pass_on(block, cores):
    pairs = []
    for z in range(PLANES):
        if 0 in cores:
            pairs.append((2 * z, 2 * ((z + 1) % PLANES)))
        if 1 in cores:
            pairs.append((2 * z + 1, 2 * ((z - 1) % PLANES) + 1))
    return lax.ppermute(block, "bal", pairs)


def project_kernel(shares, place, *refs):
    count = len(shares)
    blocks = refs[:count]
    weight, gains = refs[count : count + 2]
    q_out, kv_out, q_held, kv_held, leave = refs[-5:]
    first = place[0]
    second = place[1]
    first_step = place[2]
    second_step = place[3]

    def normalize(values, gain):
        mean_square = jnp.mean(values * values, axis=-1, keepdims=True)
        return (values * lax.rsqrt(mean_square + 1e-06) * gain).astype(jnp.bfloat16)

    rows = jnp.concatenate([block[...] for block in blocks], axis=0)
    whole = jnp.concatenate([weight[at] for at in range(3)], axis=1)
    proj = jnp.dot(rows, whole, preferred_element_type=jnp.float32)
    q_held[...] = normalize(proj[:, :HEAD], gains[0:1, :])
    kv_held[:, :HEAD] = normalize(proj[:, HEAD : 2 * HEAD], gains[1:2, :])
    kv_held[:, HEAD:] = proj[:, 2 * HEAD :].astype(jnp.bfloat16)
    row = 0
    for shift, pieces in shares:
        for piece in pieces:
            spot = ((first + piece) % 4) * first_step + ((second + shift) % 4) * second_step
            target = pl.ds(pl.multiple_of(spot * PIECE, PIECE), PIECE)
            source = pl.ds(row, PIECE)
            pltpu.make_async_copy(q_held.at[source, :], q_out.at[target, :], leave.at[0]).start()
            pltpu.make_async_copy(kv_held.at[source, :], kv_out.at[target, :], leave.at[1]).start()
            row += PIECE
    pltpu.make_async_copy(q_held, q_held, leave.at[0]).wait()
    pltpu.make_async_copy(kv_held, kv_held, leave.at[1]).wait()


def project(shares, blocks, weight, gains, place, begun=()):
    rows = 16 * PIECE
    count = len(blocks)
    rows_here = sum(len(pieces) for _, pieces in shares) * PIECE
    anywhere = pl.BlockSpec(memory_space=pl.ANY)
    return pl.pallas_call(
        functools.partial(project_kernel, shares),
        out_shape=(
            jax.ShapeDtypeStruct((rows, HEAD), jnp.bfloat16),
            jax.ShapeDtypeStruct((rows, 2 * HEAD), jnp.bfloat16),
        ),
        in_specs=[SMEM] + [VMEM] * (count + 2) + [anywhere] * len(begun),
        out_specs=(anywhere, anywhere),
        scratch_shapes=[
            pltpu.VMEM((rows_here, HEAD), jnp.bfloat16),
            pltpu.VMEM((rows_here, 2 * HEAD), jnp.bfloat16),
            pltpu.SemaphoreType.DMA((2,)),
        ],
        input_output_aliases={count + 3: 0, count + 4: 1} if begun else {},
        compiler_params=pltpu.CompilerParams(vmem_limit_bytes=20 * 1024 * 1024),
        name="project",
    )(place, *blocks, weight, gains, *begun)


def attend_kernel(scale, call, part, blocks, place, pairs, counts, q, *refs):
    pieces = refs[:blocks]
    sums, kv = refs[-2:]
    slots = pieces[0].shape[0]
    rows = q.shape[0]
    for at in range(blocks):
        kv[at * slots : (at + 1) * slots] = pieces[at][...]
    if call == 0:
        sums[...] = jnp.zeros_like(sums)
    elif part is None:
        sums[...] = refs[blocks][...]
    else:
        base = (place[4] if part == "own" else 1 - place[4]) * slots
        for at in range(slots):
            sums[at] = refs[blocks][base + at]
    ones = jnp.ones((TILE, HEAD), jnp.bfloat16)

    def turn(step, _):
        rows_here, scores, products = [], [], []
        for at in range(UNROLL):
            pair = pairs[call, step * UNROLL + at]
            rows_here.append((pair >> 7, pair & 127))
        for row, tile in rows_here:
            scores.append(
                lax.dot_general(
                    q[jnp.minimum(row, rows - 1)],
                    kv[tile, :, :HEAD],
                    (((1,), (1,)), ((), ())),
                    preferred_element_type=jnp.float32,
                )
            )
        for (row, tile), score in zip(rows_here, scores):
            weights = jnp.exp2(score * scale).astype(jnp.bfloat16)
            values = jnp.concatenate((kv[tile, :, HEAD:], ones), axis=1)
            products.append(jnp.dot(weights, values, preferred_element_type=jnp.float32))
        for (row, _), product in zip(rows_here, products):
            if part is not None:
                row = jnp.where(row == rows, slots, row - base)
            sums[row] += product
        return 0

    lax.fori_loop(0, (counts[0, call] + UNROLL - 1) // UNROLL, turn, 0)
    if part is not None:
        refs[-3][...] = sums[:slots]


def attend(call, place, pairs, counts, q, pieces, sums=None):
    scale = HEAD ** (-0.5) * LOG2E
    part = CALLS[call][2]
    blocks, slots, rows = len(pieces), pieces[0].shape[0], q.shape[0]
    scratch = [pltpu.VMEM((blocks * slots, TILE, 2 * HEAD), jnp.bfloat16)]
    rows_out = rows + 1
    if part is not None:
        rows_out = slots
        scratch.insert(0, pltpu.VMEM((slots + 1, TILE, 2 * HEAD), jnp.float32))
    more = () if call == 0 else (sums,)
    return pl.pallas_call(
        functools.partial(attend_kernel, scale, call, part, blocks),
        out_shape=jax.ShapeDtypeStruct((rows_out, TILE, 2 * HEAD), jnp.float32),
        in_specs=[SMEM] * 3 + [VMEM] * (1 + blocks + len(more)),
        out_specs=VMEM,
        scratch_shapes=scratch,
        input_output_aliases={4 + blocks: 0} if call > 0 and part is None else {},
        compiler_params=pltpu.CompilerParams(vmem_limit_bytes=16 * 1024 * 1024),
        cost_estimate=pl.CostEstimate(
            flops=blocks * 10**9, bytes_accessed=blocks * 10**6, transcendentals=0
        ),
        name="attend",
    )(place, pairs, counts, q, *pieces, *more)


def call_room(start, stop, slots):
    pairs = 2 * slots * (2 * stop - start - max(start, 1)) * slots
    return -(-pairs // TILE) * TILE


def list_kernel(slots, calls, place, tiles, counts, pairs_out, counts_out):
    core = place[4]
    plane = place[5]
    listed, rows = tiles.shape
    tile = tiles[...]
    bal = (tile * (65536 // slots + 1)) >> 16
    away = (((bal >> 1) - plane) * (2 * core - 1)) & (PLANES - 1)
    same = (bal & 1) == core
    entry = lax.broadcasted_iota(jnp.int32, (listed, rows), 0)
    column = lax.broadcasted_iota(jnp.int32, (listed, rows), 1)
    least = jnp.where(same, 0, 1)
    most = PLANES // 2 - 1 + core
    inside = (away >= least) & (away <= most) & (entry < counts[...])
    down = lax.broadcasted_iota(jnp.int32, (listed, listed), 0)
    along = lax.broadcasted_iota(jnp.int32, (listed, listed), 1)
    before = jnp.where(along < down, 1.0, 0.0)
    down = lax.broadcasted_iota(jnp.int32, (rows, rows), 0)
    along = lax.broadcasted_iota(jnp.int32, (rows, rows), 1)
    ahead = jnp.where(down < along, 1.0, 0.0)
    nothing = rows * TILE
    totals = []
    theirs = jnp.where(column >= slots, 1 - core, core)
    for call, (start, stop, part) in enumerate(calls):
        here = inside & (away >= start) & (away < stop)
        if part is not None:
            here = here & (theirs == (0 if part == "own" else 1))
        held = jnp.where(here, 1.0, 0.0)
        total = jnp.sum(held, axis=0, keepdims=True)
        order = jnp.dot(before, held, preferred_element_type=jnp.float32)
        order = order + jnp.dot(
            jnp.broadcast_to(total, (8, rows)), ahead, preferred_element_type=jnp.float32
        )[:1]
        order = jnp.where(held > 0.0, order, -1.0).astype(jnp.int32)
        skip = stop - start - max(start, 1)
        block = jnp.where(same, away - start, away + skip)
        pair = column * TILE + block * slots + tile - bal * slots - nothing
        room = call_room(start, stop, slots)
        spot = lax.broadcasted_iota(jnp.int32, (listed, room), 1)
        placed = jnp.zeros((1, room), jnp.int32)
        for row in range(rows):
            hit = order[:, row : row + 1] == spot
            placed += jnp.sum(jnp.where(hit, pair[:, row : row + 1], 0), axis=0, keepdims=True)
        pairs_out[call : call + 1, :room] = placed + nothing
        totals.append(jnp.sum(total, axis=1, keepdims=True).astype(jnp.int32))
    counts_out[...] = jnp.concatenate(totals, axis=1)


def list_pairs(calls, key_tiles, key_counts, place, slots):
    rows = 2 * slots
    tiles = lax.dynamic_slice_in_dim(key_tiles.T, place[5] * rows, rows, 1)
    counts = lax.dynamic_slice_in_dim(key_counts, place[5] * rows, rows, 1)
    room = max(call_room(start, stop, slots) for start, stop, _ in calls)
    return pl.pallas_call(
        functools.partial(list_kernel, slots, calls),
        out_shape=(
            jax.ShapeDtypeStruct((len(calls), room), jnp.int32),
            jax.ShapeDtypeStruct((1, len(calls)), jnp.int32),
        ),
        in_specs=[SMEM, VMEM, VMEM],
        out_specs=(VMEM, VMEM),
        compiler_params=pltpu.CompilerParams(vmem_limit_bytes=12 * 1024 * 1024),
        name="lists",
    )(place, tiles, counts)


def on_device(tokens, qkv_weight, q_gain, k_gain, key_tiles, key_counts):
    me_seq = lax.axis_index("seq")
    me_bal = lax.axis_index("bal")
    y, x = me_seq // 4, me_seq % 4
    core = me_bal % 2
    place = jnp.stack(
        (
            jnp.where(core == 0, x, y),
            jnp.where(core == 0, y, x),
            jnp.where(core == 0, 1, 4),
            jnp.where(core == 0, 4, 1),
            core,
            me_bal // 2,
        )
    ).astype(jnp.int32)
    slots = 16 * PIECE // TILE
    before = send(tokens, 1, 1)
    after = send(tokens, 1, -1)
    across = send(tokens, 1, 2)
    gains = jnp.concatenate((q_gain, k_gain), axis=0)
    weight = jnp.transpose(qkv_weight[:, 0], (1, 0, 2))
    own = join(2 * PIECE, (0,), (tokens,))
    after, own, gains = lax.optimization_barrier((after, own, gains))
    high = join(2 * PIECE, (0, PIECE), (after, across))
    after_high = send(high, 2, -1)
    low = join(2 * PIECE, (PIECE,), (before,), (own,))
    before_low = send(low, 2, 1)
    before_high = send(high, 2, 1)
    after_low = send(low, 2, -1)
    across_low = send(before_low, 2, 1)
    across_high = send(after_high, 2, -1)

    low_pieces, high_pieces = (0, 3), (1, 2)
    begun = project(
        ((0, low_pieces), (0, high_pieces), (3, low_pieces), (1, high_pieces)),
        (low, high, before_low, after_high),
        weight,
        gains,
        place,
    )
    begun = project(
        ((1, low_pieces), (3, high_pieces)),
        (after_low, before_high),
        weight,
        gains,
        place,
        begun,
    )
    queries, keys_values = project(
        ((2, low_pieces), (2, high_pieces)),
        (across_low, across_high),
        weight,
        gains,
        place,
        begun,
    )
    def tiles(block):
        return block.reshape(-1, TILE, block.shape[1])

    same, other, sums = [keys_values], [swap_cores(keys_values)], None
    for step in range(1, PLANES // 2 + 1):
        cores = (0, 1) if step < PLANES // 2 else (1,)
        same.append(pass_on(same[-1], cores))
        other.append(pass_on(other[-1], cores))
        if sums is not None:
            same[-1], sums = lax.optimization_barrier((same[-1], sums))
        if step == 1:
            queries, other[0] = lax.optimization_barrier((queries, other[0]))
            other_queries = swap_cores(queries)
            other[1], other_queries = lax.optimization_barrier((other[1], other_queries))
        if step == 2:
            key_tiles, other[1] = lax.optimization_barrier((key_tiles, other[1]))
            pairs, counts = list_pairs(CALLS, key_tiles[0], key_counts, place, slots)
            same[2], pairs, counts = lax.optimization_barrier((same[2], pairs, counts))
            low_queries = jnp.where(core == 0, queries, other_queries)
            high_queries = jnp.where(core == 0, other_queries, queries)
            chip_queries = tiles(jnp.concatenate((low_queries, high_queries), axis=0))
            other[2], chip_queries = lax.optimization_barrier((other[2], chip_queries))
        call = step - CALLS[0][1] + 1
        if call >= 0:
            start, stop, part = CALLS[call]
            blocks = [tiles(block) for block in same[start:stop] + other[max(start, 1) : stop]]
            if part is None:
                sums = attend(call, place, pairs, counts, chip_queries, blocks, sums)
    given = swap_cores(attend(call, place, pairs, counts, chip_queries, blocks, sums))
    kept = attend(call + 1, place, pairs, counts, chip_queries, blocks, sums)
    sums = kept + given
    result = (sums[:, :, :HEAD] / sums[:, :, HEAD:]).astype(jnp.bfloat16)
    return lax.all_to_all(
        result.reshape(slots * TILE, HEAD), "seq", split_axis=0, concat_axis=1, tiled=True
    )


def solution(mesh):
    placed = (
        P(("bal", "seq"), None),
        P(None, "seq", None, None),
        P("seq", None),
        P("seq", None),
        P("seq", None, None),
        P("seq", None),
    )
    return jax.shard_map(
        on_device, mesh=mesh, in_specs=placed, out_specs=P(("bal", "seq"), None), check_vma=False
    )
```
